256 devices in a mesh: row: 32 (over x, z_hi, core), col: 8 (over z_lo, y).
Axes of the slice: x: 4, y: 4, z: 8 (z_hi: 4, z_lo: 2; z = z_hi * 2 + z_lo), core: 2. Of those that a mesh axis runs over, the one named last changes fastest.
Arguments:
- src_emb: bfloat16 [32768, 1024], P(('row', 'col')), may hold values from -48 to 48
- tgt_emb: bfloat16 [8192, 1024], P(('col', 'row')), may hold values from -16 to 16
- src_lang: int32 [32768], P('row'), may hold values from 0 to 3, as said below
- tgt_lang: int32 [8192], P('col'), may hold values from 0 to 3, as said below
Outputs:
- src_pull: float32 [32768, 1024], P(('row', 'col'))
- tgt_pull: float32 [8192, 1024], P(('col', 'row'))
- row_cost: float32 [32768], P(('row', 'col'))
The draws below stay inside these ranges and needn't reach their ends.
Inputs may be any that keep to these rules, and one draw needn't show every extreme that they name: `src_lang`: every bucket holds at least one source sentence. `tgt_lang`: every bucket holds at least one target sentence.
All inputs are finite; a program needn't handle non-finite values.
Results may differ from the reference program's by a relative error of at most 0.005.
Values may be sent and summed in bfloat16 or wider, within the bound.
No kernel may reach another device: no remote copies, remote signals or barrier semaphores. Data moves between devices by JAX's collectives and lax.ppermute only.
A program may use at most 64 MiB of HBM per device.

```python
import math
import jax
import jax.numpy as jnp
from jax import lax

D = 1024
SRC_BLK = 1024
BUCKETS = 4
ITERS = 3
NS = 32768
NT = 8192


def shared_layout(key):
    keys = jax.random.split(key, 7)
    src_lang = jax.random.randint(keys[0], (NS,), 0, BUCKETS)
    tgt_lang = jax.random.randint(keys[1], (NT,), 0, BUCKETS)
    labels = jnp.arange(BUCKETS, dtype=jnp.int32)
    src_lang = src_lang.at[labels * (NS // BUCKETS)].set(labels)
    tgt_lang = tgt_lang.at[labels * (NT // BUCKETS) + 1].set(labels)
    quarter = jnp.arange(4, dtype=jnp.int32)
    src_index = quarter * (NS // 4) + jax.random.randint(keys[2], (4,), 1, NS // 4)
    first_index = quarter * (NT // 4) + jax.random.randint(keys[3], (4,), 2, NT // 8)
    second_index = first_index + NT // 8
    paired = src_lang[src_index]
    tgt_lang = tgt_lang.at[first_index].set(paired).at[second_index].set(paired)
    common = jax.random.truncated_normal(keys[4], -4.0, 4.0, (4, D // 2))
    first_half = jax.random.truncated_normal(keys[5], -4.0, 4.0, (4, D - D // 2))
    second_half = jax.random.truncated_normal(keys[6], -4.0, 4.0, (4, D - D // 2))
    return (src_lang, tgt_lang, src_index, first_index, second_index, common, first_half, second_half)


def draw_src_lang(key, part):
    return shared_layout(key)[0]


def draw_tgt_lang(key, part):
    return shared_layout(key)[1]


def draw_src_emb(key, part):
    layout = shared_layout(key)
    key = jax.random.fold_in(key, 11)
    keys = jax.random.split(key, 2)
    scales = jnp.exp(jax.random.uniform(keys[0], (NS, 1), jnp.float32, math.log(0.3), math.log(3.0)))
    base = jax.random.truncated_normal(keys[1], -4.0, 4.0, (NS, D)) * scales
    strengths = jnp.array([4.0, 6.0, 8.0, 10.0], jnp.float32)
    tilt = 2.0 * 0.5 / math.sqrt(D) * (layout[6] - layout[7])
    aligned = jnp.concatenate([strengths[:, None] * layout[5], tilt], axis=1)
    base = base.at[layout[2]].set(aligned)
    return base.astype(jnp.bfloat16)


def draw_tgt_emb(key, part):
    layout = shared_layout(key)
    key = jax.random.fold_in(key, 23)
    keys = jax.random.split(key, 2)
    scales = jnp.exp(jax.random.uniform(keys[0], (NT, 1), jnp.float32, math.log(0.3), math.log(3.0)))
    base = jax.random.truncated_normal(keys[1], -4.0, 4.0, (NT, D)) * scales
    first_rows = jnp.concatenate([layout[5], layout[6]], axis=1)
    second_rows = jnp.concatenate([layout[5], layout[7]], axis=1)
    base = base.at[layout[3]].set(first_rows).at[layout[4]].set(second_rows)
    return base.astype(jnp.bfloat16)


def setup_inputs(seed: int = 0) -> dict:
    key_list = jax.random.split(jax.random.key(seed), 5)
    src_emb = draw_src_emb(jax.random.fold_in(key_list[4], 71), 0)
    tgt_emb = draw_tgt_emb(jax.random.fold_in(key_list[4], 71), 0)
    src_lang = draw_src_lang(jax.random.fold_in(key_list[4], 71), 0)
    tgt_lang = draw_tgt_lang(jax.random.fold_in(key_list[4], 71), 0)
    return {"src_emb": src_emb, "tgt_emb": tgt_emb, "src_lang": src_lang, "tgt_lang": tgt_lang}


NEG = -1e+30
EPSILON = 0.5

def masked_lse(logits, allowed):
    top = lax.optimization_barrier(jnp.max(jnp.where(allowed, logits, NEG), axis=1))
    total = lax.optimization_barrier(jnp.sum(jnp.where(allowed, jnp.exp(logits - top[:, None]), 0.0), axis=1))
    return top + jnp.log(total)

def reference(src_emb, tgt_emb, src_lang, tgt_lang):
    root = math.sqrt(D)
    blocks = NS // SRC_BLK
    src_parts = src_emb.reshape(blocks, SRC_BLK, D)
    lang_parts = src_lang.reshape(blocks, SRC_BLK)

    def block_cost(rows):
        return jnp.dot(rows, tgt_emb.T, preferred_element_type=jnp.float32) * (-1.0 / root)

    def sweep(tgt_pot):

        def visit(carry, inputs):
            rows, langs = inputs
            cost = block_cost(rows)
            allowed = langs[:, None] == tgt_lang[None, :]
            src_pot = -EPSILON * (masked_lse((tgt_pot[None, :] - cost) / EPSILON, allowed) - math.log(NT))
            logits = (src_pot[:, None] - cost) / EPSILON
            top = lax.optimization_barrier(jnp.max(jnp.where(allowed, logits, NEG), axis=0))
            total = lax.optimization_barrier(jnp.sum(jnp.where(allowed, jnp.exp(logits - top[None, :]), 0.0), axis=0))
            run_top, run_total = carry
            merged = jnp.maximum(run_top, top)
            run_total = run_total * jnp.exp(run_top - merged) + total * jnp.exp(top - merged)
            return ((merged, run_total), src_pot)
        start = (jnp.full((NT,), NEG, jnp.float32), jnp.zeros((NT,), jnp.float32))
        (top, total), src_pot = lax.scan(visit, start, (src_parts, lang_parts))
        new_tgt = -EPSILON * (top + jnp.log(total) - math.log(NS))
        return (src_pot, new_tgt)
    tgt_pot = jnp.zeros((NT,), jnp.float32)
    src_pot = jnp.zeros((blocks, SRC_BLK), jnp.float32)
    for step in range(ITERS):
        src_pot, tgt_pot = sweep(tgt_pot)

    def final(acc, inputs):
        rows, langs, pots = inputs
        cost = block_cost(rows)
        allowed = langs[:, None] == tgt_lang[None, :]
        weight = jnp.where(allowed, jnp.exp((pots[:, None] + tgt_pot[None, :] - cost) / EPSILON), 0.0)
        weight_low = weight.astype(jnp.bfloat16)
        pull = jnp.dot(weight_low, tgt_emb, preferred_element_type=jnp.float32) / NT
        carried = lax.optimization_barrier(jnp.sum(weight * cost, axis=1)) / NT
        acc = acc + jnp.dot(weight_low.T, rows, preferred_element_type=jnp.float32)
        return (acc, (pull, carried))
    acc, (pulls, carried) = lax.scan(final, jnp.zeros((NT, D), jnp.float32), (src_parts, lang_parts, src_pot))
    src_pull = pulls.reshape(NS, D)
    row_cost = carried.reshape(NS)
    tgt_pull = acc / NS
    return (src_pull, tgt_pull, row_cost)
```

```python
import math

import jax
import jax.numpy as jnp
from jax import lax
from jax.sharding import Mesh, PartitionSpec as P

ITERS = 3
NEG = -1e30
EPSILON = 0.5
LOG2E = math.log2(math.e)

AXES = ("x", "zh", "core", "zl", "y")
SIZES = (4, 4, 2, 2, 4)
ROW = ("x", "zh", "core")
COL = ("zl", "y")
RING = ("zh", "zl")
PLANE = ("x", "y")
SPREAD = ("x", "y", "core")


def gather(value, axes):
    size = lax.axis_size(axes)
    return lax.all_to_all(jnp.broadcast_to(value, (size, *value.shape)), axes, 0, 0)


def shift(value, step):
    size = lax.axis_size(RING)
    return lax.ppermute(value, RING, [(i, (i + step) % size) for i in range(size)])


def ring_gather(value):
    size = lax.axis_size(RING)
    up = down = value
    found = {0: value}
    for step in range(1, size // 2):
        up, down = shift(up, 1), shift(down, -1)
        found[-step], found[step] = up, down
    half = value.shape[0] // 2
    found[size // 2] = jnp.concatenate([shift(up[:half], 1), shift(down[half:], -1)])
    return found


def log2sumexp2(values, axis):
    top = jnp.max(values, axis=axis)
    total = jnp.sum(jnp.exp2(values - jnp.expand_dims(top, axis)), axis=axis)
    return top + jnp.log2(total)


def shards(src_emb, tgt_emb, src_lang, tgt_lang):
    rows, depth = src_emb.shape
    columns = tgt_emb.shape[0]
    row, col = lax.axis_index(ROW), lax.axis_index(COL)
    ring = lax.axis_size(RING)
    place = lax.axis_index(RING)
    core = lax.axis_index("core")
    total_src = src_lang.shape[0] * lax.axis_size(ROW)
    total_tgt = tgt_lang.shape[0] * lax.axis_size(COL)

    own_src_lang = lax.dynamic_slice(src_lang, (col * rows,), (rows,))
    own_tgt_lang = lax.dynamic_slice(tgt_lang, (row * columns,), (columns,))
    src_langs = gather(own_src_lang.reshape(1, rows), RING).reshape(ring, rows)
    tgt_langs = gather(own_tgt_lang.reshape(1, columns), SPREAD).reshape(-1)

    found = ring_gather(src_emb)
    src_block = jnp.concatenate([found[k] for k in range(1 - ring // 2, ring // 2 + 1)])
    order = (place + jnp.arange(1 - ring // 2, ring // 2 + 1)) % ring
    src_block_lang = src_langs[order].reshape(-1)

    mine = gather(tgt_emb, PLANE)
    theirs = lax.ppermute(mine, "core", [(0, 1), (1, 0)])
    both = jnp.where(core == 0, jnp.stack([mine, theirs], 1), jnp.stack([theirs, mine], 1))
    tgt_block = both.reshape(-1, depth)

    product = lax.dot_general(
        src_block, tgt_block, (((1,), (1,)), ((), ())), preferred_element_type=jnp.float32
    )
    allowed = src_block_lang[:, None] == tgt_langs[None, :]
    logits = jnp.where(allowed, product * (LOG2E / (EPSILON * math.sqrt(depth))), NEG)
    tgt_pot = jnp.zeros((logits.shape[1],), jnp.float32)
    for step in range(ITERS):
        part = log2sumexp2(logits + tgt_pot[None, :], 1)
        part = jnp.zeros((ring, rows)).at[order].set(part.reshape(ring, rows))
        whole = log2sumexp2(gather(part, RING), 0)
        src_pot = math.log2(total_tgt) - whole[order].reshape(-1)
        part = log2sumexp2(logits + src_pot[:, None], 0)
        whole = log2sumexp2(gather(part.reshape(8, -1), SPREAD), 0).reshape(-1)
        tgt_pot = math.log2(total_src) - whole
    weight = jnp.exp2(logits + src_pot[:, None] + tgt_pot[None, :])
    weight_low = weight.astype(jnp.bfloat16)
    cost_terms = jnp.sum(weight * logits, axis=1) * (-EPSILON / LOG2E / total_tgt)
    src_terms = jnp.dot(weight_low, tgt_block, preferred_element_type=jnp.float32) / total_tgt
    src_terms = src_terms.reshape(ring, rows, depth)
    tgt_terms = (
        lax.dot_general(
            weight_low, src_block, (((0,), (0,)), ((), ())), preferred_element_type=jnp.float32
        )
        / total_src
    )
    tgt_terms = tgt_terms.reshape(-1, 2, columns, depth)
    keep = jnp.where(core == 0, tgt_terms[:, 0], tgt_terms[:, 1])
    give = jnp.where(core == 0, tgt_terms[:, 1], tgt_terms[:, 0]).astype(jnp.bfloat16)
    keep = keep + lax.ppermute(give, "core", [(0, 1), (1, 0)]).astype(jnp.float32)
    parts = lax.all_to_all(keep.astype(jnp.bfloat16), PLANE, 0, 0)
    tgt_pull = jnp.sum(parts.astype(jnp.float32), axis=0)
    base = ring // 2 - 1
    half = rows // 2
    up = src_terms[base + ring // 2]
    up, down = up[:half].astype(jnp.bfloat16), up[half:].astype(jnp.bfloat16)
    up = shift(up, 1).astype(jnp.float32)
    down = shift(down, -1).astype(jnp.float32)
    pad = jnp.zeros((half, depth), jnp.float32)
    up, down = jnp.concatenate([up, pad]), jnp.concatenate([pad, down])
    for distance in range(ring // 2 - 1, 0, -1):
        up = shift((up + src_terms[base + distance]).astype(jnp.bfloat16), 1).astype(jnp.float32)
        down = shift((down + src_terms[base - distance]).astype(jnp.bfloat16), -1).astype(jnp.float32)
    src_pull = src_terms[base] + up + down
    costs = jnp.zeros((ring, rows)).at[order].set(cost_terms.reshape(ring, rows))
    row_cost = jnp.sum(lax.all_to_all(costs.reshape(ring, 1, rows), RING, 0, 0), axis=0)[0]
    return (src_pull, tgt_pull, row_cost)


def solution(mesh):
    split = Mesh(mesh.devices.reshape(SIZES), AXES)
    return jax.shard_map(
        shards,
        mesh=split,
        in_specs=(P(ROW + COL, None), P(COL + ROW, None), P(ROW), P(COL)),
        out_specs=(P(ROW + COL, None), P(COL + ROW, None), P(ROW + COL)),
        check_vma=False,
    )
```

```python
import functools
import math

import jax
import jax.numpy as jnp
from jax import lax
from jax.experimental import pallas as pl
from jax.experimental.pallas import tpu as pltpu
from jax.sharding import Mesh, PartitionSpec as P

ITERS = 3
NEG = -1e30
EPSILON = 0.5
LOG2E = math.log2(math.e)
LANES = 128

AXES = ("x", "zh", "core", "zl", "y")
SIZES = (4, 4, 2, 2, 4)
ROW = ("x", "zh", "core")
COL = ("zl", "y")
RING = ("zh", "zl")
PLANE = ("x", "y")
SPREAD = ("x", "y", "core")
SWAP = [(0, 1), (1, 0)]

VMEM = pl.BlockSpec(memory_space=pltpu.VMEM)
SMEM = pl.BlockSpec(memory_space=pltpu.SMEM)
CONTRACT_LAST = (((1,), (1,)), ((), ()))


def dot(a, b, dims=(((1,), (0,)), ((), ()))):
    return lax.dot_general(a, b, dims, preferred_element_type=jnp.float32)


def call(kernel, outs, scratch, *operands, smem=0, flops=0, bytes_accessed=0):
    specs = [SMEM] * smem + [VMEM] * (len(operands) - smem)
    return pl.pallas_call(
        kernel,
        out_shape=outs,
        in_specs=specs,
        out_specs=jax.tree.map(lambda _: VMEM, outs),
        scratch_shapes=scratch,
        compiler_params=pltpu.CompilerParams(vmem_limit_bytes=30 * 2**20),
        cost_estimate=pl.CostEstimate(
            flops=flops, bytes_accessed=bytes_accessed, transcendentals=0
        ),
    )(*operands)


def shift(value, step):
    size = lax.axis_size(RING)
    return lax.ppermute(value, RING, [(i, (i + step) % size) for i in range(size)])


def ring_gather(value):
    size = lax.axis_size(RING)
    up = down = value
    found = {0: value}
    for step in range(1, size // 2):
        up, down = shift(up, 1), shift(down, -1)
        found[-step], found[step] = up, down
    half = value.shape[0] // 2
    far = (shift(up[:half], 1), shift(down[half:], -1))
    return [found[k] for k in range(1 - size // 2, size // 2)], far


def with_language(emb, lang):
    hot = lang[:, None] == lax.broadcasted_iota(jnp.int32, (1, LANES), 1)
    return jnp.concatenate([emb, hot.astype(emb.dtype)], axis=1)


def columns_lse(table, added):
    rows, width = table.shape
    tiles = width // LANES

    def block(c, t):
        at = pl.ds(pl.multiple_of(c * LANES, LANES), LANES)
        z = table[at, t * LANES : (t + 1) * LANES]
        if added is not None:
            z = z + added[at, :]
        return z.reshape(LANES // 8, 8, LANES)

    def find_top(c, tops):
        return tuple(
            jnp.maximum(top, jnp.max(block(c, t), axis=0)) for t, top in enumerate(tops)
        )

    tops = (jnp.full((8, LANES), 2 * NEG, jnp.float32),) * tiles
    tops = lax.fori_loop(0, rows // LANES, find_top, tops)
    tops = [jnp.max(top, axis=0, keepdims=True) for top in tops]

    def add_up(c, sums):
        return tuple(
            s + jnp.sum(jnp.exp2(block(c, t) - tops[t][None]), axis=0)
            for t, s in enumerate(sums)
        )

    sums = (jnp.zeros((8, LANES), jnp.float32),) * tiles
    sums = lax.fori_loop(0, rows // LANES, add_up, sums)
    return [
        top + jnp.log2(jnp.sum(s, axis=0, keepdims=True)) for top, s in zip(tops, sums)
    ]


def send_out(parts, offset, order, out):
    for t, part in enumerate(parts):
        order[pl.ds(lax.rem(t + offset, 8), 1), :] = part
    out[...] = jnp.broadcast_to(order[...][None], out.shape)


def merge(gathered, log_count, offset, order):
    parts = gathered[...]
    top = jnp.max(parts, axis=0)
    total = jnp.sum(jnp.exp2(parts - top[None]), axis=0)
    order[...] = log_count - (top + jnp.log2(total))
    return jnp.concatenate([order[pl.ds(lax.rem(t + offset, 8), 1), :] for t in range(8)])


def spread(pots, wide):
    columns = pots.T
    for c in range(8):
        wide[c * LANES : (c + 1) * LANES, :] = jnp.broadcast_to(
            columns[:, c : c + 1], (LANES, LANES)
        )


def first_kernel(scale, offsets, *refs):
    chunks, (far_up, far_down, mine, theirs) = refs[:7], refs[7:11]
    logits, logits_t, src_block, out, order = refs[11:]
    depth = src_block.shape[1]
    half = mine.shape[0]
    parts = []
    for unit in range(4):
        if unit < 3:
            src = jnp.concatenate([chunks[2 * unit][...], chunks[2 * unit + 1][...]])
        else:
            src = jnp.concatenate([chunks[6][...], far_up[...], far_down[...]])
        src, hot = src[:, :depth], src[:, depth:]
        at = slice(unit * 256, (unit + 1) * 256)
        src_block[at, :] = src
        for side, tgt in enumerate((mine, theirs)):
            to = slice(side * half, (side + 1) * half)
            emb, tgt_hot = tgt[:, :depth], tgt[:, depth:]
            same = dot(hot, tgt_hot, CONTRACT_LAST) > 0.5
            logits[at, to] = jnp.where(same, dot(src, emb, CONTRACT_LAST) * scale, NEG)
            same = dot(tgt_hot, hot, CONTRACT_LAST) > 0.5
            logits_t[to, at] = jnp.where(same, dot(emb, src, CONTRACT_LAST) * scale, NEG)
    parts = columns_lse(logits_t, None)
    send_out(parts, offsets[0], order, out)


def half_step_kernel(log_count, enter, leave, offsets, table, gathered, out, pots, order, wide):
    local = merge(gathered, log_count, offsets[enter], order)
    pots[...] = local
    spread(local, wide)
    send_out(columns_lse(table, wide), offsets[leave], order, out)


def src_kernel(log_count, share, offsets, logits, gathered, src_pots, mine, theirs, out, order, wide):
    depth = out.shape[1]
    half = mine.shape[0]
    tgt = merge(gathered, log_count, offsets[1], order)
    spread(src_pots[...], wide)
    for unit in range(4):
        at = slice(unit * 256, (unit + 1) * 256)
        weight = [
            jnp.exp2(logits[at, t * LANES : (t + 1) * LANES] + wide[at, :] + tgt[t : t + 1, :])
            .astype(jnp.bfloat16)
            for t in range(8)
        ]
        first = jnp.concatenate(weight[:4], axis=1)
        second = jnp.concatenate(weight[4:], axis=1)
        pull = dot(first, mine[:, :depth]) + dot(second, theirs[:, :depth])
        out[at, :] = pull * share


def tgt_kernel(
    log_count, share, offsets, logits_t, gathered, src_pots, src_block, keep, give, order, wide
):
    half = keep.shape[0]
    spread(merge(gathered, log_count, offsets[1], order), wide)
    src = src_pots[...]
    for unit in range(4):
        at = slice(unit * 256, (unit + 1) * 256)
        weight = [
            jnp.exp2(logits_t[at, t * LANES : (t + 1) * LANES] + wide[at, :] + src[t : t + 1, :])
            .astype(jnp.bfloat16)
            for t in range(8)
        ]
        pull = dot(jnp.concatenate(weight, axis=1), src_block[...]) * share
        to = slice((unit % 2) * 256, (unit % 2 + 1) * 256)
        if unit < 2:
            keep[to, :] = pull
        else:
            give[to, :] = pull.astype(give.dtype)


def shards(src_emb, tgt_emb, src_lang, tgt_lang):
    f32, bf16 = jnp.float32, jnp.bfloat16
    rows, depth = src_emb.shape
    columns = tgt_emb.shape[0]
    row, col = lax.axis_index(ROW), lax.axis_index(COL)
    ring, plane = lax.axis_size(RING), lax.axis_size(PLANE)
    spread_size = lax.axis_size(SPREAD)
    n_src, n_tgt = rows * ring, columns * spread_size
    place, core = lax.axis_index(RING), lax.axis_index("core")
    total_src = src_lang.shape[0] * lax.axis_size(ROW)
    total_tgt = tgt_lang.shape[0] * lax.axis_size(COL)
    offsets = jnp.stack([(place + ring // 2 + 1) % ring, 4 * core]).astype(jnp.int32)

    own_src_lang = lax.dynamic_slice(src_lang, (col * rows,), (rows,))
    own_tgt_lang = lax.dynamic_slice(tgt_lang, (row * columns,), (columns,))
    chunks, far = ring_gather(with_language(src_emb, own_src_lang))
    tgt = with_language(tgt_emb, own_tgt_lang)
    mine = lax.all_to_all(jnp.broadcast_to(tgt, (plane, *tgt.shape)), PLANE, 0, 0)
    theirs = lax.ppermute(mine, "core", SWAP)
    mine, theirs = (v.reshape(plane * columns, -1) for v in (mine, theirs))

    order = pltpu.VMEM((8, LANES), f32)
    table = jax.ShapeDtypeStruct((n_src, n_tgt), f32)
    table_t = jax.ShapeDtypeStruct((n_tgt, n_src), f32)
    pots = jax.ShapeDtypeStruct((8, LANES), f32)
    to_ring = jax.ShapeDtypeStruct((ring, 8, LANES), f32)
    to_spread = jax.ShapeDtypeStruct((spread_size, 8, LANES), f32)
    logits, logits_t, src_block, part = call(
        functools.partial(first_kernel, LOG2E / (EPSILON * math.sqrt(depth))),
        (table, table_t, jax.ShapeDtypeStruct((n_src, depth), bf16), to_ring),
        [order],
        offsets, *chunks, *far, mine, theirs,
        smem=1, flops=4 * n_src * n_tgt * depth, bytes_accessed=2**23,
    )
    wide_src = pltpu.VMEM((n_src, LANES), f32)
    wide_tgt = pltpu.VMEM((n_tgt, LANES), f32)
    for step in range(ITERS):
        gathered = lax.all_to_all(part, RING, 0, 0)
        part, src_pots = call(
            functools.partial(half_step_kernel, math.log2(total_tgt), 0, 1),
            (to_spread, pots), [order, wide_src],
            offsets, logits, gathered, smem=1, flops=8 * n_src * n_tgt, bytes_accessed=2**22,
        )
        gathered = lax.all_to_all(part, SPREAD, 0, 0)
        if step < ITERS - 1:
            part, _ = call(
                functools.partial(half_step_kernel, math.log2(total_src), 1, 0),
                (to_ring, pots), [order, wide_tgt],
                offsets, logits_t, gathered, smem=1, flops=8 * n_src * n_tgt, bytes_accessed=2**22,
            )
    src_terms = call(
        functools.partial(src_kernel, math.log2(total_src), 1.0 / total_tgt),
        jax.ShapeDtypeStruct((n_src, depth), f32),
        [order, wide_src],
        offsets, logits, gathered, src_pots, mine, theirs,
        smem=1, flops=2 * n_src * n_tgt * depth, bytes_accessed=2**23,
    )
    keep, give = call(
        functools.partial(tgt_kernel, math.log2(total_src), 1.0 / total_src),
        (jax.ShapeDtypeStruct((n_tgt // 2, depth), f32), jax.ShapeDtypeStruct((n_tgt // 2, depth), bf16)),
        [order, wide_tgt],
        offsets, logits_t, gathered, src_pots, src_block,
        smem=1, flops=2 * n_src * n_tgt * depth, bytes_accessed=2**23,
    )
    keep = keep + lax.ppermute(give, "core", SWAP).astype(f32)
    parts = lax.all_to_all(keep.astype(bf16).reshape(plane, columns, depth), PLANE, 0, 0)
    tgt_pull = jnp.sum(parts.astype(f32), axis=0)
    src_terms = src_terms.reshape(ring, rows, depth)
    base = ring // 2 - 1
    half = rows // 2
    far = src_terms[base + ring // 2].astype(bf16)
    pad = jnp.zeros((half, depth), f32)
    up = jnp.concatenate([shift(far[:half], 1).astype(f32), pad])
    down = jnp.concatenate([pad, shift(far[half:], -1).astype(f32)])
    for distance in range(ring // 2 - 1, 0, -1):
        up = shift((up + src_terms[base + distance]).astype(bf16), 1).astype(f32)
        down = shift((down + src_terms[base - distance]).astype(bf16), -1).astype(f32)
    src_pull = src_terms[base] + up + down
    row_cost = jnp.sum(src_pull * src_emb.astype(f32), axis=1) * (-1.0 / math.sqrt(depth))
    return (src_pull, tgt_pull, row_cost)


def solution(mesh):
    split = Mesh(mesh.devices.reshape(SIZES), AXES)
    return jax.shard_map(
        shards,
        mesh=split,
        in_specs=(P(ROW + COL, None), P(COL + ROW, None), P(ROW), P(COL)),
        out_specs=(P(ROW + COL, None), P(COL + ROW, None), P(ROW + COL)),
        check_vma=False,
    )
```

```python
import functools
import math

import jax
import jax.numpy as jnp
from jax import lax
from jax.experimental import pallas as pl
from jax.experimental.pallas import tpu as pltpu
from jax.sharding import Mesh, PartitionSpec as P

ITERS = 3
NEG = -1e30
EPSILON = 0.5
LOG2E = math.log2(math.e)
LANES = 128
DISTANCES = (1, 7, 2, 6, 3, 5, 0, 4)

AXES = ("x", "zh", "core", "zl", "y")
SIZES = (4, 4, 2, 2, 4)
ROW = ("x", "zh", "core")
COL = ("zl", "y")
RING = ("zh", "zl")
PLANE = ("x", "y")
SPREAD = ("x", "y", "core")
SWAP = [(0, 1), (1, 0)]

VMEM = pl.BlockSpec(memory_space=pltpu.VMEM)
SMEM = pl.BlockSpec(memory_space=pltpu.SMEM)
CONTRACT_LAST = (((1,), (1,)), ((), ()))


def dot(a, b, dims=(((1,), (0,)), ((), ()))):
    return lax.dot_general(a, b, dims, preferred_element_type=jnp.float32)


def call(kernel, outs, scratch, *operands, smem=0, flops=0, bytes_accessed=0):
    specs = [SMEM] * smem + [VMEM] * (len(operands) - smem)
    return pl.pallas_call(
        kernel,
        out_shape=outs,
        in_specs=specs,
        out_specs=jax.tree.map(lambda _: VMEM, outs),
        scratch_shapes=scratch,
        compiler_params=pltpu.CompilerParams(vmem_limit_bytes=30 * 2**20),
        cost_estimate=pl.CostEstimate(
            flops=flops, bytes_accessed=bytes_accessed, transcendentals=0
        ),
    )(*operands)


def shift(value, step):
    size = lax.axis_size(RING)
    return lax.ppermute(value, RING, [(i, (i + step) % size) for i in range(size)])


def with_language(emb, lang):
    hot = lang[:, None] == lax.broadcasted_iota(jnp.int32, (1, LANES), 1)
    return jnp.concatenate([emb, hot.astype(emb.dtype)], axis=1)


def columns_lse(tables, added):
    tiles = tables[0].shape[1] // LANES

    def blocks(t):
        start = 0
        for table in tables:
            for c in range(table.shape[0] // LANES):
                z = table[c * LANES : (c + 1) * LANES, t * LANES : (t + 1) * LANES]
                if added is not None:
                    z = z + added[start : start + LANES, :]
                start += LANES
                yield z.reshape(LANES // 8, 8, LANES)

    results = []
    for t in range(tiles):
        top = functools.reduce(jnp.maximum, (jnp.max(z, axis=0) for z in blocks(t)))
        top = jnp.max(top, axis=0, keepdims=True)
        total = functools.reduce(
            jnp.add, (jnp.sum(jnp.exp2(z - top[None]), axis=0) for z in blocks(t))
        )
        results.append(top + jnp.log2(jnp.sum(total, axis=0, keepdims=True)))
    return results


def send_out(parts, offset, table, order, out):
    for part, at in zip(parts, table):
        order[pl.ds(lax.rem(at + offset, 8), 1), :] = part
    out[...] = jnp.broadcast_to(order[...][None], out.shape)


def merge(gathered, log_count, offset, table, order):
    parts = gathered[...]
    top = jnp.max(parts, axis=0)
    total = jnp.sum(jnp.exp2(parts - top[None]), axis=0)
    order[...] = log_count - (top + jnp.log2(total))
    return jnp.concatenate([order[pl.ds(lax.rem(at + offset, 8), 1), :] for at in table])


def spread(pots, wide):
    columns = pots.T
    for c in range(8):
        wide[c * LANES : (c + 1) * LANES, :] = jnp.broadcast_to(
            columns[:, c : c + 1], (LANES, LANES)
        )


def make_logits(scale, src, mine, theirs, logits, logits_t, src_block):
    depth = src_block.shape[1]
    half = mine.shape[0]
    src, hot = src[:, :depth], src[:, depth:]
    src_block[...] = src
    for side, tgt in enumerate((mine, theirs)):
        to = slice(side * half, (side + 1) * half)
        emb, tgt_hot = tgt[:, :depth], tgt[:, depth:]
        same = dot(hot, tgt_hot, CONTRACT_LAST) > 0.5
        logits[:, to] = jnp.where(same, dot(src, emb, CONTRACT_LAST) * scale, NEG)
        same = dot(tgt_hot, hot, CONTRACT_LAST) > 0.5
        logits_t[to, :] = jnp.where(same, dot(emb, src, CONTRACT_LAST) * scale, NEG)


def pair_kernel(scale, near, other, mine, theirs, logits, logits_t, src_block, part):
    src = jnp.concatenate([near[...], other[...]])
    make_logits(scale, src, mine, theirs, logits, logits_t, src_block)
    part[...] = jnp.concatenate(columns_lse([logits_t], None))


def last_pair_kernel(
    scale, offsets, own, far_up, far_down, mine, theirs, *refs
):
    parts, (logits, logits_t, src_block, out, order) = refs[:3], refs[3:]
    src = jnp.concatenate([own[...], far_up[...], far_down[...]])
    make_logits(scale, src, mine, theirs, logits, logits_t, src_block)
    parts = [part[r : r + 1, :] for part in parts for r in range(2)]
    send_out(parts + columns_lse([logits_t], None), offsets[0], DISTANCES, order, out)


def src_pots_kernel(log_count, offsets, *refs):
    tables, (gathered, out, pots, order, wide) = refs[:4], refs[4:]
    local = merge(gathered, log_count, offsets[0], DISTANCES, order)
    pots[...] = local
    spread(local, wide)
    send_out(columns_lse(tables, wide), offsets[1], range(8), order, out)


def tgt_pots_kernel(log_count, offsets, *refs):
    tables, (gathered, out, order, wide) = refs[:4], refs[4:]
    spread(merge(gathered, log_count, offsets[1], range(8), order), wide)
    parts = [part for table in tables for part in columns_lse([table], wide)]
    send_out(parts, offsets[0], DISTANCES, order, out)


def src_kernel(log_count, share, units, offsets, *refs):
    n = len(units)
    tables, (gathered, src_pots, mine, theirs), outs = refs[:n], refs[n : n + 4], refs[n + 4 : -2]
    order, wide = refs[-2:]
    depth = outs[0].shape[1]
    tgt = merge(gathered, log_count, offsets[1], range(8), order)
    spread(src_pots[...], wide)
    for k, (unit, table) in enumerate(zip(units, tables)):
        at = slice(unit * 256, (unit + 1) * 256)
        weight = [
            jnp.exp2(table[:, t * LANES : (t + 1) * LANES] + wide[at, :] + tgt[t : t + 1, :])
            .astype(jnp.bfloat16)
            for t in range(8)
        ]
        first = jnp.concatenate(weight[:4], axis=1)
        second = jnp.concatenate(weight[4:], axis=1)
        pull = (dot(first, mine[:, :depth]) + dot(second, theirs[:, :depth])) * share
        for out, value in zip(outs[2 * k : 2 * k + 2], (pull[:LANES], pull[LANES:])):
            out[...] = value.astype(out.dtype)


def tgt_kernel(log_count, share, offsets, *refs):
    tables, (gathered, src_pots), blocks = refs[:4], refs[4:6], refs[6:10]
    keep, give, order, wide = refs[10:]
    spread(merge(gathered, log_count, offsets[1], range(8), order), wide)
    src = src_pots[...]
    for unit in (2, 3, 0, 1):
        at = slice(unit * 256, (unit + 1) * 256)
        pull = 0.0
        for k, (table, block) in enumerate(zip(tables, blocks)):
            weight = [
                jnp.exp2(table[at, t * LANES : (t + 1) * LANES] + wide[at, :] + src[2 * k + t : 2 * k + t + 1, :])
                .astype(jnp.bfloat16)
                for t in range(2)
            ]
            pull = pull + dot(jnp.concatenate(weight, axis=1), block[...])
        to = slice((unit % 2) * 256, (unit % 2 + 1) * 256)
        if unit < 2:
            keep[to, :] = pull * share
        else:
            give[to, :] = (pull * share).astype(give.dtype)


def shards(src_emb, tgt_emb, src_lang, tgt_lang):
    f32, bf16 = jnp.float32, jnp.bfloat16
    rows, depth = src_emb.shape
    columns = tgt_emb.shape[0]
    row, col = lax.axis_index(ROW), lax.axis_index(COL)
    ring, plane = lax.axis_size(RING), lax.axis_size(PLANE)
    spread_size = lax.axis_size(SPREAD)
    n_src, n_tgt = rows * ring, columns * spread_size
    place, core = lax.axis_index(RING), lax.axis_index("core")
    total_src = src_lang.shape[0] * lax.axis_size(ROW)
    total_tgt = tgt_lang.shape[0] * lax.axis_size(COL)
    offsets = jnp.stack([place, 4 * core]).astype(jnp.int32)

    own_src_lang = lax.dynamic_slice(src_lang, (col * rows,), (rows,))
    own_tgt_lang = lax.dynamic_slice(tgt_lang, (row * columns,), (columns,))
    own = with_language(src_emb, own_src_lang)
    tgt = with_language(tgt_emb, own_tgt_lang)
    mine = lax.all_to_all(jnp.broadcast_to(tgt, (plane, *tgt.shape)), PLANE, 0, 0)
    up, down = shift(own, 1), shift(own, -1)
    pairs = [(down, up)]
    up, down = shift(up, 1), shift(down, -1)
    mine, up, down = lax.optimization_barrier((mine, up, down))
    pairs.append((down, up))
    theirs = lax.ppermute(mine, "core", SWAP)
    mine, theirs = (v.reshape(plane * columns, -1) for v in (mine, theirs))
    up, down = shift(up, 1), shift(down, -1)
    pairs.append((down, up))
    far = (shift(up[: rows // 2], 1), shift(down[rows // 2 :], -1))

    order = pltpu.VMEM((8, LANES), f32)
    pots = jax.ShapeDtypeStruct((8, LANES), f32)
    to_ring = jax.ShapeDtypeStruct((ring, 8, LANES), f32)
    to_spread = jax.ShapeDtypeStruct((spread_size, 8, LANES), f32)
    pair = (
        jax.ShapeDtypeStruct((2 * rows, n_tgt), f32),
        jax.ShapeDtypeStruct((n_tgt, 2 * rows), f32),
        jax.ShapeDtypeStruct((2 * rows, depth), bf16),
    )
    matmul = 2 * n_src * n_tgt * depth
    scale = LOG2E / (EPSILON * math.sqrt(depth))
    made = [
        call(
            functools.partial(pair_kernel, scale),
            (*pair, jax.ShapeDtypeStruct((2, LANES), f32)), [],
            near, other, mine, theirs,
            flops=matmul // 2, bytes_accessed=2**22,
        )
        for near, other in pairs
    ]
    *last, part = call(
        functools.partial(last_pair_kernel, scale),
        (*pair, to_ring), [order],
        offsets, own, *far, mine, theirs, *(m[3] for m in made),
        smem=1, flops=matmul // 2, bytes_accessed=2**22,
    )
    made.append(last)
    logits, logits_t, src_blocks = ([m[k] for m in made] for k in range(3))
    wide_src = pltpu.VMEM((n_src, LANES), f32)
    wide_tgt = pltpu.VMEM((n_tgt, LANES), f32)
    for step in range(ITERS):
        gathered = lax.all_to_all(part, RING, 0, 0)
        part, src_pots = call(
            functools.partial(src_pots_kernel, math.log2(total_tgt)),
            (to_spread, pots), [order, wide_src],
            offsets, *logits, gathered, smem=1, flops=8 * n_src * n_tgt, bytes_accessed=2**22,
        )
        gathered = lax.all_to_all(part, SPREAD, 0, 0)
        if step < ITERS - 1:
            (part,) = call(
                functools.partial(tgt_pots_kernel, math.log2(total_src)),
                (to_ring,), [order, wide_tgt],
                offsets, *logits_t, gathered, smem=1, flops=8 * n_src * n_tgt, bytes_accessed=2**22,
            )
    term = jax.ShapeDtypeStruct((rows, depth), f32)
    own_term, far_term = call(
        functools.partial(src_kernel, math.log2(total_src), 1.0 / total_tgt, (3,)),
        (term, jax.ShapeDtypeStruct((rows, depth), bf16)), [order, wide_src],
        offsets, logits[3], gathered, src_pots, mine, theirs,
        smem=1, flops=matmul // 4, bytes_accessed=2**22,
    )
    half = rows // 2
    up, down = shift(far_term[:half], 1), shift(far_term[half:], -1)
    gathered, own_term = lax.optimization_barrier((gathered, own_term))
    terms = call(
        functools.partial(src_kernel, math.log2(total_src), 1.0 / total_tgt, (0, 1, 2)),
        (term,) * 6, [order, wide_src],
        offsets, *logits[:3], gathered, src_pots, mine, theirs,
        smem=1, flops=3 * matmul // 4, bytes_accessed=2**23,
    )
    gathered, *terms = lax.optimization_barrier((gathered, *terms))
    keep, give = call(
        functools.partial(tgt_kernel, math.log2(total_src), 1.0 / total_src),
        (jax.ShapeDtypeStruct((n_tgt // 2, depth), f32), jax.ShapeDtypeStruct((n_tgt // 2, depth), bf16)),
        [order, wide_tgt],
        offsets, *logits_t, gathered, src_pots, *src_blocks,
        smem=1, flops=matmul, bytes_accessed=2**23,
    )
    keep = keep + lax.ppermute(give, "core", SWAP).astype(f32)
    parts = lax.all_to_all(keep.astype(bf16).reshape(plane, columns, depth), PLANE, 0, 0)
    tgt_pull = jnp.sum(parts.astype(f32), axis=0)
    pad = jnp.zeros((half, depth), f32)
    up = jnp.concatenate([up.astype(f32), pad])
    down = jnp.concatenate([pad, down.astype(f32)])
    for k in (2, 1, 0):
        up = shift((up + terms[2 * k]).astype(bf16), 1).astype(f32)
        down = shift((down + terms[2 * k + 1]).astype(bf16), -1).astype(f32)
    src_pull = own_term + up + down
    row_cost = jnp.sum(src_pull * src_emb.astype(f32), axis=1) * (-1.0 / math.sqrt(depth))
    return (src_pull, tgt_pull, row_cost)


def solution(mesh):
    split = Mesh(mesh.devices.reshape(SIZES), AXES)
    return jax.shard_map(
        shards,
        mesh=split,
        in_specs=(P(ROW + COL, None), P(COL + ROW, None), P(ROW), P(COL)),
        out_specs=(P(ROW + COL, None), P(COL + ROW, None), P(ROW + COL)),
        check_vma=False,
    )
```

```python
import functools
import math

import jax
import jax.numpy as jnp
from jax import lax
from jax.experimental import pallas as pl
from jax.experimental.pallas import tpu as pltpu
from jax.sharding import Mesh, PartitionSpec as P

ITERS = 3
NEG = -1e30
EPSILON = 0.5
LOG2E = math.log2(math.e)
LANES = 128
DISTANCES = (1, 7, 2, 6, 3, 5, 0, 4)

AXES = ("x", "zh", "core", "zl", "y")
SIZES = (4, 4, 2, 2, 4)
ROW = ("x", "zh", "core")
COL = ("zl", "y")
RING = ("zh", "zl")
PLANE = ("x", "y")
SPREAD = ("x", "y", "core")
SWAP = [(0, 1), (1, 0)]

VMEM = pl.BlockSpec(memory_space=pltpu.VMEM)
SMEM = pl.BlockSpec(memory_space=pltpu.SMEM)
IN_HBM = pl.BlockSpec(memory_space=pl.ANY)
CONTRACT_LAST = (((1,), (1,)), ((), ()))


def dot(a, b, dims=(((1,), (0,)), ((), ()))):
    return lax.dot_general(a, b, dims, preferred_element_type=jnp.float32)


def call(kernel, outs, scratch, *operands, smem=0, in_hbm=(), outs_in_hbm=(), flops=0, bytes_accessed=0):
    specs = [
        SMEM if k < smem else IN_HBM if k in in_hbm else VMEM for k in range(len(operands))
    ]
    operands = [
        pltpu.with_memory_space_constraint(v, pltpu.HBM) if k in in_hbm else v
        for k, v in enumerate(operands)
    ]
    outs = [
        pltpu.HBM(out.shape, out.dtype) if k in outs_in_hbm else out for k, out in enumerate(outs)
    ]
    return pl.pallas_call(
        kernel,
        out_shape=outs,
        in_specs=specs,
        out_specs=[IN_HBM if k in outs_in_hbm else VMEM for k in range(len(outs))],
        scratch_shapes=scratch,
        compiler_params=pltpu.CompilerParams(vmem_limit_bytes=16 * 2**20),
        cost_estimate=pl.CostEstimate(
            flops=flops, bytes_accessed=bytes_accessed, transcendentals=0
        ),
    )(*operands)


def shift(value, step):
    size = lax.axis_size(RING)
    return lax.ppermute(value, RING, [(i, (i + step) % size) for i in range(size)])


def copy_all(pairs, sems):
    copies = [pltpu.make_async_copy(a, b, sems.at[k]) for k, (a, b) in enumerate(pairs)]
    for copy in copies:
        copy.start()
    for copy in copies:
        copy.wait()


def one_hot(line, dtype):
    labels = jnp.broadcast_to(line.astype(jnp.float32), (LANES, LANES)).T
    lanes = lax.broadcasted_iota(jnp.int32, (LANES, LANES), 1).astype(jnp.float32)
    return (labels == lanes).astype(dtype)


def label_kernel(offsets, src_lang, tgt_lang, src, tgt, src_out, tgt_out, src_labels, tgt_labels, hot, one, sems):
    columns, depth = tgt.shape
    copy_all([(tgt_lang, tgt_labels), (tgt, one.at[:, :depth]), (src_lang, src_labels)], sems)
    bulk = pltpu.make_async_copy(src, src_out.at[:, :depth], sems.at[0])
    bulk.start()
    here = offsets[3] * columns
    hot[...] = one_hot(tgt_labels[pl.ds(here // LANES, 1), :], jnp.float32)
    one[:, depth:] = hot[pl.ds(pl.multiple_of(lax.rem(here, LANES), columns), columns), :].astype(one.dtype)
    bulk.wait()
    copies = [
        pltpu.make_async_copy(one, tgt_out.at[k], sems.at[k]) for k in range(tgt_out.shape[0])
    ]
    for copy in copies:
        copy.start()
    src_out[:, depth:] = one_hot(src_labels[pl.ds(offsets[2], 1), :], src_out.dtype)
    for copy in copies:
        copy.wait()


def columns_sums(tables, added):
    tiles = tables[0].shape[1] // LANES

    def blocks(t):
        start = 0
        for table in tables:
            for c in range(table.shape[0] // LANES):
                z = table[c * LANES : (c + 1) * LANES, t * LANES : (t + 1) * LANES]
                if added is not None:
                    z = z + added[start : start + LANES, :]
                start += LANES
                yield z.reshape(LANES // 8, 8, LANES)

    tops, totals = [], []
    for t in range(tiles):
        top = functools.reduce(jnp.maximum, (jnp.max(z, axis=0) for z in blocks(t)))
        top = jnp.max(top, axis=0, keepdims=True)
        total = functools.reduce(
            jnp.add, (jnp.sum(jnp.exp2(z - top[None]), axis=0) for z in blocks(t))
        )
        tops.append(top)
        totals.append(jnp.sum(total, axis=0, keepdims=True))
    return tops, totals


def columns_lse(tables, added):
    return [top + jnp.log2(total) for top, total in zip(*columns_sums(tables, added))]


def send_out(parts, offset, table, order, out):
    for part, at in zip(parts, table):
        order[pl.ds(lax.rem(at + offset, 8), 1), :] = part
    out[...] = jnp.broadcast_to(order[...][None], out.shape)


def merge(gathered, log_count, offset, table, order):
    parts = gathered[...]
    top = jnp.max(parts, axis=0)
    total = jnp.sum(jnp.exp2(parts - top[None]), axis=0)
    order[...] = log_count - (top + jnp.log2(total))
    return jnp.concatenate([order[pl.ds(lax.rem(at + offset, 8), 1), :] for at in table])


def spread(pots, wide):
    columns = pots.T
    for c in range(8):
        wide[c * LANES : (c + 1) * LANES, :] = jnp.broadcast_to(
            columns[:, c : c + 1], (LANES, LANES)
        )


def make_logits(scale, src, tgt, logits, logits_t):
    depth = src.shape[1] - LANES
    half = tgt.shape[0] // 2
    emb, hot = src[:, :depth], src[:, depth:]
    for side in range(2):
        to = slice(side * half, (side + 1) * half)
        tgt_emb, tgt_hot = tgt[to, :depth], tgt[to, depth:]
        same = dot(tgt_hot, hot, CONTRACT_LAST) > 0.5
        logits_t[to, :] = jnp.where(same, dot(tgt_emb, emb, CONTRACT_LAST) * scale, NEG)
        same = dot(hot, tgt_hot, CONTRACT_LAST) > 0.5
        logits[:, to] = jnp.where(same, dot(emb, tgt_emb, CONTRACT_LAST) * scale, NEG)


def first_pair_kernel(scale, near, other, mine, theirs, src, logits, logits_t, part, tgt, sems):
    half = mine.shape[0]
    copy_all(
        [
            (mine, tgt.at[:half]),
            (theirs, tgt.at[half:]),
            (near, src.at[: near.shape[0]]),
            (other, src.at[near.shape[0] :]),
        ],
        sems,
    )
    make_logits(scale, src, tgt, logits, logits_t)
    part[...] = jnp.concatenate(columns_lse([logits_t], None))


def halves_kernel(up, down, up_out, down_out, sems):
    half = up_out.shape[0]
    copy_all([(up.at[:half], up_out), (down.at[half:], down_out)], sems)


def pair_kernel(scale, near, other, tgt, src, logits, logits_t, part, sems):
    copy_all([(near, src.at[: near.shape[0]]), (other, src.at[near.shape[0] :])], sems)
    make_logits(scale, src, tgt, logits, logits_t)
    part[...] = jnp.concatenate(columns_lse([logits_t], None))


def last_pair_kernel(scale, offsets, own, far_up, far_down, tgt, *refs):
    parts, (src, logits, logits_t, out, order, sems) = refs[:3], refs[3:]
    rows, half = own.shape[0], far_up.shape[0]
    copy_all(
        [
            (own, src.at[:rows]),
            (far_up, src.at[rows : rows + half]),
            (far_down, src.at[rows + half :]),
        ],
        sems,
    )
    make_logits(scale, src, tgt, logits, logits_t)
    parts = [part[r : r + 1, :] for part in parts for r in range(2)]
    send_out(parts + columns_lse([logits_t], None), offsets[0], DISTANCES, order, out)


def src_pots_kernel(log_count, offsets, *refs):
    tables, (gathered, out, pots, order, wide) = refs[:4], refs[4:]
    local = merge(gathered, log_count, offsets[0], DISTANCES, order)
    pots[...] = local
    spread(local, wide)
    send_out(columns_lse(tables, wide), offsets[1], range(8), order, out)


def tgt_pots_kernel(log_count, offsets, *refs):
    tables, (gathered, out, order, wide) = refs[:4], refs[4:]
    spread(merge(gathered, log_count, offsets[1], range(8), order), wide)
    parts = [part for table in tables for part in columns_lse([table], wide)]
    send_out(parts, offsets[0], DISTANCES, order, out)


def src_kernel(log_count, share, units, offsets, *refs):
    n = len(units)
    tables, (tgt_pots, src_pots, block), outs = refs[:n], refs[n : n + 3], refs[n + 3 : -2]
    order, wide = refs[-2:]
    depth, half = outs[0].shape[1], block.shape[0] // 2
    if log_count is None:
        tgt = tgt_pots[...]
    else:
        tgt = merge(tgt_pots, log_count, offsets[1], range(8), order)
        outs[-1][...] = tgt
        outs = outs[:-1]
    spread(src_pots[...], wide)
    for k, (unit, table) in enumerate(zip(units, tables)):
        at = slice(unit * 256, (unit + 1) * 256)
        weight = [
            jnp.exp2(table[:, t * LANES : (t + 1) * LANES] + wide[at, :] + tgt[t : t + 1, :])
            .astype(jnp.bfloat16)
            for t in range(8)
        ]
        first = jnp.concatenate(weight[:4], axis=1)
        second = jnp.concatenate(weight[4:], axis=1)
        pull = (dot(first, block[:half, :depth]) + dot(second, block[half:, :depth])) * share
        start = 0
        for out in outs[2 * k : 2 * k + 2 + len(outs) % 2]:
            out[...] = pull[start : start + out.shape[0]].astype(out.dtype)
            start += out.shape[0]


def tgt_kernel(share, *refs):
    tables, (tgt_pots, src_pots), blocks = refs[:4], refs[4:6], refs[6:10]
    keep, give, wide = refs[10:]
    spread(tgt_pots[...], wide)
    src = src_pots[...]
    for unit in (2, 3, 0, 1):
        at = slice(unit * 256, (unit + 1) * 256)
        pull = 0.0
        for k, (table, block) in enumerate(zip(tables, blocks)):
            weight = [
                jnp.exp2(table[at, t * LANES : (t + 1) * LANES] + src[2 * k + t : 2 * k + t + 1, :] + wide[at, :])
                .astype(jnp.bfloat16)
                for t in range(2)
            ]
            pull = pull + dot(jnp.concatenate(weight, axis=1), block[:, : keep.shape[1]])
        to = slice((unit % 2) * 256, (unit % 2 + 1) * 256)
        if unit < 2:
            keep[to, :] = pull * share
        else:
            give[to, :] = (pull * share).astype(give.dtype)


def add_cores_kernel(keep, taken, out, total, sems):
    rows = keep.shape[0] // sems.shape[0]
    copies = []
    for c in range(sems.shape[0]):
        at = slice(c * rows, (c + 1) * rows)
        total[at, :] = (keep[at, :] + taken[at, :].astype(jnp.float32)).astype(total.dtype)
        copies.append(pltpu.make_async_copy(total.at[at], out.at[at], sems.at[c]))
        copies[-1].start()
    for copy in copies:
        copy.wait()


def first_add_kernel(up, up_term, down, down_term, up_out, down_out):
    half = up.shape[0]
    up_out[:half, :] = (up_term[:half, :] + up[...].astype(jnp.float32)).astype(up_out.dtype)
    up_out[half:, :] = up_term[half:, :].astype(up_out.dtype)
    down_out[:half, :] = down_term[:half, :].astype(down_out.dtype)
    down_out[half:, :] = (down_term[half:, :] + down[...].astype(jnp.float32)).astype(down_out.dtype)


def add_kernel(up, up_term, down, down_term, up_out, down_out):
    for out, term, add in ((up_out, up_term, up), (down_out, down_term, down)):
        out[...] = (term[...] + add[...].astype(jnp.float32)).astype(out.dtype)


def shards(src_emb, tgt_emb, src_lang, tgt_lang):
    f32, bf16 = jnp.float32, jnp.bfloat16
    rows, depth = src_emb.shape
    columns = tgt_emb.shape[0]
    row, col = lax.axis_index(ROW), lax.axis_index(COL)
    ring, plane = lax.axis_size(RING), lax.axis_size(PLANE)
    spread_size = lax.axis_size(SPREAD)
    n_src, n_tgt = rows * ring, columns * spread_size
    place, core = lax.axis_index(RING), lax.axis_index("core")
    total_src = src_lang.shape[0] * lax.axis_size(ROW)
    total_tgt = tgt_lang.shape[0] * lax.axis_size(COL)
    offsets = jnp.stack([place, 4 * core, col, row]).astype(jnp.int32)

    n_label = depth + LANES
    dma = pltpu.SemaphoreType.DMA
    own, tgt = call(
        label_kernel,
        [jax.ShapeDtypeStruct((rows, n_label), bf16), jax.ShapeDtypeStruct((plane, columns, n_label), bf16)],
        [
            pltpu.VMEM((src_lang.shape[0] // LANES, LANES), jnp.int32),
            pltpu.VMEM((tgt_lang.shape[0] // LANES, LANES), jnp.int32),
            pltpu.VMEM((LANES, LANES), f32), pltpu.VMEM((columns, n_label), bf16), dma((plane,)),
        ],
        offsets, src_lang.reshape(-1, LANES), tgt_lang.reshape(-1, LANES), src_emb, tgt_emb,
        smem=1, in_hbm=range(1, 5), outs_in_hbm=(1,), flops=1, bytes_accessed=2**20,
    )
    mine = lax.all_to_all(tgt, PLANE, 0, 0)
    up, down = shift(own, 1), shift(own, -1)
    pairs = [(down, up)]
    up, down = shift(up, 1), shift(down, -1)
    mine, up, down = lax.optimization_barrier((mine, up, down))
    pairs.append((down, up))
    theirs = lax.ppermute(mine, "core", SWAP)
    mine, theirs = (v.reshape(plane * columns, -1) for v in (mine, theirs))
    up, down = shift(up, 1), shift(down, -1)

    order = pltpu.VMEM((8, LANES), f32)
    pots = jax.ShapeDtypeStruct((8, LANES), f32)
    to_ring = jax.ShapeDtypeStruct((ring, 8, LANES), f32)
    to_spread = jax.ShapeDtypeStruct((spread_size, 8, LANES), f32)
    pair = [
        jax.ShapeDtypeStruct((2 * rows, n_label), bf16),
        jax.ShapeDtypeStruct((2 * rows, n_tgt), f32),
        jax.ShapeDtypeStruct((n_tgt, 2 * rows), f32),
    ]
    pair_part = jax.ShapeDtypeStruct((2, LANES), f32)
    matmul = 2 * n_src * n_tgt * depth
    scale = LOG2E / (EPSILON * math.sqrt(depth))
    cost = dict(flops=matmul // 2, bytes_accessed=2**22)
    *first, tgt_block = call(
        functools.partial(first_pair_kernel, scale),
        [*pair, pair_part, jax.ShapeDtypeStruct((n_tgt, n_label), bf16)], [dma((4,))],
        *pairs[0], mine, theirs, in_hbm=range(3), **cost,
    )

    def pair_logits(near, other, in_hbm):
        return call(
            functools.partial(pair_kernel, scale),
            [*pair, pair_part], [dma((2,))],
            near, other, tgt_block, in_hbm=in_hbm, **cost,
        )

    made = [list(first), list(pair_logits(*pairs[1], range(2)))]
    made[0][3], made[1][3], up, down = lax.optimization_barrier((made[0][3], made[1][3], up, down))
    made.append(pair_logits(down, up, ()))
    half = rows // 2
    far = [jax.ShapeDtypeStruct((half, n_label), bf16)] * 2
    up, down = call(halves_kernel, far, [dma((2,))], up, down, flops=1, bytes_accessed=1)
    far = shift(up, 1), shift(down, -1)
    *last, part = call(
        functools.partial(last_pair_kernel, scale),
        [*pair, to_ring], [order, dma((3,))],
        offsets, own, *far, tgt_block, *(m[3] for m in made),
        smem=1, in_hbm=(1,), **cost,
    )
    made.append(last)
    src_blocks, logits, logits_t = ([m[k] for m in made] for k in range(3))
    wide_src = pltpu.VMEM((n_src, LANES), f32)
    wide_tgt = pltpu.VMEM((n_tgt, LANES), f32)
    for step in range(ITERS):
        gathered = lax.all_to_all(part, RING, 0, 0)
        part, src_pots = call(
            functools.partial(src_pots_kernel, math.log2(total_tgt)),
            [to_spread, pots], [order, wide_src],
            offsets, *logits, gathered, smem=1, flops=8 * n_src * n_tgt, bytes_accessed=2**22,
        )
        gathered = lax.all_to_all(part, SPREAD, 0, 0)
        if step < ITERS - 1:
            (part,) = call(
                functools.partial(tgt_pots_kernel, math.log2(total_src)),
                [to_ring], [order, wide_tgt],
                offsets, *logits_t, gathered, smem=1, flops=8 * n_src * n_tgt, bytes_accessed=2**22,
            )
    term = jax.ShapeDtypeStruct((rows, depth), f32)

    def src_terms(log_count, units, tgt_pots, kinds):
        return call(
            functools.partial(src_kernel, log_count, 1.0 / total_tgt, units),
            kinds, [order, wide_src],
            offsets, *(logits[u] for u in units), tgt_pots, src_pots, tgt_block,
            smem=1, flops=len(units) * matmul // 4, bytes_accessed=2**22,
        )

    low = jax.ShapeDtypeStruct((rows, depth), bf16)
    far = [jax.ShapeDtypeStruct((half, depth), bf16)] * 2
    own_term, up, down, tgt_pots = src_terms(math.log2(total_src), (3,), gathered, [term, *far, pots])
    up, down = shift(up, 1), shift(down, -1)
    terms = src_terms(None, (0, 1, 2), tgt_pots, [term] * 6)
    keep, give = call(
        functools.partial(tgt_kernel, 1.0 / total_src),
        [jax.ShapeDtypeStruct((n_tgt // 2, depth), f32), jax.ShapeDtypeStruct((n_tgt // 2, depth), bf16)],
        [wide_tgt],
        *logits_t, tgt_pots, src_pots, *src_blocks,
        flops=matmul, bytes_accessed=2**23,
    )
    taken = lax.ppermute(give, "core", SWAP)
    keep, taken, up, down, *terms = lax.optimization_barrier((keep, taken, up, down, *terms))
    shares = jax.ShapeDtypeStruct((n_tgt // 2, depth), bf16)
    (sent,) = call(
        add_cores_kernel, [shares], [pltpu.VMEM(shares.shape, bf16), dma((4,))],
        keep, taken, outs_in_hbm=(0,), flops=n_tgt * depth, bytes_accessed=2**22,
    )
    parts = lax.all_to_all(sent.reshape(plane, columns, depth), PLANE, 0, 0)
    for k in (2, 1, 0):
        up, down = call(
            first_add_kernel if k == 2 else add_kernel, [low] * 2, [],
            up, terms[2 * k], down, terms[2 * k + 1], flops=1, bytes_accessed=2**20,
        )
        if k == 0:
            parts, up, down = lax.optimization_barrier((parts, up, down))
        up, down = shift(up, 1), shift(down, -1)
    tgt_pull = jnp.sum(parts.astype(f32), axis=0)
    src_pull = own_term + up.astype(f32) + down.astype(f32)
    row_cost = jnp.sum(src_pull * src_emb.astype(f32), axis=1) * (-1.0 / math.sqrt(depth))
    return (src_pull, tgt_pull, row_cost)


def solution(mesh):
    split = Mesh(mesh.devices.reshape(SIZES), AXES)
    return jax.shard_map(
        shards,
        mesh=split,
        in_specs=(P(ROW + COL, None), P(COL + ROW, None), P(ROW), P(COL)),
        out_specs=(P(ROW + COL, None), P(COL + ROW, None), P(ROW + COL)),
        check_vma=False,
    )
```

```python
import functools
import math

import jax
import jax.numpy as jnp
from jax import lax
from jax.experimental import pallas as pl
from jax.experimental.pallas import tpu as pltpu
from jax.sharding import Mesh, PartitionSpec as P

ITERS = 3
NEG = -1e30
EPSILON = 0.5
LOG2E = math.log2(math.e)
LANES = 128
DISTANCES = (1, 7, 2, 6, 3, 5, 0, 4)

AXES = ("x", "zh", "core", "zl", "y")
SIZES = (4, 4, 2, 2, 4)
ROW = ("x", "zh", "core")
COL = ("zl", "y")
RING = ("zh", "zl")
PLANE = ("x", "y")
SPREAD = ("x", "y", "core")
SWAP = [(0, 1), (1, 0)]

VMEM = pl.BlockSpec(memory_space=pltpu.VMEM)
SMEM = pl.BlockSpec(memory_space=pltpu.SMEM)
IN_HBM = pl.BlockSpec(memory_space=pl.ANY)
CONTRACT_LAST = (((1,), (1,)), ((), ()))


def dot(a, b, dims=(((1,), (0,)), ((), ()))):
    return lax.dot_general(a, b, dims, preferred_element_type=jnp.float32)


def call(kernel, outs, scratch, *operands, smem=0, in_hbm=(), outs_in_hbm=(), flops=0, bytes_accessed=0):
    specs = [
        SMEM if k < smem else IN_HBM if k in in_hbm else VMEM for k in range(len(operands))
    ]
    operands = [
        pltpu.with_memory_space_constraint(v, pltpu.HBM) if k in in_hbm else v
        for k, v in enumerate(operands)
    ]
    outs = [
        pltpu.HBM(out.shape, out.dtype) if k in outs_in_hbm else out for k, out in enumerate(outs)
    ]
    return pl.pallas_call(
        kernel,
        out_shape=outs,
        in_specs=specs,
        out_specs=[IN_HBM if k in outs_in_hbm else VMEM for k in range(len(outs))],
        scratch_shapes=scratch,
        compiler_params=pltpu.CompilerParams(vmem_limit_bytes=16 * 2**20),
        cost_estimate=pl.CostEstimate(
            flops=flops, bytes_accessed=bytes_accessed, transcendentals=0
        ),
    )(*operands)


def shift(value, step):
    size = lax.axis_size(RING)
    return lax.ppermute(value, RING, [(i, (i + step) % size) for i in range(size)])


def copy_all(pairs, sems):
    copies = [pltpu.make_async_copy(a, b, sems.at[k]) for k, (a, b) in enumerate(pairs)]
    for copy in copies:
        copy.start()
    for copy in copies:
        copy.wait()


def one_hot(line, dtype):
    labels = jnp.broadcast_to(line.astype(jnp.float32), (LANES, LANES)).T
    lanes = lax.broadcasted_iota(jnp.int32, (LANES, LANES), 1).astype(jnp.float32)
    return (labels == lanes).astype(dtype)


def label_kernel(offsets, src_lang, tgt_lang, src, tgt, src_out, tgt_out, src_labels, tgt_labels, hot, sems):
    columns, depth = tgt.shape
    copies = [
        pltpu.make_async_copy(a, b, sems.at[k])
        for k, (a, b) in enumerate(
            [
                (tgt_lang, tgt_labels),
                (src_lang, src_labels),
                (tgt, tgt_out.at[:, :depth]),
                (src, src_out.at[:, :depth]),
            ]
        )
    ]
    for copy in copies:
        copy.start()
    copies[0].wait()
    here = offsets[3] * columns
    hot[...] = one_hot(tgt_labels[pl.ds(here // LANES, 1), :], jnp.float32)
    tgt_out[:, depth:] = hot[pl.ds(pl.multiple_of(lax.rem(here, LANES), columns), columns), :].astype(tgt_out.dtype)
    copies[1].wait()
    src_out[:, depth:] = one_hot(src_labels[pl.ds(offsets[2], 1), :], src_out.dtype)
    copies[2].wait()
    copies[3].wait()


def assemble_kernel(axis, offsets, *refs):
    (*blocks, out, sems), n = refs, len(refs) - 2
    rows = blocks[0].shape[0]
    places = [lax.rem(offsets[axis] + k, n) * rows for k in range(n)]
    copy_all(
        [(block, out.at[pl.ds(pl.multiple_of(at, rows), rows)]) for block, at in zip(blocks, places)],
        sems,
    )


def columns_sums(tables, added):
    tiles = tables[0].shape[1] // LANES

    def blocks(t):
        start = 0
        for table in tables:
            for c in range(table.shape[0] // LANES):
                z = table[c * LANES : (c + 1) * LANES, t * LANES : (t + 1) * LANES]
                if added is not None:
                    z = z + added[start : start + LANES, :]
                start += LANES
                yield z.reshape(LANES // 8, 8, LANES)

    tops, totals = [], []
    for t in range(tiles):
        top = functools.reduce(jnp.maximum, (jnp.max(z, axis=0) for z in blocks(t)))
        top = jnp.max(top, axis=0, keepdims=True)
        total = functools.reduce(
            jnp.add, (jnp.sum(jnp.exp2(z - top[None]), axis=0) for z in blocks(t))
        )
        tops.append(top)
        totals.append(jnp.sum(total, axis=0, keepdims=True))
    return tops, totals


def columns_lse(tables, added):
    return [top + jnp.log2(total) for top, total in zip(*columns_sums(tables, added))]


def send_out(parts, offset, table, order, out):
    for part, at in zip(parts, table):
        order[pl.ds(lax.rem(at + offset, 8), 1), :] = part
    out[...] = jnp.broadcast_to(order[...][None], out.shape)


def merge(gathered, log_count, offset, table, order):
    parts = gathered[...]
    top = jnp.max(parts, axis=0)
    total = jnp.sum(jnp.exp2(parts - top[None]), axis=0)
    order[...] = log_count - (top + jnp.log2(total))
    return jnp.concatenate([order[pl.ds(lax.rem(at + offset, 8), 1), :] for at in table])


def spread(pots, wide):
    columns = pots.T
    for c in range(8):
        wide[c * LANES : (c + 1) * LANES, :] = jnp.broadcast_to(
            columns[:, c : c + 1], (LANES, LANES)
        )


def make_logits(scale, src, tgt, logits, logits_t):
    depth = src.shape[1] - LANES
    emb, hot = src[:, :depth], src[:, depth:]
    step = 256
    for start in range(0, tgt.shape[0], step):
        to = slice(start, start + step)
        same = dot(tgt[to, depth:], hot, CONTRACT_LAST) > 0.5
        value = jnp.where(same, dot(tgt[to, :depth], emb, CONTRACT_LAST) * scale, NEG)
        logits_t[to, :] = value
        logits[:, to] = value.T


def first_pair_kernel(scale, near, other, mine, theirs, src, logits, logits_t, part, tgt, sems):
    half = mine.shape[0]
    copy_all(
        [
            (mine, tgt.at[:half]),
            (theirs, tgt.at[half:]),
            (near, src.at[: near.shape[0]]),
            (other, src.at[near.shape[0] :]),
        ],
        sems,
    )
    make_logits(scale, src, tgt, logits, logits_t)
    part[...] = jnp.concatenate(columns_lse([logits_t], None))


def halves_kernel(up, down, up_out, down_out, sems):
    half = up_out.shape[0]
    copy_all([(up.at[:half], up_out), (down.at[half:], down_out)], sems)


def pair_kernel(scale, near, other, tgt, src, logits, logits_t, part, sems):
    copy_all([(near, src.at[: near.shape[0]]), (other, src.at[near.shape[0] :])], sems)
    make_logits(scale, src, tgt, logits, logits_t)
    part[...] = jnp.concatenate(columns_lse([logits_t], None))


def own_kernel(scale, own, tgt, src, logits, logits_t, part, sems):
    copy_all([(own, src)], sems)
    make_logits(scale, src, tgt, logits, logits_t)
    part[...] = jnp.concatenate(columns_lse([logits_t], None))


def far_kernel(scale, offsets, far_up, far_down, tgt, *refs):
    parts, (src, logits, logits_t, out, order, sems) = refs[:4], refs[4:]
    half = far_up.shape[0]
    copy_all([(far_up, src.at[:half]), (far_down, src.at[half:])], sems)
    make_logits(scale, src, tgt, logits, logits_t)
    parts = [part[r : r + 1, :] for part in parts for r in range(part.shape[0])]
    send_out(parts + columns_lse([logits_t], None), offsets[0], DISTANCES, order, out)


def src_pots_kernel(log_count, offsets, *refs):
    tables, (gathered, out, pots, order, wide) = refs[:5], refs[5:]
    local = merge(gathered, log_count, offsets[0], DISTANCES, order)
    pots[...] = local
    spread(local, wide)
    send_out(columns_lse(tables, wide), offsets[1], range(8), order, out)


def tgt_pots_kernel(log_count, offsets, *refs):
    tables, (gathered, out, order, wide) = refs[:5], refs[5:]
    spread(merge(gathered, log_count, offsets[1], range(8), order), wide)
    parts = [part for table in tables for part in columns_lse([table], wide)]
    send_out(parts, offsets[0], DISTANCES, order, out)


def src_kernel(log_count, share, pieces, offsets, *refs):
    n = len(pieces)
    tables, (tgt_pots, src_pots, block), outs = refs[:n], refs[n : n + 3], refs[n + 3 : -2]
    order, wide = refs[-2:]
    depth, half = outs[0].shape[1], block.shape[0] // 2
    if log_count is None:
        tgt = tgt_pots[...]
    else:
        tgt = merge(tgt_pots, log_count, offsets[1], range(8), order)
        outs[-1][...] = tgt
        outs = outs[:-1]
    spread(src_pots[...], wide)
    outs = list(outs)
    for (first, rows, place), table in zip(pieces, tables):
        at = slice(place, place + rows)
        weight = [
            jnp.exp2(table[first : first + rows, t * LANES : (t + 1) * LANES] + wide[at, :] + tgt[t : t + 1, :])
            .astype(jnp.bfloat16)
            for t in range(8)
        ]
        left = jnp.concatenate(weight[:4], axis=1)
        right = jnp.concatenate(weight[4:], axis=1)
        pull = (dot(left, block[:half, :depth]) + dot(right, block[half:, :depth])) * share
        start = 0
        while start < rows:
            out = outs.pop(0)
            out[...] = pull[start : start + out.shape[0]].astype(out.dtype)
            start += out.shape[0]


def tgt_kernel(share, *refs):
    tables, (tgt_pots, src_pots), blocks = refs[:5], refs[5:7], refs[7:12]
    keep, give, wide = refs[12:]
    spread(tgt_pots[...], wide)
    src = src_pots[...]
    depth = keep.shape[1]
    for unit in (2, 3, 0, 1):
        at = slice(unit * 256, (unit + 1) * 256)
        weight, line = [], 0
        for table in tables:
            for t in range(table.shape[1] // LANES):
                z = table[at, t * LANES : (t + 1) * LANES] + src[line : line + 1, :] + wide[at, :]
                weight.append(jnp.exp2(z).astype(jnp.bfloat16))
                line += 1
        pull = 0.0
        for k in range(3):
            pull = pull + dot(jnp.concatenate(weight[2 * k : 2 * k + 2], axis=1), blocks[k][:, :depth])
        last = jnp.concatenate([blocks[3][:, :depth], blocks[4][:, :depth]])
        pull = pull + dot(jnp.concatenate(weight[6:], axis=1), last)
        to = slice((unit % 2) * 256, (unit % 2 + 1) * 256)
        if unit < 2:
            keep[to, :] = pull * share
        else:
            give[to, :] = (pull * share).astype(give.dtype)


def add_cores_kernel(keep, taken, out, total, sems):
    rows = keep.shape[0] // sems.shape[0]
    copies = []
    for c in range(sems.shape[0]):
        at = slice(c * rows, (c + 1) * rows)
        total[at, :] = (keep[at, :] + taken[at, :].astype(jnp.float32)).astype(total.dtype)
        copies.append(pltpu.make_async_copy(total.at[at], out.at[at], sems.at[c]))
        copies[-1].start()
    for copy in copies:
        copy.wait()


def first_add_kernel(up, up_term, down, down_term, up_out, down_out):
    half = up.shape[0]
    up_out[:half, :] = (up_term[:half, :] + up[...].astype(jnp.float32)).astype(up_out.dtype)
    up_out[half:, :] = up_term[half:, :].astype(up_out.dtype)
    down_out[:half, :] = down_term[:half, :].astype(down_out.dtype)
    down_out[half:, :] = (down_term[half:, :] + down[...].astype(jnp.float32)).astype(down_out.dtype)


def add_kernel(up, up_term, down, down_term, up_out, down_out):
    for out, term, add in ((up_out, up_term, up), (down_out, down_term, down)):
        out[...] = (term[...] + add[...].astype(jnp.float32)).astype(out.dtype)


def shards(src_emb, tgt_emb, src_lang, tgt_lang):
    f32, bf16 = jnp.float32, jnp.bfloat16
    rows, depth = src_emb.shape
    columns = tgt_emb.shape[0]
    row, col = lax.axis_index(ROW), lax.axis_index(COL)
    ring, plane = lax.axis_size(RING), lax.axis_size(PLANE)
    spread_size = lax.axis_size(SPREAD)
    n_src, n_tgt = rows * ring, columns * spread_size
    place, core = lax.axis_index(RING), lax.axis_index("core")
    total_src = src_lang.shape[0] * lax.axis_size(ROW)
    total_tgt = tgt_lang.shape[0] * lax.axis_size(COL)
    offsets = jnp.stack(
        [place, 4 * core, col, row, lax.axis_index("x"), lax.axis_index("y")]
    ).astype(jnp.int32)

    n_label = depth + LANES
    dma = pltpu.SemaphoreType.DMA
    own, tgt = call(
        label_kernel,
        [jax.ShapeDtypeStruct((rows, n_label), bf16), jax.ShapeDtypeStruct((columns, n_label), bf16)],
        [
            pltpu.VMEM((src_lang.shape[0] // LANES, LANES), jnp.int32),
            pltpu.VMEM((tgt_lang.shape[0] // LANES, LANES), jnp.int32),
            pltpu.VMEM((LANES, LANES), f32), dma((4,)),
        ],
        offsets, src_lang.reshape(-1, LANES), tgt_lang.reshape(-1, LANES), src_emb, tgt_emb,
        smem=1, in_hbm=range(1, 5), flops=1, bytes_accessed=2**20,
    )

    def gather_axis(block, axis, at):
        size = lax.axis_size(axis)
        found = [
            lax.ppermute(block, axis, [((i + k) % size, i) for i in range(size)]) for k in range(1, size)
        ]
        return call(
            functools.partial(assemble_kernel, at),
            [jax.ShapeDtypeStruct((size * block.shape[0], block.shape[1]), bf16)], [dma((size,))],
            offsets, block, *found, smem=1, flops=1, bytes_accessed=2**20,
        )[0]

    up, down = shift(own, 1), shift(own, -1)
    pairs = [(down, up)]
    block = gather_axis(tgt, "y", 5)
    block, up, down = lax.optimization_barrier((block, up, down))
    up, down = shift(up, 1), shift(down, -1)
    mine = gather_axis(block, "x", 4)
    pairs.append((down, up))
    up, down = shift(up, 1), shift(down, -1)
    mine, up, down = lax.optimization_barrier((mine, up, down))
    theirs = lax.ppermute(mine, "core", SWAP)

    order = pltpu.VMEM((8, LANES), f32)
    pots = jax.ShapeDtypeStruct((8, LANES), f32)
    to_ring = jax.ShapeDtypeStruct((ring, 8, LANES), f32)
    to_spread = jax.ShapeDtypeStruct((spread_size, 8, LANES), f32)
    pair = [
        jax.ShapeDtypeStruct((2 * rows, n_label), bf16),
        jax.ShapeDtypeStruct((2 * rows, n_tgt), f32),
        jax.ShapeDtypeStruct((n_tgt, 2 * rows), f32),
    ]
    pair_part = jax.ShapeDtypeStruct((2, LANES), f32)
    matmul = 2 * n_src * n_tgt * depth
    scale = LOG2E / (EPSILON * math.sqrt(depth))
    cost = dict(flops=matmul // 2, bytes_accessed=2**22)
    *first, tgt_block = call(
        functools.partial(first_pair_kernel, scale),
        [*pair, pair_part, jax.ShapeDtypeStruct((n_tgt, n_label), bf16)], [dma((4,))],
        *pairs[0], mine, theirs, **cost,
    )

    def pair_logits(near, other, in_hbm):
        return call(
            functools.partial(pair_kernel, scale),
            [*pair, pair_part], [dma((2,))],
            near, other, tgt_block, in_hbm=in_hbm, **cost,
        )

    made = [list(first), list(pair_logits(*pairs[1], ()))]
    made.append(pair_logits(down, up, ()))
    half = rows // 2
    far = [jax.ShapeDtypeStruct((half, n_label), bf16)] * 2
    up, down = call(halves_kernel, far, [dma((2,))], up, down, flops=1, bytes_accessed=1)
    far = shift(up, 1), shift(down, -1)
    single = [
        jax.ShapeDtypeStruct((rows, n_label), bf16),
        jax.ShapeDtypeStruct((rows, n_tgt), f32),
        jax.ShapeDtypeStruct((n_tgt, rows), f32),
    ]
    made.append(
        call(
            functools.partial(own_kernel, scale),
            [*single, jax.ShapeDtypeStruct((1, LANES), f32)], [dma((1,))],
            own, tgt_block, **cost,
        )
    )
    *last, part = call(
        functools.partial(far_kernel, scale),
        [*single, to_ring], [order, dma((2,))],
        offsets, *far, tgt_block, *(m[3] for m in made),
        smem=1, **cost,
    )
    made.append(last)
    src_blocks, logits, logits_t = ([m[k] for m in made] for k in range(3))
    wide_src = pltpu.VMEM((n_src, LANES), f32)
    wide_tgt = pltpu.VMEM((n_tgt, LANES), f32)
    for step in range(ITERS):
        gathered = lax.all_to_all(part, RING, 0, 0)
        part, src_pots = call(
            functools.partial(src_pots_kernel, math.log2(total_tgt)),
            [to_spread, pots], [order, wide_src],
            offsets, *logits, gathered, smem=1, flops=8 * n_src * n_tgt, bytes_accessed=2**22,
        )
        gathered = lax.all_to_all(part, SPREAD, 0, 0)
        if step < ITERS - 1:
            (part,) = call(
                functools.partial(tgt_pots_kernel, math.log2(total_src)),
                [to_ring], [order, wide_tgt],
                offsets, *logits_t, gathered, smem=1, flops=8 * n_src * n_tgt, bytes_accessed=2**22,
            )
    term = jax.ShapeDtypeStruct((rows, depth), f32)

    def src_terms(log_count, units, pieces, tgt_pots, kinds):
        return call(
            functools.partial(src_kernel, log_count, 1.0 / total_tgt, pieces),
            kinds, [order, wide_src],
            offsets, *(logits[u] for u in units), tgt_pots, src_pots, tgt_block,
            smem=1, flops=matmul // 4, bytes_accessed=2**22,
        )

    low = jax.ShapeDtypeStruct((rows, depth), bf16)
    far = [jax.ShapeDtypeStruct((half, depth), bf16)] * 2
    up, down, tgt_pots = src_terms(math.log2(total_src), (4,), [(0, rows, 7 * rows)], gathered, [*far, pots])
    up, down = shift(up, 1), shift(down, -1)
    pieces = [(0, 2 * rows, 0), (0, 2 * rows, 2 * rows), (0, 2 * rows, 4 * rows), (0, rows, 6 * rows)]
    *terms, own_term = src_terms(None, (0, 1, 2, 3), pieces, tgt_pots, [term] * 7)
    keep, give = call(
        functools.partial(tgt_kernel, 1.0 / total_src),
        [jax.ShapeDtypeStruct((n_tgt // 2, depth), f32), jax.ShapeDtypeStruct((n_tgt // 2, depth), bf16)],
        [wide_tgt],
        *logits_t, tgt_pots, src_pots, *src_blocks,
        flops=matmul, bytes_accessed=2**23,
    )
    taken = lax.ppermute(give, "core", SWAP)
    keep, taken, up, down, own_term, *terms = lax.optimization_barrier((keep, taken, up, down, own_term, *terms))
    shares = jax.ShapeDtypeStruct((n_tgt // 2, depth), bf16)
    (sent,) = call(
        add_cores_kernel, [shares], [pltpu.VMEM(shares.shape, bf16), dma((4,))],
        keep, taken, outs_in_hbm=(0,), flops=n_tgt * depth, bytes_accessed=2**22,
    )
    parts = lax.all_to_all(sent.reshape(plane, columns, depth), PLANE, 0, 0)
    for k in (2, 1, 0):
        up, down = call(
            first_add_kernel if k == 2 else add_kernel, [low] * 2, [],
            up, terms[2 * k], down, terms[2 * k + 1], flops=1, bytes_accessed=2**20,
        )
        if k == 0:
            parts, up, down = lax.optimization_barrier((parts, up, down))
        up, down = shift(up, 1), shift(down, -1)
    tgt_pull = jnp.sum(parts.astype(f32), axis=0)
    src_pull = own_term + up.astype(f32) + down.astype(f32)
    row_cost = jnp.sum(src_pull * src_emb.astype(f32), axis=1) * (-1.0 / math.sqrt(depth))
    return (src_pull, tgt_pull, row_cost)


def solution(mesh):
    split = Mesh(mesh.devices.reshape(SIZES), AXES)
    return jax.shard_map(
        shards,
        mesh=split,
        in_specs=(P(ROW + COL, None), P(COL + ROW, None), P(ROW), P(COL)),
        out_specs=(P(ROW + COL, None), P(COL + ROW, None), P(ROW + COL)),
        check_vma=False,
    )
```

```python
import functools
import math

import jax
import jax.numpy as jnp
from jax import lax
from jax.experimental import pallas as pl
from jax.experimental.pallas import tpu as pltpu
from jax.sharding import Mesh, PartitionSpec as P

ITERS = 3
NEG = -1e30
EPSILON = 0.5
LOG2E = math.log2(math.e)
LANES = 128
DISTANCES = (1, 7, 2, 6, 3, 5, 0, 4)

AXES = ("x", "zh", "core", "zl", "y")
SIZES = (4, 4, 2, 2, 4)
ROW = ("x", "zh", "core")
COL = ("zl", "y")
RING = ("zh", "zl")
PLANE = ("x", "y")
SPREAD = ("x", "y", "core")
SWAP = [(0, 1), (1, 0)]

VMEM = pl.BlockSpec(memory_space=pltpu.VMEM)
SMEM = pl.BlockSpec(memory_space=pltpu.SMEM)
IN_HBM = pl.BlockSpec(memory_space=pl.ANY)
CONTRACT_LAST = (((1,), (1,)), ((), ()))


def dot(a, b, dims=(((1,), (0,)), ((), ()))):
    return lax.dot_general(a, b, dims, preferred_element_type=jnp.float32)


def call(kernel, outs, scratch, *operands, smem=0, in_hbm=(), outs_in_hbm=(), flops=0, bytes_accessed=0):
    specs = [
        SMEM if k < smem else IN_HBM if k in in_hbm else VMEM for k in range(len(operands))
    ]
    operands = [
        pltpu.with_memory_space_constraint(v, pltpu.HBM) if k in in_hbm else v
        for k, v in enumerate(operands)
    ]
    outs = [
        pltpu.HBM(out.shape, out.dtype) if k in outs_in_hbm else out for k, out in enumerate(outs)
    ]
    return pl.pallas_call(
        kernel,
        out_shape=outs,
        in_specs=specs,
        out_specs=[IN_HBM if k in outs_in_hbm else VMEM for k in range(len(outs))],
        scratch_shapes=scratch,
        compiler_params=pltpu.CompilerParams(vmem_limit_bytes=16 * 2**20),
        cost_estimate=pl.CostEstimate(
            flops=flops, bytes_accessed=bytes_accessed, transcendentals=0
        ),
    )(*operands)


def shift(value, step):
    size = lax.axis_size(RING)
    return lax.ppermute(value, RING, [(i, (i + step) % size) for i in range(size)])


def copy_all(pairs, sems):
    copies = [pltpu.make_async_copy(a, b, sems.at[k]) for k, (a, b) in enumerate(pairs)]
    for copy in copies:
        copy.start()
    for copy in copies:
        copy.wait()


def one_hot(line, dtype):
    labels = jnp.broadcast_to(line.astype(jnp.float32), (LANES, LANES)).T
    lanes = lax.broadcasted_iota(jnp.int32, (LANES, LANES), 1).astype(jnp.float32)
    return (labels == lanes).astype(dtype)


def label_kernel(offsets, src_lang, tgt_lang, src, tgt, src_out, tgt_out, src_labels, tgt_labels, hot, sems):
    columns, depth = tgt.shape
    copies = [
        pltpu.make_async_copy(a, b, sems.at[k])
        for k, (a, b) in enumerate(
            [
                (tgt_lang, tgt_labels),
                (src_lang, src_labels),
                (tgt, tgt_out.at[:, :depth]),
                (src, src_out.at[:, :depth]),
            ]
        )
    ]
    for copy in copies:
        copy.start()
    copies[0].wait()
    here = offsets[3] * columns
    hot[...] = one_hot(tgt_labels[pl.ds(here // LANES, 1), :], jnp.float32)
    tgt_out[:, depth:] = hot[pl.ds(pl.multiple_of(lax.rem(here, LANES), columns), columns), :].astype(tgt_out.dtype)
    copies[1].wait()
    src_out[:, depth:] = one_hot(src_labels[pl.ds(offsets[2], 1), :], src_out.dtype)
    copies[2].wait()
    copies[3].wait()


def assemble_kernel(axis, offsets, *refs):
    (*blocks, out, sems), n = refs, len(refs) - 2
    rows = blocks[0].shape[0]
    places = [lax.rem(offsets[axis] + k, n) * rows for k in range(n)]
    copy_all(
        [(block, out.at[pl.ds(pl.multiple_of(at, rows), rows)]) for block, at in zip(blocks, places)],
        sems,
    )


def columns_sums(tables, added):
    tiles = tables[0].shape[1] // LANES

    def fold(start, join):
        results, row = start, 0
        for table in tables:
            for c in range(table.shape[0] // LANES):
                add = None if added is None else added[row : row + LANES, :]
                for t in range(tiles):
                    z = table[c * LANES : (c + 1) * LANES, t * LANES : (t + 1) * LANES]
                    z = (z if add is None else z + add).reshape(LANES // 8, 8, LANES)
                    results[t] = join(t, results[t], z)
                row += LANES
        return results

    def larger(t, top, z):
        z = jnp.max(z, axis=0)
        return z if top is None else jnp.maximum(top, z)

    tops = [jnp.max(top, axis=0, keepdims=True) for top in fold([None] * tiles, larger)]

    def total(t, so_far, z):
        z = jnp.sum(jnp.exp2(z - tops[t][None]), axis=0)
        return z if so_far is None else so_far + z

    totals = [jnp.sum(v, axis=0, keepdims=True) for v in fold([None] * tiles, total)]
    return tops, totals


def columns_lse(tables, added):
    return [top + jnp.log2(total) for top, total in zip(*columns_sums(tables, added))]


def send_out(parts, offset, table, order, out):
    for part, at in zip(parts, table):
        order[pl.ds(lax.rem(at + offset, 8), 1), :] = part
    out[...] = jnp.broadcast_to(order[...][None], out.shape)


def merge(gathered, log_count, offset, table, order):
    parts = gathered[...]
    top = jnp.max(parts, axis=0)
    total = jnp.sum(jnp.exp2(parts - top[None]), axis=0)
    order[...] = log_count - (top + jnp.log2(total))
    return jnp.concatenate([order[pl.ds(lax.rem(at + offset, 8), 1), :] for at in table])


def spread(pots, wide):
    columns = pots.T
    for c in range(8):
        wide[c * LANES : (c + 1) * LANES, :] = jnp.broadcast_to(
            columns[:, c : c + 1], (LANES, LANES)
        )


def make_logits(scale, src, tgt, logits, logits_t):
    depth = src.shape[1] - LANES
    emb, hot = src[:, :depth], src[:, depth:]
    step = 256
    for start in range(0, tgt.shape[0], step):
        to = slice(start, start + step)
        same = dot(tgt[to, depth:], hot, CONTRACT_LAST) > 0.5
        value = jnp.where(same, dot(tgt[to, :depth], emb, CONTRACT_LAST) * scale, NEG)
        logits_t[to, :] = value
        logits[:, to] = value.T


def first_pair_kernel(scale, near, other, mine, theirs, src, logits, logits_t, part, tgt, sems):
    half = mine.shape[0]
    copy_all(
        [
            (mine, tgt.at[:half]),
            (theirs, tgt.at[half:]),
            (near, src.at[: near.shape[0]]),
            (other, src.at[near.shape[0] :]),
        ],
        sems,
    )
    make_logits(scale, src, tgt, logits, logits_t)
    part[...] = jnp.concatenate(columns_lse([logits_t], None))


def halves_kernel(up, down, up_out, down_out, sems):
    half = up_out.shape[0]
    copy_all([(up.at[:half], up_out), (down.at[half:], down_out)], sems)


def pair_kernel(scale, near, other, tgt, src, logits, logits_t, part, sems):
    copy_all([(near, src.at[: near.shape[0]]), (other, src.at[near.shape[0] :])], sems)
    make_logits(scale, src, tgt, logits, logits_t)
    part[...] = jnp.concatenate(columns_lse([logits_t], None))


def own_kernel(scale, own, tgt, src, logits, logits_t, part, sems):
    copy_all([(own, src)], sems)
    make_logits(scale, src, tgt, logits, logits_t)
    part[...] = jnp.concatenate(columns_lse([logits_t], None))


def far_kernel(scale, offsets, far_up, far_down, tgt, *refs):
    parts, (src, logits, logits_t, out, order, sems) = refs[:4], refs[4:]
    half = far_up.shape[0]
    copy_all([(far_up, src.at[:half]), (far_down, src.at[half:])], sems)
    make_logits(scale, src, tgt, logits, logits_t)
    parts = [part[r : r + 1, :] for part in parts for r in range(part.shape[0])]
    send_out(parts + columns_lse([logits_t], None), offsets[0], DISTANCES, order, out)


def src_pots_kernel(log_count, offsets, *refs):
    tables, (gathered, out, pots, order, wide) = refs[:5], refs[5:]
    local = merge(gathered, log_count, offsets[0], DISTANCES, order)
    pots[...] = local
    spread(local, wide)
    send_out(columns_lse(tables, wide), offsets[1], range(8), order, out)


def tgt_pots_kernel(log_count, offsets, *refs):
    tables, (gathered, out, order, wide) = refs[:5], refs[5:]
    spread(merge(gathered, log_count, offsets[1], range(8), order), wide)
    parts = [part for table in tables for part in columns_lse([table], wide)]
    send_out(parts, offsets[0], DISTANCES, order, out)


def src_kernel(log_count, share, pieces, offsets, *refs):
    n = len(pieces)
    tables, (tgt_pots, src_pots, block), outs = refs[:n], refs[n : n + 3], refs[n + 3 : -2]
    order, wide = refs[-2:]
    depth, half = outs[0].shape[1], block.shape[0] // 2
    if log_count is None:
        tgt = tgt_pots[...]
    else:
        tgt = merge(tgt_pots, log_count, offsets[1], range(8), order)
        outs[-1][...] = tgt
        outs = outs[:-1]
    spread(src_pots[...], wide)
    outs = list(outs)
    for (first, rows, place), table in zip(pieces, tables):
        at = slice(place, place + rows)
        weight = [
            jnp.exp2(table[first : first + rows, t * LANES : (t + 1) * LANES] + wide[at, :] + tgt[t : t + 1, :])
            .astype(jnp.bfloat16)
            for t in range(8)
        ]
        left = jnp.concatenate(weight[:4], axis=1)
        right = jnp.concatenate(weight[4:], axis=1)
        pull = (dot(left, block[:half, :depth]) + dot(right, block[half:, :depth])) * share
        start = 0
        while start < rows:
            out = outs.pop(0)
            out[...] = pull[start : start + out.shape[0]].astype(out.dtype)
            start += out.shape[0]


def tgt_kernel(share, *refs):
    tables, (tgt_pots, src_pots), blocks = refs[:5], refs[5:7], refs[7:12]
    keep, give, wide = refs[12:]
    spread(tgt_pots[...], wide)
    src = src_pots[...]
    depth = keep.shape[1]
    for unit in (2, 3, 0, 1):
        at = slice(unit * 256, (unit + 1) * 256)
        weight, line = [], 0
        for table in tables:
            for t in range(table.shape[1] // LANES):
                z = table[at, t * LANES : (t + 1) * LANES] + src[line : line + 1, :] + wide[at, :]
                weight.append(jnp.exp2(z).astype(jnp.bfloat16))
                line += 1
        pull = 0.0
        for k in range(3):
            pull = pull + dot(jnp.concatenate(weight[2 * k : 2 * k + 2], axis=1), blocks[k][:, :depth])
        last = jnp.concatenate([blocks[3][:, :depth], blocks[4][:, :depth]])
        pull = pull + dot(jnp.concatenate(weight[6:], axis=1), last)
        to = slice((unit % 2) * 256, (unit % 2 + 1) * 256)
        if unit < 2:
            keep[to, :] = pull * share
        else:
            give[to, :] = (pull * share).astype(give.dtype)


def split(axis, offsets, value, own, outs):
    rows, n = own.shape[0], len(outs) + 1
    for k, out in enumerate((own, *outs)):
        at = pl.multiple_of(lax.rem(offsets[axis] + k, n) * rows, rows)
        out[...] = value(pl.ds(at, rows)).astype(out.dtype)


def split_x_kernel(offsets, keep, taken, own, *outs):
    split(4, offsets, lambda at: keep[at, :] + taken[at, :].astype(jnp.float32), own, outs)


def split_y_kernel(offsets, keep, *refs):
    taken, (own, *outs) = refs[:3], refs[3:]

    def value(at):
        return functools.reduce(jnp.add, (t[at, :].astype(jnp.float32) for t in taken), keep[at, :])

    split(5, offsets, value, own, outs)


def finish_kernel(scale, own, up, down, src, pull_out, cost, pull, sem):
    pull[...] = own[...] + up[...].astype(jnp.float32) + down[...].astype(jnp.float32)
    copy = pltpu.make_async_copy(pull, pull_out, sem)
    copy.start()
    costs = jnp.sum(pull[...] * src[...].astype(jnp.float32), axis=1, keepdims=True) * scale
    cost[...] = jnp.broadcast_to(costs, (costs.shape[0], LANES)).T[:1, :]
    copy.wait()


def first_add_kernel(up, up_term, down, down_term, up_out, down_out):
    half = up.shape[0]
    up_out[:half, :] = (up_term[:half, :] + up[...].astype(jnp.float32)).astype(up_out.dtype)
    up_out[half:, :] = up_term[half:, :].astype(up_out.dtype)
    down_out[:half, :] = down_term[:half, :].astype(down_out.dtype)
    down_out[half:, :] = (down_term[half:, :] + down[...].astype(jnp.float32)).astype(down_out.dtype)


def add_kernel(up, up_term, down, down_term, up_out, down_out):
    for out, term, add in ((up_out, up_term, up), (down_out, down_term, down)):
        out[...] = (term[...] + add[...].astype(jnp.float32)).astype(out.dtype)


def shards(src_emb, tgt_emb, src_lang, tgt_lang):
    f32, bf16 = jnp.float32, jnp.bfloat16
    rows, depth = src_emb.shape
    columns = tgt_emb.shape[0]
    row, col = lax.axis_index(ROW), lax.axis_index(COL)
    ring, plane = lax.axis_size(RING), lax.axis_size(PLANE)
    spread_size = lax.axis_size(SPREAD)
    n_src, n_tgt = rows * ring, columns * spread_size
    place, core = lax.axis_index(RING), lax.axis_index("core")
    total_src = src_lang.shape[0] * lax.axis_size(ROW)
    total_tgt = tgt_lang.shape[0] * lax.axis_size(COL)
    offsets = jnp.stack(
        [place, 4 * core, col, row, lax.axis_index("x"), lax.axis_index("y")]
    ).astype(jnp.int32)

    n_label = depth + LANES
    dma = pltpu.SemaphoreType.DMA
    own, tgt = call(
        label_kernel,
        [jax.ShapeDtypeStruct((rows, n_label), bf16), jax.ShapeDtypeStruct((columns, n_label), bf16)],
        [
            pltpu.VMEM((src_lang.shape[0] // LANES, LANES), jnp.int32),
            pltpu.VMEM((tgt_lang.shape[0] // LANES, LANES), jnp.int32),
            pltpu.VMEM((LANES, LANES), f32), dma((4,)),
        ],
        offsets, src_lang.reshape(-1, LANES), tgt_lang.reshape(-1, LANES), src_emb, tgt_emb,
        smem=1, in_hbm=range(1, 5), flops=1, bytes_accessed=2**20,
    )

    def gather_axis(block, axis, at):
        size = lax.axis_size(axis)
        found = [
            lax.ppermute(block, axis, [((i + k) % size, i) for i in range(size)]) for k in range(1, size)
        ]
        return call(
            functools.partial(assemble_kernel, at),
            [jax.ShapeDtypeStruct((size * block.shape[0], block.shape[1]), bf16)], [dma((size,))],
            offsets, block, *found, smem=1, flops=1, bytes_accessed=2**20,
        )[0]

    up, down = shift(own, 1), shift(own, -1)
    pairs = [(down, up)]
    block = gather_axis(tgt, "y", 5)
    block, up, down = lax.optimization_barrier((block, up, down))
    up, down = shift(up, 1), shift(down, -1)
    mine = gather_axis(block, "x", 4)
    pairs.append((down, up))
    up, down = shift(up, 1), shift(down, -1)
    mine, up, down = lax.optimization_barrier((mine, up, down))
    theirs = lax.ppermute(mine, "core", SWAP)

    order = pltpu.VMEM((8, LANES), f32)
    pots = jax.ShapeDtypeStruct((8, LANES), f32)
    to_ring = jax.ShapeDtypeStruct((ring, 8, LANES), f32)
    to_spread = jax.ShapeDtypeStruct((spread_size, 8, LANES), f32)
    pair = [
        jax.ShapeDtypeStruct((2 * rows, n_label), bf16),
        jax.ShapeDtypeStruct((2 * rows, n_tgt), f32),
        jax.ShapeDtypeStruct((n_tgt, 2 * rows), f32),
    ]
    pair_part = jax.ShapeDtypeStruct((2, LANES), f32)
    matmul = 2 * n_src * n_tgt * depth
    scale = LOG2E / (EPSILON * math.sqrt(depth))
    cost = dict(flops=matmul // 2, bytes_accessed=2**22)
    *first, tgt_block = call(
        functools.partial(first_pair_kernel, scale),
        [*pair, pair_part, jax.ShapeDtypeStruct((n_tgt, n_label), bf16)], [dma((4,))],
        *pairs[0], mine, theirs, **cost,
    )

    def pair_logits(near, other, in_hbm):
        return call(
            functools.partial(pair_kernel, scale),
            [*pair, pair_part], [dma((2,))],
            near, other, tgt_block, in_hbm=in_hbm, **cost,
        )

    made = [list(first), list(pair_logits(*pairs[1], ()))]
    made.append(pair_logits(down, up, ()))
    half = rows // 2
    far = [jax.ShapeDtypeStruct((half, n_label), bf16)] * 2
    up, down = call(halves_kernel, far, [dma((2,))], up, down, flops=1, bytes_accessed=1)
    far = shift(up, 1), shift(down, -1)
    single = [
        jax.ShapeDtypeStruct((rows, n_label), bf16),
        jax.ShapeDtypeStruct((rows, n_tgt), f32),
        jax.ShapeDtypeStruct((n_tgt, rows), f32),
    ]
    made.append(
        call(
            functools.partial(own_kernel, scale),
            [*single, jax.ShapeDtypeStruct((1, LANES), f32)], [dma((1,))],
            own, tgt_block, **cost,
        )
    )
    *last, part = call(
        functools.partial(far_kernel, scale),
        [*single, to_ring], [order, dma((2,))],
        offsets, *far, tgt_block, *(m[3] for m in made),
        smem=1, **cost,
    )
    made.append(last)
    src_blocks, logits, logits_t = ([m[k] for m in made] for k in range(3))
    wide_src = pltpu.VMEM((n_src, LANES), f32)
    wide_tgt = pltpu.VMEM((n_tgt, LANES), f32)
    for step in range(ITERS):
        gathered = lax.all_to_all(part, RING, 0, 0)
        part, src_pots = call(
            functools.partial(src_pots_kernel, math.log2(total_tgt)),
            [to_spread, pots], [order, wide_src],
            offsets, *logits, gathered, smem=1, flops=8 * n_src * n_tgt, bytes_accessed=2**22,
        )
        gathered = lax.all_to_all(part, SPREAD, 0, 0)
        if step < ITERS - 1:
            (part,) = call(
                functools.partial(tgt_pots_kernel, math.log2(total_src)),
                [to_ring], [order, wide_tgt],
                offsets, *logits_t, gathered, smem=1, flops=8 * n_src * n_tgt, bytes_accessed=2**22,
            )
    term = jax.ShapeDtypeStruct((rows, depth), f32)

    def src_terms(log_count, units, pieces, tgt_pots, kinds):
        return call(
            functools.partial(src_kernel, log_count, 1.0 / total_tgt, pieces),
            kinds, [order, wide_src],
            offsets, *(logits[u] for u in units), tgt_pots, src_pots, tgt_block,
            smem=1, flops=matmul // 4, bytes_accessed=2**22,
        )

    low = jax.ShapeDtypeStruct((rows, depth), bf16)
    far = [jax.ShapeDtypeStruct((half, depth), bf16)] * 2
    up, down, tgt_pots = src_terms(math.log2(total_src), (4,), [(0, rows, 7 * rows)], gathered, [*far, pots])
    up, down = shift(up, 1), shift(down, -1)
    pieces = [(0, 2 * rows, 0), (0, 2 * rows, 2 * rows), (0, 2 * rows, 4 * rows), (0, rows, 6 * rows)]
    *terms, own_term = src_terms(None, (0, 1, 2, 3), pieces, tgt_pots, [term] * 7)
    keep, give = call(
        functools.partial(tgt_kernel, 1.0 / total_src),
        [jax.ShapeDtypeStruct((n_tgt // 2, depth), f32), jax.ShapeDtypeStruct((n_tgt // 2, depth), bf16)],
        [wide_tgt],
        *logits_t, tgt_pots, src_pots, *src_blocks,
        flops=matmul, bytes_accessed=2**23,
    )
    taken = lax.ppermute(give, "core", SWAP)
    keep, taken, up, down, own_term, *terms = lax.optimization_barrier((keep, taken, up, down, own_term, *terms))

    def exchange(kernel, axis, values):
        size = lax.axis_size(axis)
        left = values[0].shape[0] // size
        own, *parts = call(
            kernel,
            [jax.ShapeDtypeStruct((left, depth), f32)] + [jax.ShapeDtypeStruct((left, depth), bf16)] * (size - 1), [],
            offsets, *values, smem=1, flops=1, bytes_accessed=2**20,
        )
        return own, *(
            lax.ppermute(v, axis, [(i, (i + k) % size) for i in range(size)])
            for k, v in enumerate(parts, 1)
        )

    tgt_sums = exchange(split_x_kernel, "x", (keep, taken))
    for k in (2, 1, 0):
        if k == 0:
            tgt_sums, up, down = lax.optimization_barrier((tgt_sums, up, down))
            tgt_sums = exchange(split_y_kernel, "y", tgt_sums)
        up, down = call(
            first_add_kernel if k == 2 else add_kernel, [low] * 2, [],
            up, terms[2 * k], down, terms[2 * k + 1], flops=1, bytes_accessed=2**20,
        )
        up, down = shift(up, 1), shift(down, -1)
    src_pull, row_cost = call(
        functools.partial(finish_kernel, -1.0 / math.sqrt(depth)),
        [term, jax.ShapeDtypeStruct((1, rows), f32)],
        [pltpu.VMEM((rows, depth), f32), dma],
        own_term, up, down, src_emb, outs_in_hbm=(0,), flops=1, bytes_accessed=2**20,
    )
    row_cost = row_cost.reshape(rows)
    src_pull, row_cost, tgt_sums = lax.optimization_barrier((src_pull, row_cost, tgt_sums))
    tgt_pull = functools.reduce(jnp.add, (v.astype(f32) for v in tgt_sums))
    return (src_pull, tgt_pull, row_cost)


def solution(mesh):
    split = Mesh(mesh.devices.reshape(SIZES), AXES)
    return jax.shard_map(
        shards,
        mesh=split,
        in_specs=(P(ROW + COL, None), P(COL + ROW, None), P(ROW), P(COL)),
        out_specs=(P(ROW + COL, None), P(COL + ROW, None), P(ROW + COL)),
        check_vma=False,
    )
```

```python
import functools
import math

import jax
import jax.numpy as jnp
from jax import lax
from jax.experimental import pallas as pl
from jax.experimental.pallas import tpu as pltpu
from jax.sharding import Mesh, PartitionSpec as P

ITERS = 3
NEG = -1e30
EPSILON = 0.5
LOG2E = math.log2(math.e)
LANES = 128
DISTANCES = (1, 7, 2, 6, 3, 5, 0, 4)

AXES = ("x", "zh", "core", "zl", "y")
SIZES = (4, 4, 2, 2, 4)
ROW = ("x", "zh", "core")
COL = ("zl", "y")
RING = ("zh", "zl")
PLANE = ("x", "y")
SPREAD = ("x", "y", "core")
SWAP = [(0, 1), (1, 0)]

VMEM = pl.BlockSpec(memory_space=pltpu.VMEM)
SMEM = pl.BlockSpec(memory_space=pltpu.SMEM)
IN_HBM = pl.BlockSpec(memory_space=pl.ANY)
CONTRACT_LAST = (((1,), (1,)), ((), ()))


def dot(a, b, dims=(((1,), (0,)), ((), ()))):
    return lax.dot_general(a, b, dims, preferred_element_type=jnp.float32)


def call(kernel, outs, scratch, *operands, smem=0, in_hbm=(), outs_in_hbm=(), flops=0, bytes_accessed=0):
    specs = [
        SMEM if k < smem else IN_HBM if k in in_hbm else VMEM for k in range(len(operands))
    ]
    operands = [
        pltpu.with_memory_space_constraint(v, pltpu.HBM) if k in in_hbm else v
        for k, v in enumerate(operands)
    ]
    outs = [
        pltpu.HBM(out.shape, out.dtype) if k in outs_in_hbm else out for k, out in enumerate(outs)
    ]
    return pl.pallas_call(
        kernel,
        out_shape=outs,
        in_specs=specs,
        out_specs=[IN_HBM if k in outs_in_hbm else VMEM for k in range(len(outs))],
        scratch_shapes=scratch,
        compiler_params=pltpu.CompilerParams(vmem_limit_bytes=16 * 2**20),
        cost_estimate=pl.CostEstimate(
            flops=flops, bytes_accessed=bytes_accessed, transcendentals=0
        ),
    )(*operands)


def shift(value, step):
    size = lax.axis_size(RING)
    return lax.ppermute(value, RING, [(i, (i + step) % size) for i in range(size)])


def copy_all(pairs, sems):
    copies = [pltpu.make_async_copy(a, b, sems.at[k]) for k, (a, b) in enumerate(pairs)]
    for copy in copies:
        copy.start()
    for copy in copies:
        copy.wait()


def one_hot(line, dtype):
    labels = jnp.broadcast_to(line.astype(jnp.float32), (LANES, LANES)).T
    lanes = lax.broadcasted_iota(jnp.int32, (LANES, LANES), 1).astype(jnp.float32)
    return (labels == lanes).astype(dtype)


def label_kernel(offsets, src_lang, tgt_lang, src, tgt, src_out, tgt_out, src_labels, tgt_labels, hot, sems):
    columns, depth = tgt.shape
    copies = [
        pltpu.make_async_copy(a, b, sems.at[k])
        for k, (a, b) in enumerate(
            [
                (tgt_lang, tgt_labels),
                (src_lang, src_labels),
                (tgt, tgt_out.at[:, :depth]),
                (src, src_out.at[:, :depth]),
            ]
        )
    ]
    for copy in copies:
        copy.start()
    copies[0].wait()
    here = offsets[3] * columns
    hot[...] = one_hot(tgt_labels[pl.ds(here // LANES, 1), :], jnp.float32)
    tgt_out[:, depth:] = hot[pl.ds(pl.multiple_of(lax.rem(here, LANES), columns), columns), :].astype(tgt_out.dtype)
    copies[1].wait()
    src_out[:, depth:] = one_hot(src_labels[pl.ds(offsets[2], 1), :], src_out.dtype)
    copies[2].wait()
    copies[3].wait()


def assemble_kernel(axis, offsets, *refs):
    (*blocks, out, sems), n = refs, len(refs) - 2
    rows = blocks[0].shape[0]
    places = [lax.rem(offsets[axis] + k, n) * rows for k in range(n)]
    copy_all(
        [(block, out.at[pl.ds(pl.multiple_of(at, rows), rows)]) for block, at in zip(blocks, places)],
        sems,
    )


def columns_sums(tables, added):
    tiles = tables[0].shape[1] // LANES

    def fold(start, join):
        results, row = start, 0
        for table in tables:
            for c in range(table.shape[0] // LANES):
                add = None if added is None else added[row : row + LANES, :]
                for t in range(tiles):
                    z = table[c * LANES : (c + 1) * LANES, t * LANES : (t + 1) * LANES]
                    z = (z if add is None else z + add).reshape(LANES // 8, 8, LANES)
                    results[t] = join(t, results[t], z)
                row += LANES
        return results

    def larger(t, top, z):
        z = jnp.max(z, axis=0)
        return z if top is None else jnp.maximum(top, z)

    tops = [jnp.max(top, axis=0, keepdims=True) for top in fold([None] * tiles, larger)]

    def total(t, so_far, z):
        z = jnp.sum(jnp.exp2(z - tops[t][None]), axis=0)
        return z if so_far is None else so_far + z

    totals = [jnp.sum(v, axis=0, keepdims=True) for v in fold([None] * tiles, total)]
    return tops, totals


def columns_lse(tables, added):
    return [top + jnp.log2(total) for top, total in zip(*columns_sums(tables, added))]


def send_out(parts, offset, table, order, out):
    for part, at in zip(parts, table):
        order[pl.ds(lax.rem(at + offset, 8), 1), :] = part
    out[...] = jnp.broadcast_to(order[...][None], out.shape)


def merge(gathered, log_count, offset, table, order):
    parts = gathered[...]
    top = jnp.max(parts, axis=0)
    total = jnp.sum(jnp.exp2(parts - top[None]), axis=0)
    order[...] = log_count - (top + jnp.log2(total))
    return jnp.concatenate([order[pl.ds(lax.rem(at + offset, 8), 1), :] for at in table])


def spread(pots, wide):
    columns = pots.T
    for c in range(8):
        wide[c * LANES : (c + 1) * LANES, :] = jnp.broadcast_to(
            columns[:, c : c + 1], (LANES, LANES)
        )


def make_logits(scale, src, tgt, logits, logits_t):
    depth = src.shape[1] - LANES
    emb, hot = src[:, :depth], src[:, depth:]
    step = 256
    for start in range(0, tgt.shape[0], step):
        to = slice(start, start + step)
        same = dot(tgt[to, depth:], hot, CONTRACT_LAST) > 0.5
        value = jnp.where(same, dot(tgt[to, :depth], emb, CONTRACT_LAST) * scale, NEG)
        logits_t[to, :] = value
        logits[:, to] = value.T


def first_pair_kernel(scale, near, other, mine, theirs, src, logits, logits_t, part, tgt, sems):
    half = mine.shape[0]
    copy_all(
        [
            (mine, tgt.at[:half]),
            (theirs, tgt.at[half:]),
            (near, src.at[: near.shape[0]]),
            (other, src.at[near.shape[0] :]),
        ],
        sems,
    )
    make_logits(scale, src, tgt, logits, logits_t)
    part[...] = jnp.concatenate(columns_lse([logits_t], None))


def halves_kernel(up, down, up_out, down_out, sems):
    half = up_out.shape[0]
    copy_all([(up.at[:half], up_out), (down.at[half:], down_out)], sems)


def pair_kernel(scale, near, other, tgt, src, logits, logits_t, part, sems):
    copy_all([(near, src.at[: near.shape[0]]), (other, src.at[near.shape[0] :])], sems)
    make_logits(scale, src, tgt, logits, logits_t)
    part[...] = jnp.concatenate(columns_lse([logits_t], None))


def own_kernel(scale, own, tgt, src, logits, logits_t, part, sems):
    copy_all([(own, src)], sems)
    make_logits(scale, src, tgt, logits, logits_t)
    part[...] = jnp.concatenate(columns_lse([logits_t], None))


def far_kernel(scale, offsets, far_up, far_down, tgt, *refs):
    parts, (src, logits, logits_t, out, order, sems) = refs[:4], refs[4:]
    half = far_up.shape[0]
    copy_all([(far_up, src.at[:half]), (far_down, src.at[half:])], sems)
    make_logits(scale, src, tgt, logits, logits_t)
    parts = [part[r : r + 1, :] for part in parts for r in range(part.shape[0])]
    send_out(parts + columns_lse([logits_t], None), offsets[0], DISTANCES, order, out)


def src_pots_kernel(log_count, offsets, *refs):
    tables, (gathered, out, pots, order, wide) = refs[:5], refs[5:]
    local = merge(gathered, log_count, offsets[0], DISTANCES, order)
    pots[...] = local
    spread(local, wide)
    send_out(columns_lse(tables, wide), offsets[1], range(8), order, out)


def tgt_pots_kernel(log_count, offsets, *refs):
    tables, (gathered, out, order, wide) = refs[:5], refs[5:]
    spread(merge(gathered, log_count, offsets[1], range(8), order), wide)
    parts = [part for table in tables for part in columns_lse([table], wide)]
    send_out(parts, offsets[0], DISTANCES, order, out)


def src_kernel(log_count, share, pieces, offsets, *refs):
    n = len(pieces)
    tables, (tgt_pots, src_pots, block), outs = refs[:n], refs[n : n + 3], refs[n + 3 : -2]
    order, wide = refs[-2:]
    depth, half = outs[0].shape[1], block.shape[0] // 2
    if log_count is None:
        tgt = tgt_pots[...]
    else:
        tgt = merge(tgt_pots, log_count, offsets[1], range(8), order)
        outs[-1][...] = tgt
        outs = outs[:-1]
    spread(src_pots[...], wide)
    outs = list(outs)
    for (first, rows, place), table in zip(pieces, tables):
        at = slice(place, place + rows)
        weight = [
            jnp.exp2(table[first : first + rows, t * LANES : (t + 1) * LANES] + wide[at, :] + tgt[t : t + 1, :])
            .astype(jnp.bfloat16)
            for t in range(8)
        ]
        left = jnp.concatenate(weight[:4], axis=1)
        right = jnp.concatenate(weight[4:], axis=1)
        pull = (dot(left, block[:half, :depth]) + dot(right, block[half:, :depth])) * share
        start = 0
        while start < rows:
            out = outs.pop(0)
            out[...] = pull[start : start + out.shape[0]].astype(out.dtype)
            start += out.shape[0]


def tgt_kernel(share, *refs):
    tables, (tgt_pots, src_pots), blocks = refs[:5], refs[5:7], refs[7:12]
    keep, give, wide = refs[12:]
    spread(tgt_pots[...], wide)
    src = src_pots[...]
    depth = keep.shape[1]
    for unit in (2, 3, 0, 1):
        at = slice(unit * 256, (unit + 1) * 256)
        weight, line = [], 0
        for table in tables:
            for t in range(table.shape[1] // LANES):
                z = table[at, t * LANES : (t + 1) * LANES] + src[line : line + 1, :] + wide[at, :]
                weight.append(jnp.exp2(z).astype(jnp.bfloat16))
                line += 1
        pull = 0.0
        for k in range(3):
            pull = pull + dot(jnp.concatenate(weight[2 * k : 2 * k + 2], axis=1), blocks[k][:, :depth])
        last = jnp.concatenate([blocks[3][:, :depth], blocks[4][:, :depth]])
        pull = pull + dot(jnp.concatenate(weight[6:], axis=1), last)
        to = slice((unit % 2) * 256, (unit % 2 + 1) * 256)
        if unit < 2:
            keep[to, :] = pull * share
        else:
            give[to, :] = (pull * share).astype(give.dtype)


def split(axis, offsets, value, own, outs):
    rows, n = own.shape[0], len(outs) + 1
    for k, out in enumerate((own, *outs)):
        at = pl.multiple_of(lax.rem(offsets[axis] + k, n) * rows, rows)
        out[...] = value(pl.ds(at, rows)).astype(out.dtype)


def split_x_kernel(offsets, keep, taken, own, *outs):
    split(4, offsets, lambda at: keep[at, :] + taken[at, :].astype(jnp.float32), own, outs)


def split_y_kernel(offsets, keep, *refs):
    taken, (own, *outs) = refs[:3], refs[3:]

    def value(at):
        return functools.reduce(jnp.add, (t[at, :].astype(jnp.float32) for t in taken), keep[at, :])

    split(5, offsets, value, own, outs)


def first_add_kernel(up, up_term, down, down_term, up_out, down_out):
    half = up.shape[0]
    up_out[:half, :] = (up_term[:half, :] + up[...].astype(jnp.float32)).astype(up_out.dtype)
    up_out[half:, :] = up_term[half:, :].astype(up_out.dtype)
    down_out[:half, :] = down_term[:half, :].astype(down_out.dtype)
    down_out[half:, :] = (down_term[half:, :] + down[...].astype(jnp.float32)).astype(down_out.dtype)


def add_kernel(up, up_term, down, down_term, up_out, down_out):
    for out, term, add in ((up_out, up_term, up), (down_out, down_term, down)):
        out[...] = (term[...] + add[...].astype(jnp.float32)).astype(out.dtype)


def shards(src_emb, tgt_emb, src_lang, tgt_lang):
    f32, bf16 = jnp.float32, jnp.bfloat16
    rows, depth = src_emb.shape
    columns = tgt_emb.shape[0]
    row, col = lax.axis_index(ROW), lax.axis_index(COL)
    ring, plane = lax.axis_size(RING), lax.axis_size(PLANE)
    spread_size = lax.axis_size(SPREAD)
    n_src, n_tgt = rows * ring, columns * spread_size
    place, core = lax.axis_index(RING), lax.axis_index("core")
    total_src = src_lang.shape[0] * lax.axis_size(ROW)
    total_tgt = tgt_lang.shape[0] * lax.axis_size(COL)
    offsets = jnp.stack(
        [place, 4 * core, col, row, lax.axis_index("x"), lax.axis_index("y")]
    ).astype(jnp.int32)

    n_label = depth + LANES
    dma = pltpu.SemaphoreType.DMA
    own, tgt = call(
        label_kernel,
        [jax.ShapeDtypeStruct((rows, n_label), bf16), jax.ShapeDtypeStruct((columns, n_label), bf16)],
        [
            pltpu.VMEM((src_lang.shape[0] // LANES, LANES), jnp.int32),
            pltpu.VMEM((tgt_lang.shape[0] // LANES, LANES), jnp.int32),
            pltpu.VMEM((LANES, LANES), f32), dma((4,)),
        ],
        offsets, src_lang.reshape(-1, LANES), tgt_lang.reshape(-1, LANES), src_emb, tgt_emb,
        smem=1, in_hbm=range(1, 5), flops=1, bytes_accessed=2**20,
    )

    def gather_axis(block, axis, at):
        size = lax.axis_size(axis)
        found = [
            lax.ppermute(block, axis, [((i + k) % size, i) for i in range(size)]) for k in range(1, size)
        ]
        return call(
            functools.partial(assemble_kernel, at),
            [jax.ShapeDtypeStruct((size * block.shape[0], block.shape[1]), bf16)], [dma((size,))],
            offsets, block, *found, smem=1, flops=1, bytes_accessed=2**20,
        )[0]

    up, down = shift(own, 1), shift(own, -1)
    pairs = [(down, up)]
    block = gather_axis(tgt, "y", 5)
    block, up, down = lax.optimization_barrier((block, up, down))
    up, down = shift(up, 1), shift(down, -1)
    mine = gather_axis(block, "x", 4)
    pairs.append((down, up))
    up, down = shift(up, 1), shift(down, -1)
    mine, up, down = lax.optimization_barrier((mine, up, down))
    theirs = lax.ppermute(mine, "core", SWAP)

    order = pltpu.VMEM((8, LANES), f32)
    pots = jax.ShapeDtypeStruct((8, LANES), f32)
    to_ring = jax.ShapeDtypeStruct((ring, 8, LANES), f32)
    to_spread = jax.ShapeDtypeStruct((spread_size, 8, LANES), f32)
    pair = [
        jax.ShapeDtypeStruct((2 * rows, n_label), bf16),
        jax.ShapeDtypeStruct((2 * rows, n_tgt), f32),
        jax.ShapeDtypeStruct((n_tgt, 2 * rows), f32),
    ]
    pair_part = jax.ShapeDtypeStruct((2, LANES), f32)
    matmul = 2 * n_src * n_tgt * depth
    scale = LOG2E / (EPSILON * math.sqrt(depth))
    cost = dict(flops=matmul // 2, bytes_accessed=2**22)
    *first, tgt_block = call(
        functools.partial(first_pair_kernel, scale),
        [*pair, pair_part, jax.ShapeDtypeStruct((n_tgt, n_label), bf16)], [dma((4,))],
        *pairs[0], mine, theirs, **cost,
    )

    def pair_logits(near, other, in_hbm):
        return call(
            functools.partial(pair_kernel, scale),
            [*pair, pair_part], [dma((2,))],
            near, other, tgt_block, in_hbm=in_hbm, **cost,
        )

    made = [list(first), list(pair_logits(*pairs[1], ()))]
    made.append(pair_logits(down, up, ()))
    half = rows // 2
    far = [jax.ShapeDtypeStruct((half, n_label), bf16)] * 2
    up, down = call(halves_kernel, far, [dma((2,))], up, down, flops=1, bytes_accessed=1)
    far = shift(up, 1), shift(down, -1)
    single = [
        jax.ShapeDtypeStruct((rows, n_label), bf16),
        jax.ShapeDtypeStruct((rows, n_tgt), f32),
        jax.ShapeDtypeStruct((n_tgt, rows), f32),
    ]
    made.append(
        call(
            functools.partial(own_kernel, scale),
            [*single, jax.ShapeDtypeStruct((1, LANES), f32)], [dma((1,))],
            own, tgt_block, **cost,
        )
    )
    *last, part = call(
        functools.partial(far_kernel, scale),
        [*single, to_ring], [order, dma((2,))],
        offsets, *far, tgt_block, *(m[3] for m in made),
        smem=1, **cost,
    )
    made.append(last)
    src_blocks, logits, logits_t = ([m[k] for m in made] for k in range(3))
    wide_src = pltpu.VMEM((n_src, LANES), f32)
    wide_tgt = pltpu.VMEM((n_tgt, LANES), f32)
    for step in range(ITERS):
        gathered = lax.all_to_all(part, RING, 0, 0)
        part, src_pots = call(
            functools.partial(src_pots_kernel, math.log2(total_tgt)),
            [to_spread, pots], [order, wide_src],
            offsets, *logits, gathered, smem=1, flops=8 * n_src * n_tgt, bytes_accessed=2**22,
        )
        gathered = lax.all_to_all(part, SPREAD, 0, 0)
        if step < ITERS - 1:
            (part,) = call(
                functools.partial(tgt_pots_kernel, math.log2(total_src)),
                [to_ring], [order, wide_tgt],
                offsets, *logits_t, gathered, smem=1, flops=8 * n_src * n_tgt, bytes_accessed=2**22,
            )
    term = jax.ShapeDtypeStruct((rows, depth), f32)

    def src_terms(log_count, units, pieces, tgt_pots, kinds):
        return call(
            functools.partial(src_kernel, log_count, 1.0 / total_tgt, pieces),
            kinds, [order, wide_src],
            offsets, *(logits[u] for u in units), tgt_pots, src_pots, tgt_block,
            smem=1, flops=matmul // 4, bytes_accessed=2**22,
        )

    low = jax.ShapeDtypeStruct((rows, depth), bf16)
    far = [jax.ShapeDtypeStruct((half, depth), bf16)] * 2
    up, down, tgt_pots = src_terms(math.log2(total_src), (4,), [(0, rows, 7 * rows)], gathered, [*far, pots])
    up, down = shift(up, 1), shift(down, -1)
    pieces = [(0, 2 * rows, 0), (0, 2 * rows, 2 * rows), (0, 2 * rows, 4 * rows), (0, rows, 6 * rows)]
    *terms, own_term = src_terms(None, (0, 1, 2, 3), pieces, tgt_pots, [term] * 7)
    keep, give = call(
        functools.partial(tgt_kernel, 1.0 / total_src),
        [jax.ShapeDtypeStruct((n_tgt // 2, depth), f32), jax.ShapeDtypeStruct((n_tgt // 2, depth), bf16)],
        [wide_tgt],
        *logits_t, tgt_pots, src_pots, *src_blocks,
        flops=matmul, bytes_accessed=2**23,
    )
    taken = lax.ppermute(give, "core", SWAP)
    keep, taken, up, down, own_term, *terms = lax.optimization_barrier((keep, taken, up, down, own_term, *terms))

    def exchange(kernel, axis, values):
        size = lax.axis_size(axis)
        left = values[0].shape[0] // size
        own, *parts = call(
            kernel,
            [jax.ShapeDtypeStruct((left, depth), f32)] + [jax.ShapeDtypeStruct((left, depth), bf16)] * (size - 1), [],
            offsets, *values, smem=1, flops=1, bytes_accessed=2**20,
        )
        return own, *(
            lax.ppermute(v, axis, [(i, (i + k) % size) for i in range(size)])
            for k, v in enumerate(parts, 1)
        )

    tgt_sums = exchange(split_x_kernel, "x", (keep, taken))
    for k in (2, 1, 0):
        if k == 0:
            tgt_sums, up, down = lax.optimization_barrier((tgt_sums, up, down))
            tgt_sums = exchange(split_y_kernel, "y", tgt_sums)
        up, down = call(
            first_add_kernel if k == 2 else add_kernel, [low] * 2, [],
            up, terms[2 * k], down, terms[2 * k + 1], flops=1, bytes_accessed=2**20,
        )
        up, down = shift(up, 1), shift(down, -1)
    src_pull = own_term + up.astype(f32) + down.astype(f32)
    row_cost = jnp.sum(src_pull * src_emb.astype(f32), axis=1) * (-1.0 / math.sqrt(depth))
    src_pull, row_cost, tgt_sums = lax.optimization_barrier((src_pull, row_cost, tgt_sums))
    tgt_pull = functools.reduce(jnp.add, (v.astype(f32) for v in tgt_sums))
    return (src_pull, tgt_pull, row_cost)


def solution(mesh):
    split = Mesh(mesh.devices.reshape(SIZES), AXES)
    return jax.shard_map(
        shards,
        mesh=split,
        in_specs=(P(ROW + COL, None), P(COL + ROW, None), P(ROW), P(COL)),
        out_specs=(P(ROW + COL, None), P(COL + ROW, None), P(ROW + COL)),
        check_vma=False,
    )
```

```python
import functools
import math

import jax
import jax.numpy as jnp
from jax import lax
from jax.experimental import pallas as pl
from jax.experimental.pallas import tpu as pltpu
from jax.sharding import Mesh, PartitionSpec as P

ITERS = 3
NEG = -1e30
EPSILON = 0.5
LOG2E = math.log2(math.e)
LANES = 128
DISTANCES = (1, 7, 2, 6, 3, 5, 0, 4)

AXES = ("x", "zh", "core", "zl", "y")
SIZES = (4, 4, 2, 2, 4)
ROW = ("x", "zh", "core")
COL = ("zl", "y")
RING = ("zh", "zl")
PLANE = ("x", "y")
SPREAD = ("x", "y", "core")
SWAP = [(0, 1), (1, 0)]

VMEM = pl.BlockSpec(memory_space=pltpu.VMEM)
SMEM = pl.BlockSpec(memory_space=pltpu.SMEM)
IN_HBM = pl.BlockSpec(memory_space=pl.ANY)
CONTRACT_LAST = (((1,), (1,)), ((), ()))


def dot(a, b, dims=(((1,), (0,)), ((), ()))):
    return lax.dot_general(a, b, dims, preferred_element_type=jnp.float32)


def call(kernel, outs, scratch, *operands, smem=0, in_hbm=(), outs_in_hbm=(), flops=0, bytes_accessed=0):
    specs = [
        SMEM if k < smem else IN_HBM if k in in_hbm else VMEM for k in range(len(operands))
    ]
    operands = [
        pltpu.with_memory_space_constraint(v, pltpu.HBM) if k in in_hbm else v
        for k, v in enumerate(operands)
    ]
    outs = [
        pltpu.HBM(out.shape, out.dtype) if k in outs_in_hbm else out for k, out in enumerate(outs)
    ]
    return pl.pallas_call(
        kernel,
        out_shape=outs,
        in_specs=specs,
        out_specs=[IN_HBM if k in outs_in_hbm else VMEM for k in range(len(outs))],
        scratch_shapes=scratch,
        compiler_params=pltpu.CompilerParams(vmem_limit_bytes=16 * 2**20),
        cost_estimate=pl.CostEstimate(
            flops=flops, bytes_accessed=bytes_accessed, transcendentals=0
        ),
    )(*operands)


def shift(value, step):
    size = lax.axis_size(RING)
    return lax.ppermute(value, RING, [(i, (i + step) % size) for i in range(size)])


def copy_all(pairs, sems):
    copies = [pltpu.make_async_copy(a, b, sems.at[k]) for k, (a, b) in enumerate(pairs)]
    for copy in copies:
        copy.start()
    for copy in copies:
        copy.wait()


def one_hot(line, dtype):
    labels = jnp.broadcast_to(line.astype(jnp.float32), (LANES, LANES)).T
    lanes = lax.broadcasted_iota(jnp.int32, (LANES, LANES), 1).astype(jnp.float32)
    return (labels == lanes).astype(dtype)


def label_kernel(offsets, src_lang, tgt_lang, src, tgt, src_out, tgt_out, src_labels, tgt_labels, hot, sems):
    columns, depth = tgt.shape
    copies = [
        pltpu.make_async_copy(a, b, sems.at[k])
        for k, (a, b) in enumerate(
            [
                (tgt_lang, tgt_labels),
                (src_lang, src_labels),
                (tgt, tgt_out.at[:, :depth]),
                (src, src_out.at[:, :depth]),
            ]
        )
    ]
    for copy in copies:
        copy.start()
    copies[0].wait()
    here = offsets[3] * columns
    hot[...] = one_hot(tgt_labels[pl.ds(here // LANES, 1), :], jnp.float32)
    tgt_out[:, depth:] = hot[pl.ds(pl.multiple_of(lax.rem(here, LANES), columns), columns), :].astype(tgt_out.dtype)
    copies[1].wait()
    src_out[:, depth:] = one_hot(src_labels[pl.ds(offsets[2], 1), :], src_out.dtype)
    copies[2].wait()
    copies[3].wait()


def assemble_kernel(axis, offsets, *refs):
    (*blocks, out, sems), n = refs, len(refs) - 2
    rows = blocks[0].shape[0]
    places = [lax.rem(offsets[axis] + k, n) * rows for k in range(n)]
    copy_all(
        [(block, out.at[pl.ds(pl.multiple_of(at, rows), rows)]) for block, at in zip(blocks, places)],
        sems,
    )


def columns_sums(tables, added):
    tiles = tables[0].shape[1] // LANES

    def fold(start, join):
        results, row = start, 0
        for table in tables:
            for c in range(table.shape[0] // LANES):
                add = None if added is None else added[row : row + LANES, :]
                for t in range(tiles):
                    z = table[c * LANES : (c + 1) * LANES, t * LANES : (t + 1) * LANES]
                    z = (z if add is None else z + add).reshape(LANES // 8, 8, LANES)
                    results[t] = join(t, results[t], z)
                row += LANES
        return results

    def larger(t, top, z):
        z = jnp.max(z, axis=0)
        return z if top is None else jnp.maximum(top, z)

    tops = [jnp.max(top, axis=0, keepdims=True) for top in fold([None] * tiles, larger)]

    def total(t, so_far, z):
        z = jnp.sum(jnp.exp2(z - tops[t][None]), axis=0)
        return z if so_far is None else so_far + z

    totals = [jnp.sum(v, axis=0, keepdims=True) for v in fold([None] * tiles, total)]
    return tops, totals


def columns_lse(tables, added):
    return [top + jnp.log2(total) for top, total in zip(*columns_sums(tables, added))]


def send_out(parts, offset, table, order, out):
    for part, at in zip(parts, table):
        order[pl.ds(lax.rem(at + offset, 8), 1), :] = part
    out[...] = jnp.broadcast_to(order[...][None], out.shape)


def merge(gathered, log_count, offset, table, order):
    parts = gathered[...]
    top = jnp.max(parts, axis=0)
    total = jnp.sum(jnp.exp2(parts - top[None]), axis=0)
    order[...] = log_count - (top + jnp.log2(total))
    return jnp.concatenate([order[pl.ds(lax.rem(at + offset, 8), 1), :] for at in table])


def spread(pots, wide):
    columns = pots.T
    for c in range(8):
        wide[c * LANES : (c + 1) * LANES, :] = jnp.broadcast_to(
            columns[:, c : c + 1], (LANES, LANES)
        )


def make_logits(scale, src, tgt, logits, logits_t):
    depth = src.shape[1] - LANES
    emb, hot = src[:, :depth], src[:, depth:]
    step = 256
    for start in range(0, tgt.shape[0], step):
        to = slice(start, start + step)
        same = dot(tgt[to, depth:], hot, CONTRACT_LAST) > 0.5
        value = jnp.where(same, dot(tgt[to, :depth], emb, CONTRACT_LAST) * scale, NEG)
        logits_t[to, :] = value
        logits[:, to] = value.T


def first_pair_kernel(scale, near, other, mine, theirs, src, logits, logits_t, part, tgt, sems):
    half = mine.shape[0]
    copy_all(
        [
            (mine, tgt.at[:half]),
            (theirs, tgt.at[half:]),
            (near, src.at[: near.shape[0]]),
            (other, src.at[near.shape[0] :]),
        ],
        sems,
    )
    make_logits(scale, src, tgt, logits, logits_t)
    part[...] = jnp.concatenate(columns_lse([logits_t], None))


def halves_kernel(up, down, up_out, down_out, sems):
    half = up_out.shape[0]
    copy_all([(up.at[:half], up_out), (down.at[half:], down_out)], sems)


def pair_kernel(scale, near, other, tgt, src, logits, logits_t, part, sems):
    copy_all([(near, src.at[: near.shape[0]]), (other, src.at[near.shape[0] :])], sems)
    make_logits(scale, src, tgt, logits, logits_t)
    part[...] = jnp.concatenate(columns_lse([logits_t], None))


def own_kernel(scale, own, tgt, src, logits, logits_t, part, sems):
    copy_all([(own, src)], sems)
    make_logits(scale, src, tgt, logits, logits_t)
    part[...] = jnp.concatenate(columns_lse([logits_t], None))


def far_kernel(scale, offsets, far_up, far_down, tgt, *refs):
    parts, (src, logits, logits_t, out, order, sems) = refs[:4], refs[4:]
    half = far_up.shape[0]
    copy_all([(far_up, src.at[:half]), (far_down, src.at[half:])], sems)
    make_logits(scale, src, tgt, logits, logits_t)
    parts = [part[r : r + 1, :] for part in parts for r in range(part.shape[0])]
    send_out(parts + columns_lse([logits_t], None), offsets[0], DISTANCES, order, out)


def src_pots_kernel(log_count, offsets, *refs):
    tables, (gathered, out, pots, order, wide) = refs[:5], refs[5:]
    local = merge(gathered, log_count, offsets[0], DISTANCES, order)
    pots[...] = local
    spread(local, wide)
    send_out(columns_lse(tables, wide), offsets[1], range(8), order, out)


def tgt_pots_kernel(log_count, offsets, *refs):
    tables, (gathered, out, order, wide) = refs[:5], refs[5:]
    spread(merge(gathered, log_count, offsets[1], range(8), order), wide)
    parts = [part for table in tables for part in columns_lse([table], wide)]
    send_out(parts, offsets[0], DISTANCES, order, out)


def src_kernel(log_count, share, pieces, offsets, *refs):
    n = len(pieces)
    tables, (tgt_pots, src_pots, block), outs = refs[:n], refs[n : n + 3], refs[n + 3 : -2]
    order, wide = refs[-2:]
    depth, half = outs[0].shape[1], block.shape[0] // 2
    if log_count is None:
        tgt = tgt_pots[...]
    else:
        tgt = merge(tgt_pots, log_count, offsets[1], range(8), order)
        outs[-1][...] = tgt
        outs = outs[:-1]
    spread(src_pots[...], wide)
    outs = list(outs)
    for (first, rows, place), table in zip(pieces, tables):
        at = slice(place, place + rows)
        weight = [
            jnp.exp2(table[first : first + rows, t * LANES : (t + 1) * LANES] + wide[at, :] + tgt[t : t + 1, :])
            .astype(jnp.bfloat16)
            for t in range(8)
        ]
        left = jnp.concatenate(weight[:4], axis=1)
        right = jnp.concatenate(weight[4:], axis=1)
        pull = (dot(left, block[:half, :depth]) + dot(right, block[half:, :depth])) * share
        start = 0
        while start < rows:
            out = outs.pop(0)
            out[...] = pull[start : start + out.shape[0]].astype(out.dtype)
            start += out.shape[0]


def tgt_kernel(share, *refs):
    tables, (tgt_pots, src_pots), blocks = refs[:5], refs[5:7], refs[7:12]
    keep, give, wide = refs[12:]
    spread(tgt_pots[...], wide)
    src = src_pots[...]
    depth = keep.shape[1]
    for unit in (2, 3, 0, 1):
        at = slice(unit * 256, (unit + 1) * 256)
        weight, line = [], 0
        for table in tables:
            for t in range(table.shape[1] // LANES):
                z = table[at, t * LANES : (t + 1) * LANES] + src[line : line + 1, :] + wide[at, :]
                weight.append(jnp.exp2(z).astype(jnp.bfloat16))
                line += 1
        pull = 0.0
        for k in range(3):
            pull = pull + dot(jnp.concatenate(weight[2 * k : 2 * k + 2], axis=1), blocks[k][:, :depth])
        last = jnp.concatenate([blocks[3][:, :depth], blocks[4][:, :depth]])
        pull = pull + dot(jnp.concatenate(weight[6:], axis=1), last)
        to = slice((unit % 2) * 256, (unit % 2 + 1) * 256)
        if unit < 2:
            keep[to, :] = pull * share
        else:
            give[to, :] = (pull * share).astype(give.dtype)


def add_cores_kernel(keep, taken, out, total, sems):
    rows = keep.shape[0] // sems.shape[0]
    copies = []
    for c in range(sems.shape[0]):
        at = slice(c * rows, (c + 1) * rows)
        total[at, :] = (keep[at, :] + taken[at, :].astype(jnp.float32)).astype(total.dtype)
        copies.append(pltpu.make_async_copy(total.at[at], out.at[at], sems.at[c]))
        copies[-1].start()
    for copy in copies:
        copy.wait()


def first_add_kernel(up, up_term, down, down_term, up_out, down_out):
    half = up.shape[0]
    up_out[:half, :] = (up_term[:half, :] + up[...].astype(jnp.float32)).astype(up_out.dtype)
    up_out[half:, :] = up_term[half:, :].astype(up_out.dtype)
    down_out[:half, :] = down_term[:half, :].astype(down_out.dtype)
    down_out[half:, :] = (down_term[half:, :] + down[...].astype(jnp.float32)).astype(down_out.dtype)


def add_kernel(up, up_term, down, down_term, up_out, down_out):
    for out, term, add in ((up_out, up_term, up), (down_out, down_term, down)):
        out[...] = (term[...] + add[...].astype(jnp.float32)).astype(out.dtype)


def shards(src_emb, tgt_emb, src_lang, tgt_lang):
    f32, bf16 = jnp.float32, jnp.bfloat16
    rows, depth = src_emb.shape
    columns = tgt_emb.shape[0]
    row, col = lax.axis_index(ROW), lax.axis_index(COL)
    ring, plane = lax.axis_size(RING), lax.axis_size(PLANE)
    spread_size = lax.axis_size(SPREAD)
    n_src, n_tgt = rows * ring, columns * spread_size
    place, core = lax.axis_index(RING), lax.axis_index("core")
    total_src = src_lang.shape[0] * lax.axis_size(ROW)
    total_tgt = tgt_lang.shape[0] * lax.axis_size(COL)
    offsets = jnp.stack(
        [place, 4 * core, col, row, lax.axis_index("x"), lax.axis_index("y")]
    ).astype(jnp.int32)

    n_label = depth + LANES
    dma = pltpu.SemaphoreType.DMA
    own, tgt = call(
        label_kernel,
        [jax.ShapeDtypeStruct((rows, n_label), bf16), jax.ShapeDtypeStruct((columns, n_label), bf16)],
        [
            pltpu.VMEM((src_lang.shape[0] // LANES, LANES), jnp.int32),
            pltpu.VMEM((tgt_lang.shape[0] // LANES, LANES), jnp.int32),
            pltpu.VMEM((LANES, LANES), f32), dma((4,)),
        ],
        offsets, src_lang.reshape(-1, LANES), tgt_lang.reshape(-1, LANES), src_emb, tgt_emb,
        smem=1, in_hbm=range(1, 5), flops=1, bytes_accessed=2**20,
    )

    def gather_axis(block, axis, at):
        size = lax.axis_size(axis)
        found = [
            lax.ppermute(block, axis, [((i + k) % size, i) for i in range(size)]) for k in range(1, size)
        ]
        return call(
            functools.partial(assemble_kernel, at),
            [jax.ShapeDtypeStruct((size * block.shape[0], block.shape[1]), bf16)], [dma((size,))],
            offsets, block, *found, smem=1, flops=1, bytes_accessed=2**20,
        )[0]

    up, down = shift(own, 1), shift(own, -1)
    pairs = [(down, up)]
    block = gather_axis(tgt, "y", 5)
    block, up, down = lax.optimization_barrier((block, up, down))
    up, down = shift(up, 1), shift(down, -1)
    mine = gather_axis(block, "x", 4)
    pairs.append((down, up))
    up, down = shift(up, 1), shift(down, -1)
    mine, up, down = lax.optimization_barrier((mine, up, down))
    theirs = lax.ppermute(mine, "core", SWAP)

    order = pltpu.VMEM((8, LANES), f32)
    pots = jax.ShapeDtypeStruct((8, LANES), f32)
    to_ring = jax.ShapeDtypeStruct((ring, 8, LANES), f32)
    to_spread = jax.ShapeDtypeStruct((spread_size, 8, LANES), f32)
    pair = [
        jax.ShapeDtypeStruct((2 * rows, n_label), bf16),
        jax.ShapeDtypeStruct((2 * rows, n_tgt), f32),
        jax.ShapeDtypeStruct((n_tgt, 2 * rows), f32),
    ]
    pair_part = jax.ShapeDtypeStruct((2, LANES), f32)
    matmul = 2 * n_src * n_tgt * depth
    scale = LOG2E / (EPSILON * math.sqrt(depth))
    cost = dict(flops=matmul // 2, bytes_accessed=2**22)
    *first, tgt_block = call(
        functools.partial(first_pair_kernel, scale),
        [*pair, pair_part, jax.ShapeDtypeStruct((n_tgt, n_label), bf16)], [dma((4,))],
        *pairs[0], mine, theirs, **cost,
    )

    def pair_logits(near, other, in_hbm):
        return call(
            functools.partial(pair_kernel, scale),
            [*pair, pair_part], [dma((2,))],
            near, other, tgt_block, in_hbm=in_hbm, **cost,
        )

    made = [list(first), list(pair_logits(*pairs[1], ()))]
    made.append(pair_logits(down, up, ()))
    half = rows // 2
    far = [jax.ShapeDtypeStruct((half, n_label), bf16)] * 2
    up, down = call(halves_kernel, far, [dma((2,))], up, down, flops=1, bytes_accessed=1)
    far = shift(up, 1), shift(down, -1)
    single = [
        jax.ShapeDtypeStruct((rows, n_label), bf16),
        jax.ShapeDtypeStruct((rows, n_tgt), f32),
        jax.ShapeDtypeStruct((n_tgt, rows), f32),
    ]
    made.append(
        call(
            functools.partial(own_kernel, scale),
            [*single, jax.ShapeDtypeStruct((1, LANES), f32)], [dma((1,))],
            own, tgt_block, **cost,
        )
    )
    *last, part = call(
        functools.partial(far_kernel, scale),
        [*single, to_ring], [order, dma((2,))],
        offsets, *far, tgt_block, *(m[3] for m in made),
        smem=1, **cost,
    )
    made.append(last)
    src_blocks, logits, logits_t = ([m[k] for m in made] for k in range(3))
    wide_src = pltpu.VMEM((n_src, LANES), f32)
    wide_tgt = pltpu.VMEM((n_tgt, LANES), f32)
    for step in range(ITERS):
        gathered = lax.all_to_all(part, RING, 0, 0)
        part, src_pots = call(
            functools.partial(src_pots_kernel, math.log2(total_tgt)),
            [to_spread, pots], [order, wide_src],
            offsets, *logits, gathered, smem=1, flops=8 * n_src * n_tgt, bytes_accessed=2**22,
        )
        gathered = lax.all_to_all(part, SPREAD, 0, 0)
        if step < ITERS - 1:
            (part,) = call(
                functools.partial(tgt_pots_kernel, math.log2(total_src)),
                [to_ring], [order, wide_tgt],
                offsets, *logits_t, gathered, smem=1, flops=8 * n_src * n_tgt, bytes_accessed=2**22,
            )
    term = jax.ShapeDtypeStruct((rows, depth), f32)

    def src_terms(log_count, units, pieces, tgt_pots, kinds):
        return call(
            functools.partial(src_kernel, log_count, 1.0 / total_tgt, pieces),
            kinds, [order, wide_src],
            offsets, *(logits[u] for u in units), tgt_pots, src_pots, tgt_block,
            smem=1, flops=matmul // 4, bytes_accessed=2**22,
        )

    low = jax.ShapeDtypeStruct((rows, depth), bf16)
    far = [jax.ShapeDtypeStruct((half, depth), bf16)] * 2
    up, down, tgt_pots = src_terms(math.log2(total_src), (4,), [(0, rows, 7 * rows)], gathered, [*far, pots])
    up, down = shift(up, 1), shift(down, -1)
    pieces = [(0, 2 * rows, 0), (0, 2 * rows, 2 * rows), (0, 2 * rows, 4 * rows), (0, rows, 6 * rows)]
    *terms, own_term = src_terms(None, (0, 1, 2, 3), pieces, tgt_pots, [term] * 7)
    keep, give = call(
        functools.partial(tgt_kernel, 1.0 / total_src),
        [jax.ShapeDtypeStruct((n_tgt // 2, depth), f32), jax.ShapeDtypeStruct((n_tgt // 2, depth), bf16)],
        [wide_tgt],
        *logits_t, tgt_pots, src_pots, *src_blocks,
        flops=matmul, bytes_accessed=2**23,
    )
    taken = lax.ppermute(give, "core", SWAP)
    keep, taken, up, down, own_term, *terms = lax.optimization_barrier((keep, taken, up, down, own_term, *terms))
    shares = jax.ShapeDtypeStruct((n_tgt // 2, depth), bf16)
    (sent,) = call(
        add_cores_kernel, [shares], [pltpu.VMEM(shares.shape, bf16), dma((4,))],
        keep, taken, outs_in_hbm=(0,), flops=n_tgt * depth, bytes_accessed=2**22,
    )
    parts = lax.all_to_all(sent.reshape(plane, columns, depth), PLANE, 0, 0)
    for k in (2, 1, 0):
        up, down = call(
            first_add_kernel if k == 2 else add_kernel, [low] * 2, [],
            up, terms[2 * k], down, terms[2 * k + 1], flops=1, bytes_accessed=2**20,
        )
        if k == 0:
            parts, up, down = lax.optimization_barrier((parts, up, down))
        up, down = shift(up, 1), shift(down, -1)
    tgt_pull = jnp.sum(parts.astype(f32), axis=0)
    src_pull = own_term + up.astype(f32) + down.astype(f32)
    row_cost = jnp.sum(src_pull * (src_emb.astype(f32) * (-1.0 / math.sqrt(depth))), axis=1)
    return (src_pull, tgt_pull, row_cost)


def solution(mesh):
    split = Mesh(mesh.devices.reshape(SIZES), AXES)
    return jax.shard_map(
        shards,
        mesh=split,
        in_specs=(P(ROW + COL, None), P(COL + ROW, None), P(ROW), P(COL)),
        out_specs=(P(ROW + COL, None), P(COL + ROW, None), P(ROW + COL)),
        check_vma=False,
    )
```

```python
import functools
import math

import jax
import jax.numpy as jnp
from jax import lax
from jax.experimental import pallas as pl
from jax.experimental.pallas import tpu as pltpu
from jax.sharding import Mesh, PartitionSpec as P

ITERS = 3
NEG = -1e30
EPSILON = 0.5
LOG2E = math.log2(math.e)
LANES = 128
DISTANCES = (1, 7, 2, 6, 3, 5, 0, 4)

AXES = ("x", "zh", "core", "zl", "y")
SIZES = (4, 4, 2, 2, 4)
ROW = ("x", "zh", "core")
COL = ("zl", "y")
RING = ("zh", "zl")
PLANE = ("x", "y")
SPREAD = ("x", "y", "core")
SWAP = [(0, 1), (1, 0)]

VMEM = pl.BlockSpec(memory_space=pltpu.VMEM)
SMEM = pl.BlockSpec(memory_space=pltpu.SMEM)
IN_HBM = pl.BlockSpec(memory_space=pl.ANY)
CONTRACT_LAST = (((1,), (1,)), ((), ()))


def dot(a, b, dims=(((1,), (0,)), ((), ()))):
    return lax.dot_general(a, b, dims, preferred_element_type=jnp.float32)


def call(kernel, outs, scratch, *operands, smem=0, in_hbm=(), outs_in_hbm=(), flops=0, bytes_accessed=0):
    specs = [
        SMEM if k < smem else IN_HBM if k in in_hbm else VMEM for k in range(len(operands))
    ]
    operands = [
        pltpu.with_memory_space_constraint(v, pltpu.HBM) if k in in_hbm else v
        for k, v in enumerate(operands)
    ]
    outs = [
        pltpu.HBM(out.shape, out.dtype) if k in outs_in_hbm else out for k, out in enumerate(outs)
    ]
    return pl.pallas_call(
        kernel,
        out_shape=outs,
        in_specs=specs,
        out_specs=[IN_HBM if k in outs_in_hbm else VMEM for k in range(len(outs))],
        scratch_shapes=scratch,
        compiler_params=pltpu.CompilerParams(vmem_limit_bytes=16 * 2**20),
        cost_estimate=pl.CostEstimate(
            flops=flops, bytes_accessed=bytes_accessed, transcendentals=0
        ),
    )(*operands)


def shift(value, step):
    size = lax.axis_size(RING)
    return lax.ppermute(value, RING, [(i, (i + step) % size) for i in range(size)])


def copy_all(pairs, sems):
    copies = [pltpu.make_async_copy(a, b, sems.at[k]) for k, (a, b) in enumerate(pairs)]
    for copy in copies:
        copy.start()
    for copy in copies:
        copy.wait()


def one_hot(line, dtype):
    labels = jnp.broadcast_to(line.astype(jnp.float32), (LANES, LANES)).T
    lanes = lax.broadcasted_iota(jnp.int32, (LANES, LANES), 1).astype(jnp.float32)
    return (labels == lanes).astype(dtype)


def label_kernel(offsets, src_lang, tgt_lang, src, tgt, src_out, tgt_out, src_labels, tgt_labels, hot, sems):
    columns, depth = tgt.shape
    copies = [
        pltpu.make_async_copy(a, b, sems.at[k])
        for k, (a, b) in enumerate(
            [
                (tgt_lang, tgt_labels),
                (src_lang, src_labels),
                (tgt, tgt_out.at[:, :depth]),
                (src, src_out.at[:, :depth]),
            ]
        )
    ]
    for copy in copies:
        copy.start()
    copies[0].wait()
    here = offsets[3] * columns
    hot[...] = one_hot(tgt_labels[pl.ds(here // LANES, 1), :], jnp.float32)
    tgt_out[:, depth:] = hot[pl.ds(pl.multiple_of(lax.rem(here, LANES), columns), columns), :].astype(tgt_out.dtype)
    copies[1].wait()
    src_out[:, depth:] = one_hot(src_labels[pl.ds(offsets[2], 1), :], src_out.dtype)
    copies[2].wait()
    copies[3].wait()


def assemble_kernel(axis, offsets, *refs):
    (*blocks, out, sems), n = refs, len(refs) - 2
    rows = blocks[0].shape[0]
    places = [lax.rem(offsets[axis] + k, n) * rows for k in range(n)]
    copy_all(
        [(block, out.at[pl.ds(pl.multiple_of(at, rows), rows)]) for block, at in zip(blocks, places)],
        sems,
    )


def assemble_relayed_kernel(offsets, own, first, second, third, relayed, out, sems):
    rows = own.shape[0]
    places = [
        out.at[pl.ds(pl.multiple_of(lax.rem(offsets[4] + k, 4) * rows, rows), rows)] for k in range(4)
    ]

    @pl.when(offsets[1] == 0)
    def _():
        copy_all([(second, places[2])], sems)

    @pl.when(offsets[1] != 0)
    def _():
        copy_all([(relayed, places[2])], sems)

    copy_all([(own, places[0]), (first, places[1]), (third, places[3])], sems)


def columns_sums(tables, added):
    tiles = tables[0].shape[1] // LANES

    def fold(start, join):
        results, row = start, 0
        for table in tables:
            for c in range(table.shape[0] // LANES):
                add = None if added is None else added[row : row + LANES, :]
                for t in range(tiles):
                    z = table[c * LANES : (c + 1) * LANES, t * LANES : (t + 1) * LANES]
                    z = (z if add is None else z + add).reshape(LANES // 8, 8, LANES)
                    results[t] = join(t, results[t], z)
                row += LANES
        return results

    def larger(t, top, z):
        z = jnp.max(z, axis=0)
        return z if top is None else jnp.maximum(top, z)

    tops = [jnp.max(top, axis=0, keepdims=True) for top in fold([None] * tiles, larger)]

    def total(t, so_far, z):
        z = jnp.sum(jnp.exp2(z - tops[t][None]), axis=0)
        return z if so_far is None else so_far + z

    totals = [jnp.sum(v, axis=0, keepdims=True) for v in fold([None] * tiles, total)]
    return tops, totals


def columns_lse(tables, added):
    return [top + jnp.log2(total) for top, total in zip(*columns_sums(tables, added))]


def send_out(parts, offset, table, order, out):
    for part, at in zip(parts, table):
        order[pl.ds(lax.rem(at + offset, 8), 1), :] = part
    out[...] = jnp.broadcast_to(order[...][None], out.shape)


def merge(gathered, log_count, offset, table, order):
    parts = gathered[...]
    top = jnp.max(parts, axis=0)
    total = jnp.sum(jnp.exp2(parts - top[None]), axis=0)
    order[...] = log_count - (top + jnp.log2(total))
    return jnp.concatenate([order[pl.ds(lax.rem(at + offset, 8), 1), :] for at in table])


def spread(pots, wide):
    columns = pots.T
    for c in range(8):
        wide[c * LANES : (c + 1) * LANES, :] = jnp.broadcast_to(
            columns[:, c : c + 1], (LANES, LANES)
        )


def make_logits(scale, src, tgt, logits, logits_t):
    depth = src.shape[1] - LANES
    emb, hot = src[:, :depth], src[:, depth:]
    step = 256
    for start in range(0, tgt.shape[0], step):
        to = slice(start, start + step)
        same = dot(tgt[to, depth:], hot, CONTRACT_LAST) > 0.5
        value = jnp.where(same, dot(tgt[to, :depth], emb, CONTRACT_LAST) * scale, NEG)
        logits_t[to, :] = value
        logits[:, to] = value.T


def first_pair_kernel(scale, near, other, mine, theirs, src, logits, logits_t, part, tgt, sems):
    half = mine.shape[0]
    copy_all(
        [
            (mine, tgt.at[:half]),
            (theirs, tgt.at[half:]),
            (near, src.at[: near.shape[0]]),
            (other, src.at[near.shape[0] :]),
        ],
        sems,
    )
    make_logits(scale, src, tgt, logits, logits_t)
    part[...] = jnp.concatenate(columns_lse([logits_t], None))


def halves_kernel(up, down, up_out, down_out, sems):
    half = up_out.shape[0]
    copy_all([(up.at[:half], up_out), (down.at[half:], down_out)], sems)


def pair_kernel(scale, near, other, tgt, src, logits, logits_t, part, sems):
    copy_all([(near, src.at[: near.shape[0]]), (other, src.at[near.shape[0] :])], sems)
    make_logits(scale, src, tgt, logits, logits_t)
    part[...] = jnp.concatenate(columns_lse([logits_t], None))


def own_kernel(scale, own, tgt, src, logits, logits_t, part, sems):
    copy_all([(own, src)], sems)
    make_logits(scale, src, tgt, logits, logits_t)
    part[...] = jnp.concatenate(columns_lse([logits_t], None))


def far_kernel(scale, offsets, far_up, far_down, tgt, *refs):
    parts, (src, logits, logits_t, out, order, sems) = refs[:4], refs[4:]
    half = far_up.shape[0]
    copy_all([(far_up, src.at[:half]), (far_down, src.at[half:])], sems)
    make_logits(scale, src, tgt, logits, logits_t)
    parts = [part[r : r + 1, :] for part in parts for r in range(part.shape[0])]
    send_out(parts + columns_lse([logits_t], None), offsets[0], DISTANCES, order, out)


def src_pots_kernel(log_count, offsets, *refs):
    tables, (gathered, out, pots, order, wide) = refs[:5], refs[5:]
    local = merge(gathered, log_count, offsets[0], DISTANCES, order)
    pots[...] = local
    spread(local, wide)
    send_out(columns_lse(tables, wide), offsets[1], range(8), order, out)


def tgt_pots_kernel(log_count, offsets, *refs):
    tables, (gathered, out, order, wide) = refs[:5], refs[5:]
    spread(merge(gathered, log_count, offsets[1], range(8), order), wide)
    parts = [part for table in tables for part in columns_lse([table], wide)]
    send_out(parts, offsets[0], DISTANCES, order, out)


def src_kernel(log_count, share, pieces, offsets, *refs):
    n = len(pieces)
    tables, (tgt_pots, src_pots, block), outs = refs[:n], refs[n : n + 3], refs[n + 3 : -2]
    order, wide = refs[-2:]
    depth, half = outs[0].shape[1], block.shape[0] // 2
    if log_count is None:
        tgt = tgt_pots[...]
    else:
        tgt = merge(tgt_pots, log_count, offsets[1], range(8), order)
        outs[-1][...] = tgt
        outs = outs[:-1]
    spread(src_pots[...], wide)
    outs = list(outs)
    for (first, rows, place), table in zip(pieces, tables):
        at = slice(place, place + rows)
        weight = [
            jnp.exp2(table[first : first + rows, t * LANES : (t + 1) * LANES] + wide[at, :] + tgt[t : t + 1, :])
            .astype(jnp.bfloat16)
            for t in range(8)
        ]
        left = jnp.concatenate(weight[:4], axis=1)
        right = jnp.concatenate(weight[4:], axis=1)
        pull = (dot(left, block[:half, :depth]) + dot(right, block[half:, :depth])) * share
        start = 0
        while start < rows:
            out = outs.pop(0)
            out[...] = pull[start : start + out.shape[0]].astype(out.dtype)
            start += out.shape[0]


def tgt_kernel(share, *refs):
    tables, (tgt_pots, src_pots), blocks = refs[:5], refs[5:7], refs[7:12]
    keep, give, wide = refs[12:]
    spread(tgt_pots[...], wide)
    src = src_pots[...]
    depth = keep.shape[1]
    for unit in (2, 3, 0, 1):
        at = slice(unit * 256, (unit + 1) * 256)
        weight, line = [], 0
        for table in tables:
            for t in range(table.shape[1] // LANES):
                z = table[at, t * LANES : (t + 1) * LANES] + src[line : line + 1, :] + wide[at, :]
                weight.append(jnp.exp2(z).astype(jnp.bfloat16))
                line += 1
        pull = 0.0
        for k in range(3):
            pull = pull + dot(jnp.concatenate(weight[2 * k : 2 * k + 2], axis=1), blocks[k][:, :depth])
        last = jnp.concatenate([blocks[3][:, :depth], blocks[4][:, :depth]])
        pull = pull + dot(jnp.concatenate(weight[6:], axis=1), last)
        to = slice((unit % 2) * 256, (unit % 2 + 1) * 256)
        if unit < 2:
            keep[to, :] = pull * share
        else:
            give[to, :] = (pull * share).astype(give.dtype)


def add_cores_kernel(keep, taken, out, total, sems):
    rows = keep.shape[0] // sems.shape[0]
    copies = []
    for c in range(sems.shape[0]):
        at = slice(c * rows, (c + 1) * rows)
        total[at, :] = (keep[at, :] + taken[at, :].astype(jnp.float32)).astype(total.dtype)
        copies.append(pltpu.make_async_copy(total.at[at], out.at[at], sems.at[c]))
        copies[-1].start()
    for copy in copies:
        copy.wait()


def first_add_kernel(up, up_term, down, down_term, up_out, down_out):
    half = up.shape[0]
    up_out[:half, :] = (up_term[:half, :] + up[...].astype(jnp.float32)).astype(up_out.dtype)
    up_out[half:, :] = up_term[half:, :].astype(up_out.dtype)
    down_out[:half, :] = down_term[:half, :].astype(down_out.dtype)
    down_out[half:, :] = (down_term[half:, :] + down[...].astype(jnp.float32)).astype(down_out.dtype)


def add_kernel(up, up_term, down, down_term, up_out, down_out):
    for out, term, add in ((up_out, up_term, up), (down_out, down_term, down)):
        out[...] = (term[...] + add[...].astype(jnp.float32)).astype(out.dtype)


def shards(src_emb, tgt_emb, src_lang, tgt_lang):
    f32, bf16 = jnp.float32, jnp.bfloat16
    rows, depth = src_emb.shape
    columns = tgt_emb.shape[0]
    row, col = lax.axis_index(ROW), lax.axis_index(COL)
    ring, plane = lax.axis_size(RING), lax.axis_size(PLANE)
    spread_size = lax.axis_size(SPREAD)
    n_src, n_tgt = rows * ring, columns * spread_size
    place, core = lax.axis_index(RING), lax.axis_index("core")
    total_src = src_lang.shape[0] * lax.axis_size(ROW)
    total_tgt = tgt_lang.shape[0] * lax.axis_size(COL)
    offsets = jnp.stack(
        [place, 4 * core, col, row, lax.axis_index("x"), lax.axis_index("y")]
    ).astype(jnp.int32)

    n_label = depth + LANES
    dma = pltpu.SemaphoreType.DMA
    own, tgt = call(
        label_kernel,
        [jax.ShapeDtypeStruct((rows, n_label), bf16), jax.ShapeDtypeStruct((columns, n_label), bf16)],
        [
            pltpu.VMEM((src_lang.shape[0] // LANES, LANES), jnp.int32),
            pltpu.VMEM((tgt_lang.shape[0] // LANES, LANES), jnp.int32),
            pltpu.VMEM((LANES, LANES), f32), dma((4,)),
        ],
        offsets, src_lang.reshape(-1, LANES), tgt_lang.reshape(-1, LANES), src_emb, tgt_emb,
        smem=1, in_hbm=range(1, 5), flops=1, bytes_accessed=2**20,
    )

    def gather_axis(block, axis, at):
        size = lax.axis_size(axis)
        found = [
            lax.ppermute(block, axis, [((i + k) % size, i) for i in range(size)]) for k in range(1, size)
        ]
        return call(
            functools.partial(assemble_kernel, at),
            [jax.ShapeDtypeStruct((size * block.shape[0], block.shape[1]), bf16)], [dma((size,))],
            offsets, block, *found, smem=1, flops=1, bytes_accessed=2**20,
        )[0]

    up, down = shift(own, 1), shift(own, -1)
    pairs = [(down, up)]
    block = gather_axis(tgt, "y", 5)
    block, up, down = lax.optimization_barrier((block, up, down))
    up, down = shift(up, 1), shift(down, -1)
    first, third = (lax.ppermute(block, "x", [((i + k) % 4, i) for i in range(4)]) for k in (1, 3))
    pairs_of = lambda step, c: [(((i + step) % 4) * 2 + c, i * 2 + c) for i in range(4)]
    second = lax.ppermute(block, ("x", "core"), pairs_of(2, 0))
    relayed = lax.ppermute(third, ("x", "core"), pairs_of(3, 1))
    (mine,) = call(
        assemble_relayed_kernel, [jax.ShapeDtypeStruct((plane * columns, n_label), bf16)], [dma((3,))],
        offsets, block, first, second, third, relayed, smem=1, flops=1, bytes_accessed=2**20,
    )
    pairs.append((down, up))
    up, down = shift(up, 1), shift(down, -1)
    mine, up, down = lax.optimization_barrier((mine, up, down))
    theirs = lax.ppermute(mine, "core", SWAP)

    order = pltpu.VMEM((8, LANES), f32)
    pots = jax.ShapeDtypeStruct((8, LANES), f32)
    to_ring = jax.ShapeDtypeStruct((ring, 8, LANES), f32)
    to_spread = jax.ShapeDtypeStruct((spread_size, 8, LANES), f32)
    pair = [
        jax.ShapeDtypeStruct((2 * rows, n_label), bf16),
        jax.ShapeDtypeStruct((2 * rows, n_tgt), f32),
        jax.ShapeDtypeStruct((n_tgt, 2 * rows), f32),
    ]
    pair_part = jax.ShapeDtypeStruct((2, LANES), f32)
    matmul = 2 * n_src * n_tgt * depth
    scale = LOG2E / (EPSILON * math.sqrt(depth))
    cost = dict(flops=matmul // 2, bytes_accessed=2**22)
    *first, tgt_block = call(
        functools.partial(first_pair_kernel, scale),
        [*pair, pair_part, jax.ShapeDtypeStruct((n_tgt, n_label), bf16)], [dma((4,))],
        *pairs[0], mine, theirs, **cost,
    )

    def pair_logits(near, other, in_hbm):
        return call(
            functools.partial(pair_kernel, scale),
            [*pair, pair_part], [dma((2,))],
            near, other, tgt_block, in_hbm=in_hbm, **cost,
        )

    made = [list(first), list(pair_logits(*pairs[1], ()))]
    made.append(pair_logits(down, up, ()))
    half = rows // 2
    far = [jax.ShapeDtypeStruct((half, n_label), bf16)] * 2
    up, down = call(halves_kernel, far, [dma((2,))], up, down, flops=1, bytes_accessed=1)
    far = shift(up, 1), shift(down, -1)
    single = [
        jax.ShapeDtypeStruct((rows, n_label), bf16),
        jax.ShapeDtypeStruct((rows, n_tgt), f32),
        jax.ShapeDtypeStruct((n_tgt, rows), f32),
    ]
    made.append(
        call(
            functools.partial(own_kernel, scale),
            [*single, jax.ShapeDtypeStruct((1, LANES), f32)], [dma((1,))],
            own, tgt_block, **cost,
        )
    )
    *last, part = call(
        functools.partial(far_kernel, scale),
        [*single, to_ring], [order, dma((2,))],
        offsets, *far, tgt_block, *(m[3] for m in made),
        smem=1, **cost,
    )
    made.append(last)
    src_blocks, logits, logits_t = ([m[k] for m in made] for k in range(3))
    wide_src = pltpu.VMEM((n_src, LANES), f32)
    wide_tgt = pltpu.VMEM((n_tgt, LANES), f32)
    for step in range(ITERS):
        gathered = lax.all_to_all(part, RING, 0, 0)
        part, src_pots = call(
            functools.partial(src_pots_kernel, math.log2(total_tgt)),
            [to_spread, pots], [order, wide_src],
            offsets, *logits, gathered, smem=1, flops=8 * n_src * n_tgt, bytes_accessed=2**22,
        )
        gathered = lax.all_to_all(part, SPREAD, 0, 0)
        if step < ITERS - 1:
            (part,) = call(
                functools.partial(tgt_pots_kernel, math.log2(total_src)),
                [to_ring], [order, wide_tgt],
                offsets, *logits_t, gathered, smem=1, flops=8 * n_src * n_tgt, bytes_accessed=2**22,
            )
    term = jax.ShapeDtypeStruct((rows, depth), f32)

    def src_terms(log_count, units, pieces, tgt_pots, kinds):
        return call(
            functools.partial(src_kernel, log_count, 1.0 / total_tgt, pieces),
            kinds, [order, wide_src],
            offsets, *(logits[u] for u in units), tgt_pots, src_pots, tgt_block,
            smem=1, flops=matmul // 4, bytes_accessed=2**22,
        )

    low = jax.ShapeDtypeStruct((rows, depth), bf16)
    far = [jax.ShapeDtypeStruct((half, depth), bf16)] * 2
    up, down, tgt_pots = src_terms(math.log2(total_src), (4,), [(0, rows, 7 * rows)], gathered, [*far, pots])
    up, down = shift(up, 1), shift(down, -1)
    pieces = [(0, 2 * rows, 0), (0, 2 * rows, 2 * rows), (0, 2 * rows, 4 * rows), (0, rows, 6 * rows)]
    *terms, own_term = src_terms(None, (0, 1, 2, 3), pieces, tgt_pots, [term] * 7)
    keep, give = call(
        functools.partial(tgt_kernel, 1.0 / total_src),
        [jax.ShapeDtypeStruct((n_tgt // 2, depth), f32), jax.ShapeDtypeStruct((n_tgt // 2, depth), bf16)],
        [wide_tgt],
        *logits_t, tgt_pots, src_pots, *src_blocks,
        flops=matmul, bytes_accessed=2**23,
    )
    taken = lax.ppermute(give, "core", SWAP)
    keep, taken, up, down, own_term, *terms = lax.optimization_barrier((keep, taken, up, down, own_term, *terms))
    shares = jax.ShapeDtypeStruct((n_tgt // 2, depth), bf16)
    (sent,) = call(
        add_cores_kernel, [shares], [pltpu.VMEM(shares.shape, bf16), dma((4,))],
        keep, taken, outs_in_hbm=(0,), flops=n_tgt * depth, bytes_accessed=2**22,
    )
    parts = lax.all_to_all(sent.reshape(plane, columns, depth), PLANE, 0, 0)
    for k in (2, 1, 0):
        up, down = call(
            first_add_kernel if k == 2 else add_kernel, [low] * 2, [],
            up, terms[2 * k], down, terms[2 * k + 1], flops=1, bytes_accessed=2**20,
        )
        if k == 0:
            parts, up, down = lax.optimization_barrier((parts, up, down))
        up, down = shift(up, 1), shift(down, -1)
    tgt_pull = jnp.sum(parts.astype(f32), axis=0)
    src_pull = own_term + up.astype(f32) + down.astype(f32)
    row_cost = jnp.sum(src_pull * (src_emb.astype(f32) * (-1.0 / math.sqrt(depth))), axis=1)
    return (src_pull, tgt_pull, row_cost)


def solution(mesh):
    split = Mesh(mesh.devices.reshape(SIZES), AXES)
    return jax.shard_map(
        shards,
        mesh=split,
        in_specs=(P(ROW + COL, None), P(COL + ROW, None), P(ROW), P(COL)),
        out_specs=(P(ROW + COL, None), P(COL + ROW, None), P(ROW + COL)),
        check_vma=False,
    )
```

```python
import functools
import math

import jax
import jax.numpy as jnp
from jax import lax
from jax.experimental import pallas as pl
from jax.experimental.pallas import tpu as pltpu
from jax.sharding import Mesh, PartitionSpec as P

ITERS = 3
NEG = -1e30
EPSILON = 0.5
LOG2E = math.log2(math.e)
LANES = 128
DISTANCES = (1, 7, 2, 6, 3, 5, 0, 4)

AXES = ("x", "zh", "core", "zl", "y")
SIZES = (4, 4, 2, 2, 4)
ROW = ("x", "zh", "core")
COL = ("zl", "y")
RING = ("zh", "zl")
PLANE = ("x", "y")
SPREAD = ("x", "y", "core")
SWAP = [(0, 1), (1, 0)]

VMEM = pl.BlockSpec(memory_space=pltpu.VMEM)
SMEM = pl.BlockSpec(memory_space=pltpu.SMEM)
IN_HBM = pl.BlockSpec(memory_space=pl.ANY)
CONTRACT_LAST = (((1,), (1,)), ((), ()))


def dot(a, b, dims=(((1,), (0,)), ((), ()))):
    return lax.dot_general(a, b, dims, preferred_element_type=jnp.float32)


def call(kernel, outs, scratch, *operands, smem=0, in_hbm=(), outs_in_hbm=(), flops=0, bytes_accessed=0):
    specs = [
        SMEM if k < smem else IN_HBM if k in in_hbm else VMEM for k in range(len(operands))
    ]
    operands = [
        pltpu.with_memory_space_constraint(v, pltpu.HBM) if k in in_hbm else v
        for k, v in enumerate(operands)
    ]
    outs = [
        pltpu.HBM(out.shape, out.dtype) if k in outs_in_hbm else out for k, out in enumerate(outs)
    ]
    return pl.pallas_call(
        kernel,
        out_shape=outs,
        in_specs=specs,
        out_specs=[IN_HBM if k in outs_in_hbm else VMEM for k in range(len(outs))],
        scratch_shapes=scratch,
        compiler_params=pltpu.CompilerParams(vmem_limit_bytes=16 * 2**20),
        cost_estimate=pl.CostEstimate(
            flops=flops, bytes_accessed=bytes_accessed, transcendentals=0
        ),
    )(*operands)


def shift(value, step):
    size = lax.axis_size(RING)
    return lax.ppermute(value, RING, [(i, (i + step) % size) for i in range(size)])


def copy_all(pairs, sems):
    copies = [pltpu.make_async_copy(a, b, sems.at[k]) for k, (a, b) in enumerate(pairs)]
    for copy in copies:
        copy.start()
    for copy in copies:
        copy.wait()


def one_hot(line, dtype):
    labels = jnp.broadcast_to(line.astype(jnp.float32), (LANES, LANES)).T
    lanes = lax.broadcasted_iota(jnp.int32, (LANES, LANES), 1).astype(jnp.float32)
    return (labels == lanes).astype(dtype)


def label_kernel(offsets, src_lang, tgt_lang, src, tgt, src_out, tgt_out, src_labels, tgt_labels, hot, sems):
    columns, depth = tgt.shape
    copies = [
        pltpu.make_async_copy(a, b, sems.at[k])
        for k, (a, b) in enumerate(
            [
                (tgt_lang, tgt_labels),
                (src_lang, src_labels),
                (tgt, tgt_out.at[:, :depth]),
                (src, src_out.at[:, :depth]),
            ]
        )
    ]
    for copy in copies:
        copy.start()
    copies[0].wait()
    here = offsets[3] * columns
    hot[...] = one_hot(tgt_labels[pl.ds(here // LANES, 1), :], jnp.float32)
    tgt_out[:, depth:] = hot[pl.ds(pl.multiple_of(lax.rem(here, LANES), columns), columns), :].astype(tgt_out.dtype)
    copies[1].wait()
    src_out[:, depth:] = one_hot(src_labels[pl.ds(offsets[2], 1), :], src_out.dtype)
    copies[2].wait()
    copies[3].wait()


def assemble_kernel(axis, offsets, *refs):
    (*blocks, out, sems), n = refs, len(refs) - 2
    rows = blocks[0].shape[0]
    places = [lax.rem(offsets[axis] + k, n) * rows for k in range(n)]
    copy_all(
        [(block, out.at[pl.ds(pl.multiple_of(at, rows), rows)]) for block, at in zip(blocks, places)],
        sems,
    )


def assemble_relayed_kernel(offsets, own, first, second, third, relayed, out, sems):
    rows = own.shape[0]
    places = [
        out.at[pl.ds(pl.multiple_of(lax.rem(offsets[4] + k, 4) * rows, rows), rows)] for k in range(4)
    ]

    rest = [
        pltpu.make_async_copy(block, places[k], sems.at[n])
        for n, (k, block) in enumerate(((0, own), (1, first), (3, third)))
    ]
    for copy in rest:
        copy.start()

    @pl.when(offsets[1] == 0)
    def _():
        pltpu.make_async_copy(second, places[2], sems.at[3]).start()

    @pl.when(offsets[1] != 0)
    def _():
        pltpu.make_async_copy(relayed, places[2], sems.at[3]).start()

    for copy in rest:
        copy.wait()
    pltpu.make_async_copy(second, places[2], sems.at[3]).wait()


def columns_sums(tables, added):
    tiles = tables[0].shape[1] // LANES

    def fold(start, join):
        results, row = start, 0
        for table in tables:
            for c in range(table.shape[0] // LANES):
                add = None if added is None else added[row : row + LANES, :]
                for t in range(tiles):
                    z = table[c * LANES : (c + 1) * LANES, t * LANES : (t + 1) * LANES]
                    z = (z if add is None else z + add).reshape(LANES // 8, 8, LANES)
                    results[t] = join(t, results[t], z)
                row += LANES
        return results

    def larger(t, top, z):
        z = jnp.max(z, axis=0)
        return z if top is None else jnp.maximum(top, z)

    tops = [jnp.max(top, axis=0, keepdims=True) for top in fold([None] * tiles, larger)]

    def total(t, so_far, z):
        z = jnp.sum(jnp.exp2(z - tops[t][None]), axis=0)
        return z if so_far is None else so_far + z

    totals = [jnp.sum(v, axis=0, keepdims=True) for v in fold([None] * tiles, total)]
    return tops, totals


def columns_lse(tables, added):
    return [top + jnp.log2(total) for top, total in zip(*columns_sums(tables, added))]


def send_out(parts, offset, table, order, out):
    for part, at in zip(parts, table):
        order[pl.ds(lax.rem(at + offset, 8), 1), :] = part
    out[...] = jnp.broadcast_to(order[...][None], out.shape)


def merge(gathered, log_count, offset, table, order):
    parts = gathered[...]
    top = jnp.max(parts, axis=0)
    total = jnp.sum(jnp.exp2(parts - top[None]), axis=0)
    order[...] = log_count - (top + jnp.log2(total))
    return jnp.concatenate([order[pl.ds(lax.rem(at + offset, 8), 1), :] for at in table])


def spread(pots, wide, lines=range(8)):
    columns = pots.T
    for c in lines:
        wide[c * LANES : (c + 1) * LANES, :] = jnp.broadcast_to(
            columns[:, c : c + 1], (LANES, LANES)
        )


def make_logits(scale, src, tgt, logits, logits_t):
    depth = src.shape[1] - LANES
    emb, hot = src[:, :depth], src[:, depth:]
    step = 256
    for start in range(0, tgt.shape[0], step):
        to = slice(start, start + step)
        same = dot(tgt[to, depth:], hot, CONTRACT_LAST) > 0.5
        value = jnp.where(same, dot(tgt[to, :depth], emb, CONTRACT_LAST) * scale, NEG)
        logits_t[to, :] = value
        logits[:, to] = value.T


def first_pair_kernel(scale, near, other, mine, theirs, src, logits, logits_t, part, tgt, sems):
    half = mine.shape[0]
    copy_all(
        [
            (mine, tgt.at[:half]),
            (theirs, tgt.at[half:]),
            (near, src.at[: near.shape[0]]),
            (other, src.at[near.shape[0] :]),
        ],
        sems,
    )
    make_logits(scale, src, tgt, logits, logits_t)
    part[...] = jnp.concatenate(columns_lse([logits_t], None))


def halves_kernel(up, down, up_out, down_out, sems):
    half = up_out.shape[0]
    copy_all([(up.at[:half], up_out), (down.at[half:], down_out)], sems)


def pair_kernel(scale, near, other, tgt, src, logits, logits_t, part, sems):
    copy_all([(near, src.at[: near.shape[0]]), (other, src.at[near.shape[0] :])], sems)
    make_logits(scale, src, tgt, logits, logits_t)
    part[...] = jnp.concatenate(columns_lse([logits_t], None))


def own_kernel(scale, own, tgt, src, logits, logits_t, part, sems):
    copy_all([(own, src)], sems)
    make_logits(scale, src, tgt, logits, logits_t)
    part[...] = jnp.concatenate(columns_lse([logits_t], None))


def far_kernel(scale, offsets, far_up, far_down, tgt, *refs):
    parts, (src, logits, logits_t, out, order, sems) = refs[:4], refs[4:]
    half = far_up.shape[0]
    copy_all([(far_up, src.at[:half]), (far_down, src.at[half:])], sems)
    make_logits(scale, src, tgt, logits, logits_t)
    parts = [part[r : r + 1, :] for part in parts for r in range(part.shape[0])]
    send_out(parts + columns_lse([logits_t], None), offsets[0], DISTANCES, order, out)


def src_pots_kernel(log_count, offsets, *refs):
    tables, (gathered, out, pots, order, wide) = refs[:5], refs[5:]
    local = merge(gathered, log_count, offsets[0], DISTANCES, order)
    pots[...] = local
    spread(local, wide)
    send_out(columns_lse(tables, wide), offsets[1], range(8), order, out)


def tgt_pots_kernel(log_count, offsets, *refs):
    tables, (gathered, out, order, wide) = refs[:5], refs[5:]
    spread(merge(gathered, log_count, offsets[1], range(8), order), wide)
    parts = [part for table in tables for part in columns_lse([table], wide)]
    send_out(parts, offsets[0], DISTANCES, order, out)


def src_kernel(log_count, share, pieces, offsets, *refs):
    n = len(pieces)
    tables, (tgt_pots, src_pots, block), outs = refs[:n], refs[n : n + 3], refs[n + 3 : -2]
    order, wide = refs[-2:]
    depth, half = outs[0].shape[1], block.shape[0] // 2
    if log_count is None:
        tgt = tgt_pots[...]
    else:
        tgt = merge(tgt_pots, log_count, offsets[1], range(8), order)
        outs[-1][...] = tgt
        outs = outs[:-1]
    lines = [c for _, n_rows, at in pieces for c in range(at // LANES, (at + n_rows) // LANES)]
    spread(src_pots[...], wide, lines)
    outs = list(outs)
    for (first, rows, place), table in zip(pieces, tables):
        at = slice(place, place + rows)
        weight = [
            jnp.exp2(table[first : first + rows, t * LANES : (t + 1) * LANES] + wide[at, :] + tgt[t : t + 1, :])
            .astype(jnp.bfloat16)
            for t in range(8)
        ]
        left = jnp.concatenate(weight[:4], axis=1)
        right = jnp.concatenate(weight[4:], axis=1)
        pull = (dot(left, block[:half, :depth]) + dot(right, block[half:, :depth])) * share
        start = 0
        while start < rows:
            out = outs.pop(0)
            out[...] = pull[start : start + out.shape[0]].astype(out.dtype)
            start += out.shape[0]


def tgt_kernel(share, *refs):
    tables, (tgt_pots, src_pots), blocks = refs[:5], refs[5:7], refs[7:12]
    keep, give, wide = refs[12:]
    spread(tgt_pots[...], wide)
    src = src_pots[...]
    depth = keep.shape[1]
    for unit in (2, 3, 0, 1):
        at = slice(unit * 256, (unit + 1) * 256)
        weight, line = [], 0
        for table in tables:
            for t in range(table.shape[1] // LANES):
                z = table[at, t * LANES : (t + 1) * LANES] + src[line : line + 1, :] + wide[at, :]
                weight.append(jnp.exp2(z).astype(jnp.bfloat16))
                line += 1
        pull = 0.0
        for k in range(3):
            pull = pull + dot(jnp.concatenate(weight[2 * k : 2 * k + 2], axis=1), blocks[k][:, :depth])
        last = jnp.concatenate([blocks[3][:, :depth], blocks[4][:, :depth]])
        pull = pull + dot(jnp.concatenate(weight[6:], axis=1), last)
        to = slice((unit % 2) * 256, (unit % 2 + 1) * 256)
        if unit < 2:
            keep[to, :] = pull * share
        else:
            give[to, :] = (pull * share).astype(give.dtype)


def add_cores_kernel(keep, taken, out, total, sems):
    rows = keep.shape[0] // sems.shape[0]
    copies = []
    for c in range(sems.shape[0]):
        at = slice(c * rows, (c + 1) * rows)
        total[at, :] = (keep[at, :] + taken[at, :].astype(jnp.float32)).astype(total.dtype)
        copies.append(pltpu.make_async_copy(total.at[at], out.at[at], sems.at[c]))
        copies[-1].start()
    for copy in copies:
        copy.wait()


def first_add_kernel(up, up_term, down, down_term, up_out, down_out):
    half = up.shape[0]
    up_out[:half, :] = (up_term[:half, :] + up[...].astype(jnp.float32)).astype(up_out.dtype)
    up_out[half:, :] = up_term[half:, :].astype(up_out.dtype)
    down_out[:half, :] = down_term[:half, :].astype(down_out.dtype)
    down_out[half:, :] = (down_term[half:, :] + down[...].astype(jnp.float32)).astype(down_out.dtype)


def add_kernel(up, up_term, down, down_term, up_out, down_out):
    for out, term, add in ((up_out, up_term, up), (down_out, down_term, down)):
        out[...] = (term[...] + add[...].astype(jnp.float32)).astype(out.dtype)


def shards(src_emb, tgt_emb, src_lang, tgt_lang):
    f32, bf16 = jnp.float32, jnp.bfloat16
    rows, depth = src_emb.shape
    columns = tgt_emb.shape[0]
    row, col = lax.axis_index(ROW), lax.axis_index(COL)
    ring, plane = lax.axis_size(RING), lax.axis_size(PLANE)
    spread_size = lax.axis_size(SPREAD)
    n_src, n_tgt = rows * ring, columns * spread_size
    place, core = lax.axis_index(RING), lax.axis_index("core")
    total_src = src_lang.shape[0] * lax.axis_size(ROW)
    total_tgt = tgt_lang.shape[0] * lax.axis_size(COL)
    offsets = jnp.stack(
        [place, 4 * core, col, row, lax.axis_index("x"), lax.axis_index("y")]
    ).astype(jnp.int32)

    n_label = depth + LANES
    dma = pltpu.SemaphoreType.DMA
    own, tgt = call(
        label_kernel,
        [jax.ShapeDtypeStruct((rows, n_label), bf16), jax.ShapeDtypeStruct((columns, n_label), bf16)],
        [
            pltpu.VMEM((src_lang.shape[0] // LANES, LANES), jnp.int32),
            pltpu.VMEM((tgt_lang.shape[0] // LANES, LANES), jnp.int32),
            pltpu.VMEM((LANES, LANES), f32), dma((4,)),
        ],
        offsets, src_lang.reshape(-1, LANES), tgt_lang.reshape(-1, LANES), src_emb, tgt_emb,
        smem=1, in_hbm=range(1, 5), flops=1, bytes_accessed=2**20,
    )

    def gather_axis(block, axis, at):
        size = lax.axis_size(axis)
        found = [
            lax.ppermute(block, axis, [((i + k) % size, i) for i in range(size)]) for k in range(1, size)
        ]
        return call(
            functools.partial(assemble_kernel, at),
            [jax.ShapeDtypeStruct((size * block.shape[0], block.shape[1]), bf16)], [dma((size,))],
            offsets, block, *found, smem=1, flops=1, bytes_accessed=2**20,
        )[0]

    up, down = shift(own, 1), shift(own, -1)
    pairs = [(down, up)]
    block = gather_axis(tgt, "y", 5)
    block, up, down = lax.optimization_barrier((block, up, down))
    up, down = shift(up, 1), shift(down, -1)
    first, third = (lax.ppermute(block, "x", [((i + k) % 4, i) for i in range(4)]) for k in (1, 3))
    pairs_of = lambda step, c: [(((i + step) % 4) * 2 + c, i * 2 + c) for i in range(4)]
    second = lax.ppermute(block, ("x", "core"), pairs_of(2, 0))
    relayed = lax.ppermute(third, ("x", "core"), pairs_of(3, 1))
    (mine,) = call(
        assemble_relayed_kernel, [jax.ShapeDtypeStruct((plane * columns, n_label), bf16)], [dma((4,))],
        offsets, block, first, second, third, relayed, smem=1, flops=1, bytes_accessed=2**20,
    )
    pairs.append((down, up))
    up, down = shift(up, 1), shift(down, -1)
    mine, up, down = lax.optimization_barrier((mine, up, down))
    theirs = lax.ppermute(mine, "core", SWAP)

    order = pltpu.VMEM((8, LANES), f32)
    pots = jax.ShapeDtypeStruct((8, LANES), f32)
    to_ring = jax.ShapeDtypeStruct((ring, 8, LANES), f32)
    to_spread = jax.ShapeDtypeStruct((spread_size, 8, LANES), f32)
    pair = [
        jax.ShapeDtypeStruct((2 * rows, n_label), bf16),
        jax.ShapeDtypeStruct((2 * rows, n_tgt), f32),
        jax.ShapeDtypeStruct((n_tgt, 2 * rows), f32),
    ]
    pair_part = jax.ShapeDtypeStruct((2, LANES), f32)
    matmul = 2 * n_src * n_tgt * depth
    scale = LOG2E / (EPSILON * math.sqrt(depth))
    cost = dict(flops=matmul // 2, bytes_accessed=2**22)
    *first, tgt_block = call(
        functools.partial(first_pair_kernel, scale),
        [*pair, pair_part, jax.ShapeDtypeStruct((n_tgt, n_label), bf16)], [dma((4,))],
        *pairs[0], mine, theirs, **cost,
    )

    def pair_logits(near, other, in_hbm):
        return call(
            functools.partial(pair_kernel, scale),
            [*pair, pair_part], [dma((2,))],
            near, other, tgt_block, in_hbm=in_hbm, **cost,
        )

    made = [list(first), list(pair_logits(*pairs[1], ()))]
    made.append(pair_logits(down, up, ()))
    half = rows // 2
    far = [jax.ShapeDtypeStruct((half, n_label), bf16)] * 2
    up, down = call(halves_kernel, far, [dma((2,))], up, down, flops=1, bytes_accessed=1)
    far = shift(up, 1), shift(down, -1)
    single = [
        jax.ShapeDtypeStruct((rows, n_label), bf16),
        jax.ShapeDtypeStruct((rows, n_tgt), f32),
        jax.ShapeDtypeStruct((n_tgt, rows), f32),
    ]
    made.append(
        call(
            functools.partial(own_kernel, scale),
            [*single, jax.ShapeDtypeStruct((1, LANES), f32)], [dma((1,))],
            own, tgt_block, **cost,
        )
    )
    *last, part = call(
        functools.partial(far_kernel, scale),
        [*single, to_ring], [order, dma((2,))],
        offsets, *far, tgt_block, *(m[3] for m in made),
        smem=1, **cost,
    )
    made.append(last)
    src_blocks, logits, logits_t = ([m[k] for m in made] for k in range(3))
    wide_src = pltpu.VMEM((n_src, LANES), f32)
    wide_tgt = pltpu.VMEM((n_tgt, LANES), f32)
    for step in range(ITERS):
        gathered = lax.all_to_all(part, RING, 0, 0)
        part, src_pots = call(
            functools.partial(src_pots_kernel, math.log2(total_tgt)),
            [to_spread, pots], [order, wide_src],
            offsets, *logits, gathered, smem=1, flops=8 * n_src * n_tgt, bytes_accessed=2**22,
        )
        gathered = lax.all_to_all(part, SPREAD, 0, 0)
        if step < ITERS - 1:
            (part,) = call(
                functools.partial(tgt_pots_kernel, math.log2(total_src)),
                [to_ring], [order, wide_tgt],
                offsets, *logits_t, gathered, smem=1, flops=8 * n_src * n_tgt, bytes_accessed=2**22,
            )
    term = jax.ShapeDtypeStruct((rows, depth), f32)

    def src_terms(log_count, units, pieces, tgt_pots, kinds):
        return call(
            functools.partial(src_kernel, log_count, 1.0 / total_tgt, pieces),
            kinds, [order, wide_src],
            offsets, *(logits[u] for u in units), tgt_pots, src_pots, tgt_block,
            smem=1, flops=matmul // 4, bytes_accessed=2**22,
        )

    low = jax.ShapeDtypeStruct((rows, depth), bf16)
    far = [jax.ShapeDtypeStruct((half, depth), bf16)] * 2
    up, down, tgt_pots = src_terms(math.log2(total_src), (4,), [(0, rows, 7 * rows)], gathered, [*far, pots])
    up, down = shift(up, 1), shift(down, -1)
    pieces = [(0, 2 * rows, 0), (0, 2 * rows, 2 * rows), (0, 2 * rows, 4 * rows), (0, rows, 6 * rows)]
    *terms, own_term = src_terms(None, (0, 1, 2, 3), pieces, tgt_pots, [term] * 7)
    keep, give = call(
        functools.partial(tgt_kernel, 1.0 / total_src),
        [jax.ShapeDtypeStruct((n_tgt // 2, depth), f32), jax.ShapeDtypeStruct((n_tgt // 2, depth), bf16)],
        [wide_tgt],
        *logits_t, tgt_pots, src_pots, *src_blocks,
        flops=matmul, bytes_accessed=2**23,
    )
    taken = lax.ppermute(give, "core", SWAP)
    keep, taken, up, down, own_term, *terms = lax.optimization_barrier((keep, taken, up, down, own_term, *terms))
    shares = jax.ShapeDtypeStruct((n_tgt // 2, depth), bf16)
    (sent,) = call(
        add_cores_kernel, [shares], [pltpu.VMEM(shares.shape, bf16), dma((4,))],
        keep, taken, outs_in_hbm=(0,), flops=n_tgt * depth, bytes_accessed=2**22,
    )
    parts = lax.all_to_all(sent.reshape(plane, columns, depth), PLANE, 0, 0)
    for k in (2, 1, 0):
        up, down = call(
            first_add_kernel if k == 2 else add_kernel, [low] * 2, [],
            up, terms[2 * k], down, terms[2 * k + 1], flops=1, bytes_accessed=2**20,
        )
        if k == 0:
            parts, up, down = lax.optimization_barrier((parts, up, down))
        up, down = shift(up, 1), shift(down, -1)
    tgt_pull = jnp.sum(parts.astype(f32), axis=0)
    src_pull = own_term + up.astype(f32) + down.astype(f32)
    row_cost = jnp.sum(src_pull * (src_emb.astype(f32) * (-1.0 / math.sqrt(depth))), axis=1)
    return (src_pull, tgt_pull, row_cost)


def solution(mesh):
    split = Mesh(mesh.devices.reshape(SIZES), AXES)
    return jax.shard_map(
        shards,
        mesh=split,
        in_specs=(P(ROW + COL, None), P(COL + ROW, None), P(ROW), P(COL)),
        out_specs=(P(ROW + COL, None), P(COL + ROW, None), P(ROW + COL)),
        check_vma=False,
    )
```

```python
import functools
import math

import jax
import jax.numpy as jnp
from jax import lax
from jax.experimental import pallas as pl
from jax.experimental.pallas import tpu as pltpu
from jax.sharding import Mesh, PartitionSpec as P

ITERS = 3
NEG = -1e30
EPSILON = 0.5
LOG2E = math.log2(math.e)
LANES = 128
DISTANCES = (1, 7, 2, 6, 3, 5, 0, 4)

AXES = ("x", "zh", "core", "zl", "y")
SIZES = (4, 4, 2, 2, 4)
ROW = ("x", "zh", "core")
COL = ("zl", "y")
RING = ("zh", "zl")
PLANE = ("x", "y")
SPREAD = ("x", "y", "core")
SWAP = [(0, 1), (1, 0)]

VMEM = pl.BlockSpec(memory_space=pltpu.VMEM)
SMEM = pl.BlockSpec(memory_space=pltpu.SMEM)
IN_HBM = pl.BlockSpec(memory_space=pl.ANY)
CONTRACT_LAST = (((1,), (1,)), ((), ()))


def dot(a, b, dims=(((1,), (0,)), ((), ()))):
    return lax.dot_general(a, b, dims, preferred_element_type=jnp.float32)


def call(kernel, outs, scratch, *operands, smem=0, in_hbm=(), outs_in_hbm=(), flops=0, bytes_accessed=0):
    specs = [
        SMEM if k < smem else IN_HBM if k in in_hbm else VMEM for k in range(len(operands))
    ]
    operands = [
        pltpu.with_memory_space_constraint(v, pltpu.HBM) if k in in_hbm else v
        for k, v in enumerate(operands)
    ]
    outs = [
        pltpu.HBM(out.shape, out.dtype) if k in outs_in_hbm else out for k, out in enumerate(outs)
    ]
    return pl.pallas_call(
        kernel,
        out_shape=outs,
        in_specs=specs,
        out_specs=[IN_HBM if k in outs_in_hbm else VMEM for k in range(len(outs))],
        scratch_shapes=scratch,
        compiler_params=pltpu.CompilerParams(vmem_limit_bytes=16 * 2**20),
        cost_estimate=pl.CostEstimate(
            flops=flops, bytes_accessed=bytes_accessed, transcendentals=0
        ),
    )(*operands)


def shift(value, step):
    size = lax.axis_size(RING)
    return lax.ppermute(value, RING, [(i, (i + step) % size) for i in range(size)])


def copy_all(pairs, sems):
    copies = [pltpu.make_async_copy(a, b, sems.at[k]) for k, (a, b) in enumerate(pairs)]
    for copy in copies:
        copy.start()
    for copy in copies:
        copy.wait()


def one_hot(line, dtype):
    labels = jnp.broadcast_to(line.astype(jnp.float32), (LANES, LANES)).T
    lanes = lax.broadcasted_iota(jnp.int32, (LANES, LANES), 1).astype(jnp.float32)
    return (labels == lanes).astype(dtype)


def label_kernel(offsets, src_lang, tgt_lang, src, tgt, src_out, tgt_out, src_labels, tgt_labels, hot, sems):
    columns, depth = tgt.shape
    copies = [
        pltpu.make_async_copy(a, b, sems.at[k])
        for k, (a, b) in enumerate(
            [
                (tgt_lang, tgt_labels),
                (src_lang, src_labels),
                (tgt, tgt_out.at[:, :depth]),
                (src, src_out.at[:, :depth]),
            ]
        )
    ]
    for copy in copies:
        copy.start()
    copies[0].wait()
    here = offsets[3] * columns
    hot[...] = one_hot(tgt_labels[pl.ds(here // LANES, 1), :], jnp.float32)
    tgt_out[:, depth:] = hot[pl.ds(pl.multiple_of(lax.rem(here, LANES), columns), columns), :].astype(tgt_out.dtype)
    copies[1].wait()
    src_out[:, depth:] = one_hot(src_labels[pl.ds(offsets[2], 1), :], src_out.dtype)
    copies[2].wait()
    copies[3].wait()


def assemble_kernel(axis, offsets, *refs):
    (*blocks, out, sems), n = refs, len(refs) - 2
    rows = blocks[0].shape[0]
    places = [lax.rem(offsets[axis] + k, n) * rows for k in range(n)]
    copy_all(
        [(block, out.at[pl.ds(pl.multiple_of(at, rows), rows)]) for block, at in zip(blocks, places)],
        sems,
    )


def assemble_relayed_kernel(offsets, own, first, second, third, relayed, out, sems):
    rows = own.shape[0]
    places = [
        out.at[pl.ds(pl.multiple_of(lax.rem(offsets[4] + k, 4) * rows, rows), rows)] for k in range(4)
    ]

    @pl.when(offsets[1] == 0)
    def _():
        copy_all([(second, places[2])], sems)

    @pl.when(offsets[1] != 0)
    def _():
        copy_all([(relayed, places[2])], sems)

    copy_all([(own, places[0]), (first, places[1]), (third, places[3])], sems)


def columns_sums(tables, added):
    tiles = tables[0].shape[1] // LANES

    def fold(start, join):
        results, row = start, 0
        for table in tables:
            for c in range(table.shape[0] // LANES):
                add = None if added is None else added[row : row + LANES, :]
                for t in range(tiles):
                    z = table[c * LANES : (c + 1) * LANES, t * LANES : (t + 1) * LANES]
                    z = (z if add is None else z + add).reshape(LANES // 8, 8, LANES)
                    results[t] = join(t, results[t], z)
                row += LANES
        return results

    def larger(t, top, z):
        z = jnp.max(z, axis=0)
        return z if top is None else jnp.maximum(top, z)

    tops = [jnp.max(top, axis=0, keepdims=True) for top in fold([None] * tiles, larger)]

    def total(t, so_far, z):
        z = jnp.sum(jnp.exp2(z - tops[t][None]), axis=0)
        return z if so_far is None else so_far + z

    totals = [jnp.sum(v, axis=0, keepdims=True) for v in fold([None] * tiles, total)]
    return tops, totals


def columns_lse(tables, added):
    return [top + jnp.log2(total) for top, total in zip(*columns_sums(tables, added))]


def send_out(parts, offset, table, order, out):
    for part, at in zip(parts, table):
        order[pl.ds(lax.rem(at + offset, 8), 1), :] = part
    out[...] = jnp.broadcast_to(order[...][None], out.shape)


def merge(gathered, log_count, offset, table, order):
    parts = gathered[...]
    top = jnp.max(parts, axis=0)
    total = jnp.sum(jnp.exp2(parts - top[None]), axis=0)
    order[...] = log_count - (top + jnp.log2(total))
    return jnp.concatenate([order[pl.ds(lax.rem(at + offset, 8), 1), :] for at in table])


def spread(pots, wide):
    columns = pots.T
    for c in range(8):
        wide[c * LANES : (c + 1) * LANES, :] = jnp.broadcast_to(
            columns[:, c : c + 1], (LANES, LANES)
        )


def make_logits(scale, src, tgt, logits, logits_t):
    depth = src.shape[1] - LANES
    emb, hot = src[:, :depth], src[:, depth:]
    step = 256
    for start in range(0, tgt.shape[0], step):
        to = slice(start, start + step)
        same = dot(tgt[to, depth:], hot, CONTRACT_LAST) > 0.5
        value = jnp.where(same, dot(tgt[to, :depth], emb, CONTRACT_LAST) * scale, NEG)
        logits_t[to, :] = value
        logits[:, to] = value.T


def first_pair_kernel(scale, near, other, mine, theirs, src, logits, logits_t, part, tgt, sems):
    half = mine.shape[0]
    copy_all(
        [
            (mine, tgt.at[:half]),
            (theirs, tgt.at[half:]),
            (near, src.at[: near.shape[0]]),
            (other, src.at[near.shape[0] :]),
        ],
        sems,
    )
    make_logits(scale, src, tgt, logits, logits_t)
    part[...] = jnp.concatenate(columns_lse([logits_t], None))


def halves_kernel(up, down, up_out, down_out, sems):
    half = up_out.shape[0]
    copy_all([(up.at[:half], up_out), (down.at[half:], down_out)], sems)


def pair_kernel(scale, near, other, tgt, src, logits, logits_t, part, sems):
    copy_all([(near, src.at[: near.shape[0]]), (other, src.at[near.shape[0] :])], sems)
    make_logits(scale, src, tgt, logits, logits_t)
    part[...] = jnp.concatenate(columns_lse([logits_t], None))


def own_kernel(scale, own, tgt, src, logits, logits_t, part, sems):
    copy_all([(own, src)], sems)
    make_logits(scale, src, tgt, logits, logits_t)
    part[...] = jnp.concatenate(columns_lse([logits_t], None))


def pair_own_kernel(scale, near, other, own, tgt, *refs):
    sems = refs[8]
    pair_kernel(scale, near, other, tgt, *refs[:4], sems)
    own_kernel(scale, own, tgt, *refs[4:8], sems)


def far_kernel(scale, offsets, far_up, far_down, tgt, *refs):
    parts, (src, logits, logits_t, out, order, sems) = refs[:4], refs[4:]
    half = far_up.shape[0]
    copy_all([(far_up, src.at[:half]), (far_down, src.at[half:])], sems)
    make_logits(scale, src, tgt, logits, logits_t)
    parts = [part[r : r + 1, :] for part in parts for r in range(part.shape[0])]
    send_out(parts + columns_lse([logits_t], None), offsets[0], DISTANCES, order, out)


def src_pots_kernel(log_count, offsets, *refs):
    tables, (gathered, out, pots, order, wide) = refs[:5], refs[5:]
    local = merge(gathered, log_count, offsets[0], DISTANCES, order)
    pots[...] = local
    spread(local, wide)
    send_out(columns_lse(tables, wide), offsets[1], range(8), order, out)


def tgt_pots_kernel(log_count, offsets, *refs):
    tables, (gathered, out, order, wide) = refs[:5], refs[5:]
    spread(merge(gathered, log_count, offsets[1], range(8), order), wide)
    parts = [part for table in tables for part in columns_lse([table], wide)]
    send_out(parts, offsets[0], DISTANCES, order, out)


def src_kernel(log_count, share, pieces, offsets, *refs):
    n = len(pieces)
    tables, (tgt_pots, src_pots, block), outs = refs[:n], refs[n : n + 3], refs[n + 3 : -2]
    order, wide = refs[-2:]
    depth, half = outs[0].shape[1], block.shape[0] // 2
    if log_count is None:
        tgt = tgt_pots[...]
    else:
        tgt = merge(tgt_pots, log_count, offsets[1], range(8), order)
        outs[-1][...] = tgt
        outs = outs[:-1]
    spread(src_pots[...], wide)
    outs = list(outs)
    for (first, rows, place), table in zip(pieces, tables):
        at = slice(place, place + rows)
        weight = [
            jnp.exp2(table[first : first + rows, t * LANES : (t + 1) * LANES] + wide[at, :] + tgt[t : t + 1, :])
            .astype(jnp.bfloat16)
            for t in range(8)
        ]
        left = jnp.concatenate(weight[:4], axis=1)
        right = jnp.concatenate(weight[4:], axis=1)
        pull = (dot(left, block[:half, :depth]) + dot(right, block[half:, :depth])) * share
        start = 0
        while start < rows:
            out = outs.pop(0)
            out[...] = pull[start : start + out.shape[0]].astype(out.dtype)
            start += out.shape[0]


def tgt_kernel(share, *refs):
    tables, (tgt_pots, src_pots), blocks = refs[:5], refs[5:7], refs[7:12]
    keep, give, wide = refs[12:]
    spread(tgt_pots[...], wide)
    src = src_pots[...]
    depth = keep.shape[1]
    for unit in (2, 3, 0, 1):
        at = slice(unit * 256, (unit + 1) * 256)
        weight, line = [], 0
        for table in tables:
            for t in range(table.shape[1] // LANES):
                z = table[at, t * LANES : (t + 1) * LANES] + src[line : line + 1, :] + wide[at, :]
                weight.append(jnp.exp2(z).astype(jnp.bfloat16))
                line += 1
        pull = 0.0
        for k in range(3):
            pull = pull + dot(jnp.concatenate(weight[2 * k : 2 * k + 2], axis=1), blocks[k][:, :depth])
        last = jnp.concatenate([blocks[3][:, :depth], blocks[4][:, :depth]])
        pull = pull + dot(jnp.concatenate(weight[6:], axis=1), last)
        to = slice((unit % 2) * 256, (unit % 2 + 1) * 256)
        if unit < 2:
            keep[to, :] = pull * share
        else:
            give[to, :] = (pull * share).astype(give.dtype)


def add_cores_kernel(keep, taken, out, total, sems):
    rows = keep.shape[0] // sems.shape[0]
    copies = []
    for c in range(sems.shape[0]):
        at = slice(c * rows, (c + 1) * rows)
        total[at, :] = (keep[at, :] + taken[at, :].astype(jnp.float32)).astype(total.dtype)
        copies.append(pltpu.make_async_copy(total.at[at], out.at[at], sems.at[c]))
        copies[-1].start()
    for copy in copies:
        copy.wait()


def first_add_kernel(up, up_term, down, down_term, up_out, down_out):
    half = up.shape[0]
    up_out[:half, :] = (up_term[:half, :] + up[...].astype(jnp.float32)).astype(up_out.dtype)
    up_out[half:, :] = up_term[half:, :].astype(up_out.dtype)
    down_out[:half, :] = down_term[:half, :].astype(down_out.dtype)
    down_out[half:, :] = (down_term[half:, :] + down[...].astype(jnp.float32)).astype(down_out.dtype)


def add_kernel(up, up_term, down, down_term, up_out, down_out):
    for out, term, add in ((up_out, up_term, up), (down_out, down_term, down)):
        out[...] = (term[...] + add[...].astype(jnp.float32)).astype(out.dtype)


def shards(src_emb, tgt_emb, src_lang, tgt_lang):
    f32, bf16 = jnp.float32, jnp.bfloat16
    rows, depth = src_emb.shape
    columns = tgt_emb.shape[0]
    row, col = lax.axis_index(ROW), lax.axis_index(COL)
    ring, plane = lax.axis_size(RING), lax.axis_size(PLANE)
    spread_size = lax.axis_size(SPREAD)
    n_src, n_tgt = rows * ring, columns * spread_size
    place, core = lax.axis_index(RING), lax.axis_index("core")
    total_src = src_lang.shape[0] * lax.axis_size(ROW)
    total_tgt = tgt_lang.shape[0] * lax.axis_size(COL)
    offsets = jnp.stack(
        [place, 4 * core, col, row, lax.axis_index("x"), lax.axis_index("y")]
    ).astype(jnp.int32)

    n_label = depth + LANES
    dma = pltpu.SemaphoreType.DMA
    own, tgt = call(
        label_kernel,
        [jax.ShapeDtypeStruct((rows, n_label), bf16), jax.ShapeDtypeStruct((columns, n_label), bf16)],
        [
            pltpu.VMEM((src_lang.shape[0] // LANES, LANES), jnp.int32),
            pltpu.VMEM((tgt_lang.shape[0] // LANES, LANES), jnp.int32),
            pltpu.VMEM((LANES, LANES), f32), dma((4,)),
        ],
        offsets, src_lang.reshape(-1, LANES), tgt_lang.reshape(-1, LANES), src_emb, tgt_emb,
        smem=1, in_hbm=range(1, 5), flops=1, bytes_accessed=2**20,
    )

    def gather_axis(block, axis, at):
        size = lax.axis_size(axis)
        found = [
            lax.ppermute(block, axis, [((i + k) % size, i) for i in range(size)]) for k in range(1, size)
        ]
        return call(
            functools.partial(assemble_kernel, at),
            [jax.ShapeDtypeStruct((size * block.shape[0], block.shape[1]), bf16)], [dma((size,))],
            offsets, block, *found, smem=1, flops=1, bytes_accessed=2**20,
        )[0]

    up, down = shift(own, 1), shift(own, -1)
    pairs = [(down, up)]
    block = gather_axis(tgt, "y", 5)
    block, up, down = lax.optimization_barrier((block, up, down))
    up, down = shift(up, 1), shift(down, -1)
    first, third = (lax.ppermute(block, "x", [((i + k) % 4, i) for i in range(4)]) for k in (1, 3))
    pairs_of = lambda step, c: [(((i + step) % 4) * 2 + c, i * 2 + c) for i in range(4)]
    second = lax.ppermute(block, ("x", "core"), pairs_of(2, 0))
    relayed = lax.ppermute(third, ("x", "core"), pairs_of(3, 1))
    (mine,) = call(
        assemble_relayed_kernel, [jax.ShapeDtypeStruct((plane * columns, n_label), bf16)], [dma((3,))],
        offsets, block, first, second, third, relayed, smem=1, flops=1, bytes_accessed=2**20,
    )
    pairs.append((down, up))
    up, down = shift(up, 1), shift(down, -1)
    mine, up, down = lax.optimization_barrier((mine, up, down))
    theirs = lax.ppermute(mine, "core", SWAP)

    order = pltpu.VMEM((8, LANES), f32)
    pots = jax.ShapeDtypeStruct((8, LANES), f32)
    to_ring = jax.ShapeDtypeStruct((ring, 8, LANES), f32)
    to_spread = jax.ShapeDtypeStruct((spread_size, 8, LANES), f32)
    pair = [
        jax.ShapeDtypeStruct((2 * rows, n_label), bf16),
        jax.ShapeDtypeStruct((2 * rows, n_tgt), f32),
        jax.ShapeDtypeStruct((n_tgt, 2 * rows), f32),
    ]
    pair_part = jax.ShapeDtypeStruct((2, LANES), f32)
    matmul = 2 * n_src * n_tgt * depth
    scale = LOG2E / (EPSILON * math.sqrt(depth))
    cost = dict(flops=matmul // 2, bytes_accessed=2**22)
    *first, tgt_block = call(
        functools.partial(first_pair_kernel, scale),
        [*pair, pair_part, jax.ShapeDtypeStruct((n_tgt, n_label), bf16)], [dma((4,))],
        *pairs[0], mine, theirs, **cost,
    )

    def pair_logits(near, other, in_hbm):
        return call(
            functools.partial(pair_kernel, scale),
            [*pair, pair_part], [dma((2,))],
            near, other, tgt_block, in_hbm=in_hbm, **cost,
        )

    made = [list(first), list(pair_logits(*pairs[1], ()))]
    near, other = down, up
    half = rows // 2
    far = [jax.ShapeDtypeStruct((half, n_label), bf16)] * 2
    up, down = call(halves_kernel, far, [dma((2,))], up, down, flops=1, bytes_accessed=1)
    far = shift(up, 1), shift(down, -1)
    single = [
        jax.ShapeDtypeStruct((rows, n_label), bf16),
        jax.ShapeDtypeStruct((rows, n_tgt), f32),
        jax.ShapeDtypeStruct((n_tgt, rows), f32),
    ]
    both = call(
        functools.partial(pair_own_kernel, scale),
        [*pair, pair_part, *single, jax.ShapeDtypeStruct((1, LANES), f32)], [dma((2,))],
        near, other, own, tgt_block, **cost,
    )
    made += [both[:4], both[4:]]
    *last, part = call(
        functools.partial(far_kernel, scale),
        [*single, to_ring], [order, dma((2,))],
        offsets, *far, tgt_block, *(m[3] for m in made),
        smem=1, **cost,
    )
    made.append(last)
    src_blocks, logits, logits_t = ([m[k] for m in made] for k in range(3))
    wide_src = pltpu.VMEM((n_src, LANES), f32)
    wide_tgt = pltpu.VMEM((n_tgt, LANES), f32)
    for step in range(ITERS):
        gathered = lax.all_to_all(part, RING, 0, 0)
        part, src_pots = call(
            functools.partial(src_pots_kernel, math.log2(total_tgt)),
            [to_spread, pots], [order, wide_src],
            offsets, *logits, gathered, smem=1, flops=8 * n_src * n_tgt, bytes_accessed=2**22,
        )
        gathered = lax.all_to_all(part, SPREAD, 0, 0)
        if step < ITERS - 1:
            (part,) = call(
                functools.partial(tgt_pots_kernel, math.log2(total_src)),
                [to_ring], [order, wide_tgt],
                offsets, *logits_t, gathered, smem=1, flops=8 * n_src * n_tgt, bytes_accessed=2**22,
            )
    term = jax.ShapeDtypeStruct((rows, depth), f32)

    def src_terms(log_count, units, pieces, tgt_pots, kinds):
        return call(
            functools.partial(src_kernel, log_count, 1.0 / total_tgt, pieces),
            kinds, [order, wide_src],
            offsets, *(logits[u] for u in units), tgt_pots, src_pots, tgt_block,
            smem=1, flops=matmul // 4, bytes_accessed=2**22,
        )

    low = jax.ShapeDtypeStruct((rows, depth), bf16)
    far = [jax.ShapeDtypeStruct((half, depth), bf16)] * 2
    up, down, tgt_pots = src_terms(math.log2(total_src), (4,), [(0, rows, 7 * rows)], gathered, [*far, pots])
    up, down = shift(up, 1), shift(down, -1)
    pieces = [(0, 2 * rows, 0), (0, 2 * rows, 2 * rows), (0, 2 * rows, 4 * rows), (0, rows, 6 * rows)]
    *terms, own_term = src_terms(None, (0, 1, 2, 3), pieces, tgt_pots, [term] * 7)
    keep, give = call(
        functools.partial(tgt_kernel, 1.0 / total_src),
        [jax.ShapeDtypeStruct((n_tgt // 2, depth), f32), jax.ShapeDtypeStruct((n_tgt // 2, depth), bf16)],
        [wide_tgt],
        *logits_t, tgt_pots, src_pots, *src_blocks,
        flops=matmul, bytes_accessed=2**23,
    )
    taken = lax.ppermute(give, "core", SWAP)
    keep, taken, up, down, own_term, *terms = lax.optimization_barrier((keep, taken, up, down, own_term, *terms))
    shares = jax.ShapeDtypeStruct((n_tgt // 2, depth), bf16)
    (sent,) = call(
        add_cores_kernel, [shares], [pltpu.VMEM(shares.shape, bf16), dma((4,))],
        keep, taken, outs_in_hbm=(0,), flops=n_tgt * depth, bytes_accessed=2**22,
    )
    parts = lax.all_to_all(sent.reshape(plane, columns, depth), PLANE, 0, 0)
    for k in (2, 1, 0):
        up, down = call(
            first_add_kernel if k == 2 else add_kernel, [low] * 2, [],
            up, terms[2 * k], down, terms[2 * k + 1], flops=1, bytes_accessed=2**20,
        )
        if k == 0:
            parts, up, down = lax.optimization_barrier((parts, up, down))
        up, down = shift(up, 1), shift(down, -1)
    tgt_pull = jnp.sum(parts.astype(f32), axis=0)
    src_pull = own_term + up.astype(f32) + down.astype(f32)
    row_cost = jnp.sum(src_pull * (src_emb.astype(f32) * (-1.0 / math.sqrt(depth))), axis=1)
    return (src_pull, tgt_pull, row_cost)


def solution(mesh):
    split = Mesh(mesh.devices.reshape(SIZES), AXES)
    return jax.shard_map(
        shards,
        mesh=split,
        in_specs=(P(ROW + COL, None), P(COL + ROW, None), P(ROW), P(COL)),
        out_specs=(P(ROW + COL, None), P(COL + ROW, None), P(ROW + COL)),
        check_vma=False,
    )
```
